32 devices in a mesh: groups: 2 (over y), row: 4 (over z), col: 2 (over x), claim: 2 (over core).
Axes of the slice: x: 2, y: 2, z: 4, core: 2. Of those that a mesh axis runs over, the one named last changes fastest.
Arguments:
- claim_cell: int32 [32, 8, 192], P(('groups', 'row', 'col', 'claim')), parts along dimension 0, may hold values from 0 to 262143
- claim_weight: float32 [32, 8, 192], P(('groups', 'row', 'col', 'claim')), parts along dimension 0, may hold values from 0.1 to 10
- claim_count: int32 [32, 8], P(('groups', 'row', 'col', 'claim')), parts along dimension 0, may hold values from 0 to 192, as said below
- baseline: float32 [2048, 2048], P(('groups', 'row', 'claim'), 'col'), parts along dimension 0, may hold values from 0.05 to 0.3
- half_widths: int32 [16], replicated, may hold values from 0 to 64, as said below
Outputs:
- ratio_fields: float32 [16, 2048, 2048], P(None, ('groups', 'row', 'claim'), 'col'), parts along dimension 1
The draws below stay inside these ranges and needn't reach their ends.
There are 2 independent parts, one for each index of `groups`. The reference program is written for one: setup_inputs(seed, part) draws one part's arguments, and reference() takes and returns one part's arrays. A program takes and returns all parts, laid end to end along the dimension named above; an argument that names none is the same for every part. Nothing has to cross between parts.
Inputs may be any that keep to these rules, and one draw needn't show every extreme that they name: `claim_count`: live slots of one sender to one tile come first; for one tile drawn from the seed every sender fills all 192 slots. `half_widths`: distinct values; one equals 64.
All inputs are finite; a program needn't handle non-finite values.
Results may differ from the reference program's by a relative error of at most 0.0003.
Values sent between devices are 32-bit elements; how exact they have to be, the bound alone decides.
No kernel may reach another device: no remote copies, remote signals or barrier semaphores. Data moves between devices by JAX's collectives and lax.ppermute only.
A program may use at most 64 MiB of HBM per device.

```python
import math
import jax
import jax.numpy as jnp
from jax import lax

BR = 128
BC = 1024
CAP = 192
HALO = 64
NSIZES = 16
TILES = 8
SENDERS = 16
GRID_ROWS = 1024
GRID_COLS = 2048
N_ROW = 4
N_COL = 2
N_CLAIM = 2


def draw_claim_count(key, part):
    key_ceiling = jax.random.fold_in(key, 11)
    key_heavy = jax.random.fold_in(key, 12)
    key_drop = jax.random.fold_in(key, 13)
    ceiling = jax.random.randint(key_ceiling, (TILES,), CAP // 8, CAP + 1)
    heavy = jax.random.randint(key_heavy, (), 0, TILES)
    tile_index = jnp.arange(TILES, dtype=jnp.int32)
    ceiling = jnp.where(tile_index == heavy, CAP, ceiling)
    raw_drop = jax.random.randint(key_drop, (SENDERS, TILES), 0, 1 << 20)
    dropped = raw_drop % (ceiling[None, :] // 2 + 1)
    filled = ceiling[None, :] - dropped
    filled = jnp.where(tile_index[None, :] == heavy, CAP, filled)
    return filled.astype(jnp.int32)


def draw_half_widths(key, part):
    chosen = jax.random.permutation(jax.random.fold_in(key, 21), HALO)[:NSIZES - 1]
    values = jnp.concatenate([chosen.astype(jnp.int32), jnp.array([HALO], jnp.int32)])
    return jax.random.permutation(jax.random.fold_in(key, 22), values).astype(jnp.int32)


def place_ends(drawn, key, smallest, high):
    longest = drawn.shape.index(max(drawn.shape))
    spots = []
    for shift in (0, 1):
        where = [jax.random.randint(jax.random.fold_in(key, axis), (), 0, length) for axis, length in enumerate(drawn.shape)]
        where[longest] = (where[longest] + shift) % drawn.shape[longest]
        spots.append(tuple(where))
    return drawn.at[spots[0]].set(smallest).at[spots[1]].set(high)


def steps_of(key, shape, cuts, smallest, largest):
    loudness, own = 1.0, jax.random.fold_in(key, 6)
    for dim, blocks in cuts:
        steps = jnp.exp(jax.random.uniform(jax.random.fold_in(own, dim), (blocks,), jnp.float32, smallest / len(cuts), largest / len(cuts)))
        loudness = loudness * jnp.repeat(steps, shape[dim] // blocks).reshape([-1 if axis == dim else 1 for axis in range(len(shape))])
    return loudness


def setup_inputs(seed: int = 0, part: int = 0) -> dict:
    arg_keys = jax.random.split(jax.random.key(seed), 6)
    own_keys = jax.random.split(jax.random.fold_in(arg_keys[5], part), 6)
    return {
        "claim_cell": place_ends(jax.random.randint(own_keys[0], (SENDERS, TILES, CAP), 0, BR * N_CLAIM * BC), jax.random.fold_in(own_keys[0], 1), 0, (BR * N_CLAIM * BC) - 1).astype(jnp.int32),
        "claim_weight": jnp.clip(jnp.exp(math.log(10.0) - 4.6051702 * jax.random.uniform(own_keys[1], (SENDERS, TILES, CAP), jnp.float32) ** steps_of(own_keys[1], (SENDERS, TILES, CAP), ((0, 16),), -0.2, 0.2)), 0.1, 10.0),
        "claim_count": draw_claim_count(jax.random.fold_in(jax.random.fold_in(arg_keys[5], part), 71), part),
        "baseline": jnp.clip(jnp.exp(math.log(0.3) - 1.7917595 * jax.random.uniform(own_keys[3], (GRID_ROWS, GRID_COLS), jnp.float32) ** steps_of(own_keys[3], (GRID_ROWS, GRID_COLS), ((0, 8), (1, 2)), -0.2, 0.2)), 0.05, 0.3),
        "half_widths": draw_half_widths(jax.random.fold_in(arg_keys[5], 71), part),
    }


def poisson_ratio(box_counts, box_base, side):
    positive = box_counts > 0
    safe_counts = jnp.where(positive, box_counts, 1.0)
    entropy = jnp.where(positive, box_counts * jnp.log(safe_counts / box_base), 0.0)
    return (entropy + box_base - box_counts) / side


def prefix_fields(padded, half_widths):
    block_rows = padded.shape[1] - 2 * HALO
    block_cols = padded.shape[2] - 2 * HALO
    zero_row = jnp.zeros_like(padded[:, :1, :])
    row_prefix = jnp.cumsum(jnp.concatenate([zero_row, padded], axis=1), axis=1)

    def one_size(half):
        half = half.astype(jnp.int32)
        upper = lax.dynamic_slice_in_dim(row_prefix, HALO + 1 + half, block_rows, 1)
        lower = lax.dynamic_slice_in_dim(row_prefix, HALO - half, block_rows, 1)
        row_boxes = upper - lower
        zero_col = jnp.zeros_like(row_boxes[:, :, :1])
        col_prefix = jnp.cumsum(jnp.concatenate([zero_col, row_boxes], axis=2), axis=2)
        right = lax.dynamic_slice_in_dim(col_prefix, HALO + 1 + half, block_cols, 2)
        left = lax.dynamic_slice_in_dim(col_prefix, HALO - half, block_cols, 2)
        boxed = right - left
        side = (2 * half + 1).astype(boxed.dtype)
        return poisson_ratio(boxed[0], boxed[1], side)

    return lax.map(one_size, half_widths)


def reference(claim_cell, claim_weight, claim_count, baseline, half_widths):
    slot_index = jnp.arange(CAP, dtype=jnp.int32)
    live = slot_index[None, None, :] < claim_count[:, :, None]
    weights = jnp.where(live, claim_weight.astype(jnp.float32), jnp.zeros((), jnp.float32))
    tile_index = jnp.arange(TILES, dtype=jnp.int32)
    grid_row = (tile_index // N_COL)[None, :, None] * (BR * N_CLAIM) + claim_cell // BC
    grid_col = (tile_index % N_COL)[None, :, None] * BC + claim_cell % BC
    counts = jnp.zeros((GRID_ROWS, GRID_COLS), jnp.float32)
    counts = counts.at[grid_row.ravel(), grid_col.ravel()].add(weights.ravel())
    stacked = jnp.stack([counts, baseline.astype(jnp.float32)])
    padded = jnp.pad(stacked, ((0, 0), (HALO, HALO), (HALO, HALO)))
    strip_count = N_ROW * N_CLAIM

    def one_block(index):
        strip = index // N_COL
        column = index % N_COL
        window = lax.dynamic_slice(padded, (jnp.int32(0), (strip * BR).astype(jnp.int32), (column * BC).astype(jnp.int32)), (2, BR + 2 * HALO, BC + 2 * HALO))
        return prefix_fields(window, half_widths)

    blocks = lax.map(one_block, jnp.arange(strip_count * N_COL, dtype=jnp.int32))
    blocks = blocks.reshape(strip_count, N_COL, NSIZES, BR, BC)
    return blocks.transpose(2, 0, 3, 1, 4).reshape(NSIZES, GRID_ROWS, GRID_COLS)
```

```python
import functools

import jax
import jax.numpy as jnp
from jax import lax
from jax.experimental import pallas as pl
from jax.experimental.pallas import tpu as pltpu
from jax.sharding import PartitionSpec as P

HALO = 64
LANES = 128
CODE = 4096
ROW_BIAS = 256
COL_BIAS = 1024
TINY = 1e-30
F32 = jnp.float32
BF16 = jnp.bfloat16


def side_tiles(cols):
    return min(cols - 1, 2)


def pieces_of(dest, rows, cols):
    row, col, claim = dest
    other = row - 1 if claim == 0 else row + 1
    sides = [(col, 0)]
    if cols == 2:
        sides.append((1 - col, -1 if col == 1 else 1))
    elif cols > 2:
        sides += [(col - 1, -1), (col + 1, 1)]
    found = []
    for tile_row, vertical in ((row, 0), (other, 1)):
        for tile_col, side in sides:
            there = 0 <= tile_row < rows and 0 <= tile_col < cols
            found.append((tile_row * cols + tile_col if there else None, vertical, side))
    return found


def pack_kernel(rows, cols, block_rows, block_cols, cell_ref, weight_ref, count_ref, out_ref):
    cell = cell_ref[0]
    slot = lax.broadcasted_iota(jnp.int32, cell.shape, 1)
    weight = jnp.where(slot < count_ref[...], weight_ref[0], 0.0)
    tile_row = lax.div(cell, block_cols)
    tile_col = lax.rem(cell, block_cols)
    codes = {}
    for claim in (0, 1):
        for vertical in (0, 1):
            if vertical:
                first = 2 * block_rows - HALO if claim == 0 else 0
            else:
                first = 0 if claim == 0 else block_rows - HALO
            for side in (-1, 0, 1):
                shift = {-1: HALO - block_cols, 0: 0, 1: HALO}[side]
                row_code = (tile_row + (ROW_BIAS - first)) * CODE
                codes[claim, vertical, side] = (row_code + tile_col + (shift + COL_BIAS)).astype(F32)
    zero = jnp.zeros((1, cell.shape[1]), F32)
    index = 0
    for row in range(rows):
        for col in range(cols):
            for claim in (0, 1):
                for place, (tile, vertical, side) in enumerate(pieces_of((row, col, claim), rows, cols)):
                    if tile is None:
                        out_ref[index, 2 * place : 2 * place + 1, :] = zero
                        out_ref[index, 2 * place + 1 : 2 * place + 2, :] = zero
                    else:
                        out_ref[index, 2 * place : 2 * place + 1, :] = codes[claim, vertical, side][tile : tile + 1]
                        out_ref[index, 2 * place + 1 : 2 * place + 2, :] = weight[tile : tile + 1]
                index += 1


def halves(value):
    high = value.astype(BF16)
    return high, (value - high.astype(F32)).astype(BF16)


def onehot(index, size):
    return index == lax.broadcasted_iota(jnp.int32, (size, index.shape[1]), 0)


def scan_kernel(
    sides, params_ref, got_ref, base_ref, above_ref, below_ref, beside_ref, out_ref, prefix, window, code_s, weight_s, own_acc, far_acc, side_acc, corner_acc
):
    block_rows, block_cols = base_ref.shape
    blocks = block_cols // LANES
    step = pl.program_id(0)
    senders, _, slots = got_ref.shape
    chunks = senders * slots // LANES
    own_rows = block_rows + HALO

    def prefix_of(field):
        lane = lax.broadcasted_iota(jnp.int32, (2 * block_rows, LANES), 1)
        sub = lax.broadcasted_iota(jnp.int32, (2 * block_rows // 8, 8, LANES), 1)
        for block in range(blocks + 1):
            left = window[blocks] if block == 0 else pltpu.roll(window[block - 1], HALO, axis=1)
            right = window[blocks] if block == blocks else pltpu.roll(window[block], HALO, axis=1)
            cells = jnp.where(lane < HALO, left, right).reshape(-1, 8, LANES)
            for hop in (1, 2, 4):
                cells = cells + jnp.where(sub >= hop, pltpu.roll(cells, hop, axis=1), 0.0)
            carry = jnp.zeros((8, LANES), F32)
            prefix[field, block, 0:8, :] = carry
            for tile in range(2 * block_rows // 8):
                total = cells[tile] + carry
                prefix[field, block, 8 * tile + 8 : 8 * tile + 16, :] = total
                carry = jnp.broadcast_to(total[7:8], (8, LANES))

    @pl.when(step == 0)
    def _():
        claim = params_ref[0]
        for place in range(2 * sides + 2):
            code = got_ref[:, 2 * place, :].astype(jnp.int32)
            weight = got_ref[:, 2 * place + 1, :]
            half = senders // 2
            for ref, value in ((code_s, code), (weight_s, weight)):
                ref[place, 0:senders, :] = value[:, :LANES]
                ref[place, senders : senders + half, 0 : slots - LANES] = value[:half, LANES:]
                ref[place, senders : senders + half, slots - LANES : LANES] = value[half:, LANES:]
        for acc in (own_acc, far_acc, side_acc, corner_acc):
            acc[...] = jnp.zeros_like(acc)

        def add_pair(pair, _):
            for place in range(2 * sides + 2):
                vertical, side = divmod(place, sides + 1)
                rows = HALO if vertical else own_rows
                cols = LANES if side else block_cols
                row_parts, col_parts = [], []
                for one in (0, 1):
                    code = code_s[place, pl.ds(2 * pair + one, 1), :]
                    weight = weight_s[place, pl.ds(2 * pair + one, 1), :]
                    high = weight.astype(BF16).astype(F32)
                    low = weight - high
                    hit = onehot(lax.div(code, CODE) - ROW_BIAS, rows)
                    row_parts.append(
                        jnp.concatenate([jnp.where(hit, high, 0.0), jnp.where(hit, low, 0.0)], axis=0).astype(BF16)
                    )
                    col_parts.append(
                        jnp.where(onehot(lax.rem(code, CODE) - COL_BIAS, cols), 1.0, 0.0).astype(BF16)
                    )
                product = lax.dot_general(
                    jnp.concatenate(row_parts, axis=1),
                    jnp.concatenate(col_parts, axis=1),
                    (((1,), (1,)), ((), ())),
                    preferred_element_type=F32,
                )
                acc = {(0, False): own_acc, (1, False): far_acc, (0, True): side_acc, (1, True): corner_acc}[
                    vertical, side > 0
                ]
                acc[...] += product
            return 0

        lax.fori_loop(0, chunks // 2, add_pair, 0)
        own_at = pl.multiple_of((1 - claim) * HALO, HALO)
        far_at = pl.multiple_of(claim * own_rows, HALO)
        for block in range(blocks):
            here = slice(block * LANES, (block + 1) * LANES)
            window[block, pl.ds(own_at, own_rows), :] = own_acc[:own_rows, here] + own_acc[own_rows:, here]
            window[block, pl.ds(far_at, HALO), :] = far_acc[:HALO, here] + far_acc[HALO:, here]
        window[blocks, pl.ds(own_at, own_rows), :] = side_acc[:own_rows] + side_acc[own_rows:]
        window[blocks, pl.ds(far_at, HALO), :] = corner_acc[:HALO] + corner_acc[HALO:]
        prefix_of(0)
        for block in range(blocks):
            here = slice(block * LANES, (block + 1) * LANES)
            window[block, 0:HALO, :] = above_ref[:, here]
            window[block, HALO : HALO + block_rows, :] = base_ref[:, here]
            window[block, HALO + block_rows :, :] = below_ref[:, here]
        window[blocks] = beside_ref[...]
        prefix_of(1)

    half = params_ref[1 + step]
    inverse = 1.0 / (2 * half + 1).astype(F32)
    from_col = lax.broadcasted_iota(jnp.int32, (2 * LANES, LANES), 0)
    to_col = lax.broadcasted_iota(jnp.int32, (2 * LANES, LANES), 1) + HALO
    band = jnp.where(jnp.abs(from_col - to_col) <= half, 1.0, 0.0).astype(BF16)

    def boxes(field):
        parts = []
        for block in range(blocks + 1):
            strip = prefix[field, block, pl.ds(HALO + 8 + half, block_rows), :] - prefix[
                field, block, pl.ds(HALO + 7 - half, block_rows), :
            ]
            parts.append(halves(strip))
        total = None
        for part in (0, 1):
            left = jnp.concatenate(
                [jnp.concatenate([parts[b][part], parts[b + 1][part]], axis=1) for b in range(blocks)], axis=0
            )
            product = jnp.dot(left, band, preferred_element_type=F32)
            total = product if total is None else total + product
        return total

    counts = boxes(0)
    base = boxes(1)
    result = (counts * (jnp.log(jnp.maximum(counts, TINY)) - jnp.log(base) - 1.0) + base) * inverse
    for block in range(blocks):
        out_ref[0, :, block * LANES : (block + 1) * LANES] = result[block * block_rows : (block + 1) * block_rows]


def shards(rows, cols, claim_cell, claim_weight, claim_count, baseline, half_widths):
    block_rows, block_cols = baseline.shape
    slots = claim_cell.shape[2]
    sides = side_tiles(cols)
    devices = rows * cols * 2
    sent = pl.pallas_call(
        functools.partial(pack_kernel, rows, cols, block_rows, block_cols),
        out_shape=jax.ShapeDtypeStruct((devices, 4 * (sides + 1), slots), F32),
    )(claim_cell, claim_weight, claim_count.reshape(-1, 1))
    got = lax.all_to_all(sent, ("row", "col", "claim"), split_axis=0, concat_axis=0, tiled=True)

    strips = rows * 2
    down = [(i, i + 1) for i in range(strips - 1)]
    up = [(i + 1, i) for i in range(strips - 1)]
    above = lax.ppermute(baseline[block_rows - HALO :], ("row", "claim"), down)
    below = lax.ppermute(baseline[:HALO], ("row", "claim"), up)
    tall = jnp.concatenate([above, baseline, below], axis=0)
    first, last = tall[:, :HALO], tall[:, block_cols - HALO :]
    if cols == 2:
        col = lax.axis_index("col")
        beside = lax.ppermute(
            jnp.concatenate([jnp.where(col == 0, last, 0.0), jnp.where(col == 1, first, 0.0)], axis=1),
            "col",
            [(0, 1), (1, 0)],
        )
    else:
        beside = jnp.concatenate(
            [
                lax.ppermute(last, "col", [(i, i + 1) for i in range(cols - 1)]),
                lax.ppermute(first, "col", [(i + 1, i) for i in range(cols - 1)]),
            ],
            axis=1,
        )
    params = jnp.concatenate([lax.axis_index("claim").astype(jnp.int32)[None], half_widths])
    sizes = half_widths.shape[0]
    blocks = block_cols // LANES
    places = 2 * (sides + 1)
    chunk_rows = devices * slots // LANES
    whole = pl.BlockSpec(memory_space=pltpu.VMEM)
    return pl.pallas_call(
        functools.partial(scan_kernel, sides),
        grid_spec=pltpu.PrefetchScalarGridSpec(
            num_scalar_prefetch=1,
            grid=(sizes,),
            in_specs=[whole] * 5,
            out_specs=pl.BlockSpec((1, block_rows, block_cols), lambda k, params: (k, 0, 0)),
            scratch_shapes=[
                pltpu.VMEM((2, blocks + 1, 2 * block_rows + 8, LANES), F32),
                pltpu.VMEM((blocks + 1, 2 * block_rows, LANES), F32),
                pltpu.VMEM((places, chunk_rows, LANES), jnp.int32),
                pltpu.VMEM((places, chunk_rows, LANES), F32),
                pltpu.VMEM((2 * (block_rows + HALO), block_cols), F32),
                pltpu.VMEM((2 * HALO, block_cols), F32),
                pltpu.VMEM((2 * (block_rows + HALO), LANES), F32),
                pltpu.VMEM((2 * HALO, LANES), F32),
            ],
        ),
        out_shape=jax.ShapeDtypeStruct((sizes, block_rows, block_cols), F32),
        compiler_params=pltpu.CompilerParams(vmem_limit_bytes=48 * 1024 * 1024),
    )(params, got, baseline, above, below, beside)


def solution(mesh):
    in_specs = (
        P(("groups", "row", "col", "claim"), None, None),
        P(("groups", "row", "col", "claim"), None, None),
        P(("groups", "row", "col", "claim"), None),
        P(("groups", "row", "claim"), "col"),
        P(),
    )
    out_specs = P(None, ("groups", "row", "claim"), "col")
    body = functools.partial(shards, mesh.shape["row"], mesh.shape["col"])
    return jax.shard_map(body, mesh=mesh, in_specs=in_specs, out_specs=out_specs, check_vma=False)
```

```python
import functools

import jax
import jax.numpy as jnp
from jax import lax
from jax.experimental import pallas as pl
from jax.experimental.pallas import tpu as pltpu
from jax.sharding import PartitionSpec as P

HALO = 64
LANES = 128
CODE = 4096
ROW_BIAS = 256
COL_BIAS = 1024
TINY = 1e-30
VMEM_LIMIT = 52 * 1024 * 1024
F32 = jnp.float32
BF16 = jnp.bfloat16


def side_tiles(cols):
    return min(cols - 1, 2)


def pieces_of(dest, rows, cols):
    row, col, claim = dest
    other = row - 1 if claim == 0 else row + 1
    sides = [(col, 0)]
    if cols == 2:
        sides.append((1 - col, -1 if col == 1 else 1))
    elif cols > 2:
        sides += [(col - 1, -1), (col + 1, 1)]
    found = []
    for tile_row, vertical in ((row, 0), (other, 1)):
        for tile_col, side in sides:
            there = 0 <= tile_row < rows and 0 <= tile_col < cols
            found.append((tile_row * cols + tile_col if there else None, vertical, side))
    return found


def pack_kernel(rows, cols, block_rows, block_cols, cell_ref, weight_ref, count_ref, out_ref):
    cell = cell_ref[0]
    tiles, slots = cell.shape
    slot = lax.broadcasted_iota(jnp.int32, (1, slots), 1)
    weights = [jnp.where(slot < count_ref[0, tile], weight_ref[0, tile : tile + 1, :], 0.0) for tile in range(tiles)]
    tile_row = lax.div(cell, block_cols)
    tile_col = lax.rem(cell, block_cols)
    codes = {}
    for claim in (0, 1):
        for vertical in (0, 1):
            if vertical:
                first = 2 * block_rows - HALO if claim == 0 else 0
            else:
                first = 0 if claim == 0 else block_rows - HALO
            for side in (-1, 0, 1):
                shift = {-1: HALO - block_cols, 0: 0, 1: HALO}[side]
                row_code = (tile_row + (ROW_BIAS - first)) * CODE
                codes[claim, vertical, side] = (row_code + tile_col + (shift + COL_BIAS)).astype(F32)
    zero = jnp.zeros((1, slots), F32)
    index = 0
    for row in range(rows):
        for col in range(cols):
            for claim in (0, 1):
                for place, (tile, vertical, side) in enumerate(pieces_of((row, col, claim), rows, cols)):
                    there = tile is not None
                    code = codes[claim, vertical, side][tile : tile + 1] if there else zero
                    out_ref[index, 2 * place : 2 * place + 1, :] = code
                    out_ref[index, 2 * place + 1 : 2 * place + 2, :] = weights[tile] if there else zero
                index += 1


def halves(value):
    high = value.astype(BF16)
    return high, (value - high.astype(F32)).astype(BF16)


def row_prefix(window, prefix):
    side, rows, _ = window.shape
    side -= 1
    lane = lax.broadcasted_iota(jnp.int32, (rows, LANES), 1)
    sub = lax.broadcasted_iota(jnp.int32, (rows // 8, 8, LANES), 1)
    before = window[side]
    for block in range(side + 1):
        after = window[side] if block == side else pltpu.roll(window[block], HALO, axis=1)
        cells = jnp.where(lane < HALO, before, after).reshape(-1, 8, LANES)
        before = after
        for hop in (1, 2, 4):
            cells = cells + jnp.where(sub >= hop, pltpu.roll(cells, hop, axis=1), 0.0)
        carry = jnp.zeros((8, LANES), F32)
        prefix[block, 0:8, :] = carry
        for tile in range(rows // 8):
            total = cells[tile] + carry
            prefix[block, 8 * tile + 8 : 8 * tile + 16, :] = total
            carry = jnp.broadcast_to(total[7:8], (8, LANES))


def band_of(half):
    here = lax.broadcasted_iota(jnp.int32, (LANES, LANES), 0)
    there = lax.broadcasted_iota(jnp.int32, (LANES, LANES), 1)
    gap = here - there
    both = [jnp.where(jnp.abs(gap + shift) <= half, 1.0, 0.0) for shift in (-HALO, LANES - HALO)]
    band = jnp.concatenate(both, axis=1).astype(BF16)
    return jnp.concatenate([band, band], axis=0)


def column_boxes(prefix, half, block_rows, use):
    band = band_of(half)
    before = None
    for block in range(prefix.shape[0]):
        lower = prefix[block, pl.ds(HALO + 8 + half, block_rows), :]
        upper = prefix[block, pl.ds(HALO + 7 - half, block_rows), :]
        product = jnp.dot(
            jnp.concatenate(halves(lower - upper), axis=1), band, preferred_element_type=F32
        )
        if block > 0:
            use(block - 1, before + product[:, LANES:])
        before = product[:, :LANES]


def lanes_of(block):
    return slice(block * LANES, (block + 1) * LANES)


def base_kernel(halves_ref, base_ref, above_ref, below_ref, beside_ref, out_ref, buffer, sems, window, prefix):
    block_rows, block_cols = base_ref.shape
    blocks = block_cols // LANES
    for block in range(blocks):
        window[block, 0:HALO, :] = above_ref[:, lanes_of(block)]
        window[block, HALO : HALO + block_rows, :] = base_ref[:, lanes_of(block)]
        window[block, HALO + block_rows :, :] = below_ref[:, lanes_of(block)]
    window[blocks] = beside_ref[...]
    row_prefix(window, prefix)
    sizes = buffer.shape[0]

    def one_size(step, _):
        def use(block, boxes):
            buffer[step, :, lanes_of(block)] = boxes

        column_boxes(prefix, halves_ref[step], block_rows, use)
        pltpu.make_async_copy(buffer.at[step], out_ref.at[step], sems.at[step]).start()
        return 0

    lax.fori_loop(0, sizes, one_size, 0, unroll=2)

    def finish(step, _):
        pltpu.make_async_copy(buffer.at[step], out_ref.at[step], sems.at[step]).wait()
        return 0

    lax.fori_loop(0, sizes, finish, 0)


def pack16(row):
    return jnp.broadcast_to(row.astype(F32), (16, row.shape[1])).astype(BF16)


def tall(packed, size):
    return jnp.concatenate([packed] * (size // 16), axis=0)


def scan_kernel(
    sides, halves_ref, got_ref, boxes_ref, out_ref, buffer, read_sems, write_sems,
    prefix, window, code_s, weight_s, row_hot, col_hot, own_acc, far_acc, side_acc, corner_acc,
):
    sizes, block_rows, block_cols = buffer.shape
    blocks = block_cols // LANES
    senders, _, slots = got_ref.shape
    chunks = senders * slots // LANES
    depth = row_hot.shape[1] // LANES
    own_rows = block_rows + HALO
    claim = lax.axis_index("claim")

    def read_of(step):
        return pltpu.make_async_copy(boxes_ref.at[step], buffer.at[step], read_sems.at[step])

    def write_of(step):
        return pltpu.make_async_copy(buffer.at[step], out_ref.at[step], write_sems.at[step])

    def begin(step, _):
        read_of(step).start()
        return 0

    lax.fori_loop(0, sizes, begin, 0)
    for place in range(2 * sides + 2):
        code = got_ref[:, 2 * place, :].astype(jnp.int32)
        weight = got_ref[:, 2 * place + 1, :]
        split = senders // 2
        for ref, value in ((code_s, code), (weight_s, weight)):
            ref[place, 0:senders, :] = value[:, :LANES]
            ref[place, senders : senders + split, 0 : slots - LANES] = value[:split, LANES:]
            ref[place, senders : senders + split, slots - LANES : LANES] = value[split:, LANES:]
    for acc in (own_acc, far_acc, side_acc, corner_acc):
        acc[...] = jnp.zeros_like(acc)
    target = {(0, False): own_acc, (1, False): far_acc, (0, True): side_acc, (1, True): corner_acc}
    one, none = jnp.ones((), BF16), jnp.zeros((), BF16)

    def add_chunk(chunk, _):
        for place in range(2 * sides + 2):
            vertical, side = divmod(place, sides + 1)
            rows = HALO if vertical else own_rows
            cols = LANES if side else block_cols
            code8 = code_s[place, pl.ds(pl.multiple_of(chunk * depth, depth), depth), :]
            weight8 = weight_s[place, pl.ds(pl.multiple_of(chunk * depth, depth), depth), :]
            row8 = lax.shift_right_logical(code8, 12) - ROW_BIAS
            col8 = (code8 & (CODE - 1)) - COL_BIAS
            high8 = weight8.astype(BF16).astype(F32)
            low8 = weight8 - high8
            row_iota = lax.broadcasted_iota(jnp.int32, (rows, LANES), 0).astype(F32).astype(BF16)
            col_iota = lax.broadcasted_iota(jnp.int32, (LANES, LANES), 0).astype(F32).astype(BF16)
            for part in range(depth):
                at = lanes_of(part)
                hit = tall(pack16(row8[part : part + 1]), rows) == row_iota
                row_hot[0:rows, at] = jnp.where(hit, tall(pack16(high8[part : part + 1]), rows), none)
                row_hot[rows : 2 * rows, at] = jnp.where(hit, tall(pack16(low8[part : part + 1]), rows), none)
                col = col8[part : part + 1]
                for block in range(cols // LANES):
                    inside = jnp.where(lax.shift_right_arithmetic(col, 7) == block, col & (LANES - 1), -1)
                    col_hot[lanes_of(block), at] = jnp.where(
                        tall(pack16(inside), LANES) == col_iota, one, none
                    )
            acc = target[vertical, side > 0]
            acc[...] += lax.dot_general(
                row_hot[0 : 2 * rows, :],
                col_hot[0:cols, :],
                (((1,), (1,)), ((), ())),
                preferred_element_type=F32,
            )
        return 0

    lax.fori_loop(0, chunks // depth, add_chunk, 0)
    own_at = pl.multiple_of((1 - claim) * HALO, HALO)
    far_at = pl.multiple_of(claim * own_rows, HALO)
    for block in range(blocks):
        here = lanes_of(block)
        window[block, pl.ds(own_at, own_rows), :] = own_acc[:own_rows, here] + own_acc[own_rows:, here]
        window[block, pl.ds(far_at, HALO), :] = far_acc[:HALO, here] + far_acc[HALO:, here]
    window[blocks, pl.ds(own_at, own_rows), :] = side_acc[:own_rows] + side_acc[own_rows:]
    window[blocks, pl.ds(far_at, HALO), :] = corner_acc[:HALO] + corner_acc[HALO:]
    row_prefix(window, prefix)

    def one_size(step, _):
        half = halves_ref[step]
        inverse = 1.0 / (2 * half + 1).astype(F32)
        read_of(step).wait()

        def use(block, counts):
            here = lanes_of(block)
            base = buffer[step, :, here]
            gain = jnp.log(jnp.maximum(counts, TINY)) - jnp.log(base) - 1.0
            buffer[step, :, here] = (counts * gain + base) * inverse

        column_boxes(prefix, half, block_rows, use)
        write_of(step).start()
        return 0

    lax.fori_loop(0, sizes, one_size, 0, unroll=2)

    def finish(step, _):
        write_of(step).wait()
        return 0

    lax.fori_loop(0, sizes, finish, 0)


def shards(rows, cols, claim_cell, claim_weight, claim_count, baseline, half_widths):
    block_rows, block_cols = baseline.shape
    slots = claim_cell.shape[2]
    sides = side_tiles(cols)
    devices = rows * cols * 2
    whole = pl.BlockSpec(memory_space=pltpu.VMEM)
    scalars = pl.BlockSpec(memory_space=pltpu.SMEM)
    sent = pl.pallas_call(
        functools.partial(pack_kernel, rows, cols, block_rows, block_cols),
        in_specs=[whole, whole, scalars],
        out_shape=jax.ShapeDtypeStruct((devices, 4 * (sides + 1), slots), F32),
    )(claim_cell, claim_weight, claim_count)
    got = lax.all_to_all(sent, ("row", "col", "claim"), split_axis=0, concat_axis=0, tiled=True)

    strips = rows * 2
    down = [(i, i + 1) for i in range(strips - 1)]
    up = [(i + 1, i) for i in range(strips - 1)]
    above = lax.ppermute(baseline[block_rows - HALO :], ("row", "claim"), down)
    below = lax.ppermute(baseline[:HALO], ("row", "claim"), up)
    pieces = (above, baseline, below)
    first = jnp.concatenate([piece[:, :HALO] for piece in pieces], axis=0)
    last = jnp.concatenate([piece[:, block_cols - HALO :] for piece in pieces], axis=0)
    if cols == 2:
        col = lax.axis_index("col")
        beside = lax.ppermute(
            jnp.concatenate([jnp.where(col == 0, last, 0.0), jnp.where(col == 1, first, 0.0)], axis=1),
            "col",
            [(0, 1), (1, 0)],
        )
    else:
        beside = jnp.concatenate(
            [
                lax.ppermute(last, "col", [(i, i + 1) for i in range(cols - 1)]),
                lax.ppermute(first, "col", [(i + 1, i) for i in range(cols - 1)]),
            ],
            axis=1,
        )
    sizes = half_widths.shape[0]
    blocks = block_cols // LANES
    places = 2 * (sides + 1)
    chunk_rows = devices * slots // LANES
    window = pltpu.VMEM((blocks + 1, 2 * block_rows, LANES), F32)
    prefix = pltpu.VMEM((blocks + 1, 2 * block_rows + 8, LANES), F32)
    field = (sizes, block_rows, block_cols)
    work = 2 * sizes * block_rows * (blocks + 1) * (2 * LANES) ** 2
    boxes = pl.pallas_call(
        base_kernel,
        in_specs=[scalars] + [whole] * 4,
        out_specs=pl.BlockSpec(memory_space=pltpu.HBM),
        out_shape=jax.ShapeDtypeStruct(field, F32),
        scratch_shapes=[pltpu.VMEM(field, F32), pltpu.SemaphoreType.DMA((sizes,)), window, prefix],
        cost_estimate=pl.CostEstimate(flops=work, bytes_accessed=4 * sizes * block_rows * block_cols, transcendentals=0),
        compiler_params=pltpu.CompilerParams(vmem_limit_bytes=VMEM_LIMIT),
    )(half_widths, baseline, above, below, beside)
    depth = 8 * LANES
    own_rows = block_rows + HALO
    return pl.pallas_call(
        functools.partial(scan_kernel, sides),
        in_specs=[scalars, whole, pl.BlockSpec(memory_space=pltpu.HBM)],
        out_specs=pl.BlockSpec(memory_space=pltpu.HBM),
        scratch_shapes=[
            pltpu.VMEM(field, F32),
            pltpu.SemaphoreType.DMA((sizes,)),
            pltpu.SemaphoreType.DMA((sizes,)),
            prefix,
            window,
            pltpu.VMEM((places, chunk_rows, LANES), jnp.int32),
            pltpu.VMEM((places, chunk_rows, LANES), F32),
            pltpu.VMEM((2 * own_rows, depth), BF16),
            pltpu.VMEM((block_cols, depth), BF16),
            pltpu.VMEM((2 * own_rows, block_cols), F32),
            pltpu.VMEM((2 * HALO, block_cols), F32),
            pltpu.VMEM((2 * own_rows, LANES), F32),
            pltpu.VMEM((2 * HALO, LANES), F32),
        ],
        out_shape=jax.ShapeDtypeStruct(field, F32),
        compiler_params=pltpu.CompilerParams(vmem_limit_bytes=VMEM_LIMIT),
    )(half_widths, got, boxes)


def solution(mesh):
    in_specs = (
        P(("groups", "row", "col", "claim"), None, None),
        P(("groups", "row", "col", "claim"), None, None),
        P(("groups", "row", "col", "claim"), None),
        P(("groups", "row", "claim"), "col"),
        P(),
    )
    out_specs = P(None, ("groups", "row", "claim"), "col")
    body = functools.partial(shards, mesh.shape["row"], mesh.shape["col"])
    return jax.shard_map(body, mesh=mesh, in_specs=in_specs, out_specs=out_specs, check_vma=False)
```

```python
import functools

import jax
import jax.numpy as jnp
from jax import lax
from jax.experimental import pallas as pl
from jax.experimental.pallas import tpu as pltpu
from jax.sharding import PartitionSpec as P

HALO = 64
LANES = 128
CODE = 4096
ROW_BIAS = 256
COL_BIAS = 1024
TINY = 1e-30
VMEM_LIMIT = 52 * 1024 * 1024
F32 = jnp.float32
BF16 = jnp.bfloat16


def side_tiles(cols):
    return min(cols - 1, 2)


def pieces_of(dest, rows, cols):
    row, col, claim = dest
    other = row - 1 if claim == 0 else row + 1
    sides = [(col, 0)]
    if cols == 2:
        sides.append((1 - col, -1 if col == 1 else 1))
    elif cols > 2:
        sides += [(col - 1, -1), (col + 1, 1)]
    found = []
    for tile_row, vertical in ((row, 0), (other, 1)):
        for tile_col, side in sides:
            there = 0 <= tile_row < rows and 0 <= tile_col < cols
            found.append((tile_row * cols + tile_col if there else None, vertical, side))
    return found


def pack_kernel(rows, cols, block_rows, block_cols, cell_ref, weight_ref, count_ref, out_ref):
    cell = cell_ref[0]
    tiles, slots = cell.shape
    slot = lax.broadcasted_iota(jnp.int32, (1, slots), 1)
    weights = [jnp.where(slot < count_ref[0, tile], weight_ref[0, tile : tile + 1, :], 0.0) for tile in range(tiles)]
    tile_row = lax.div(cell, block_cols)
    tile_col = lax.rem(cell, block_cols)
    codes = {}
    for claim in (0, 1):
        for vertical in (0, 1):
            if vertical:
                first = 2 * block_rows - HALO if claim == 0 else 0
            else:
                first = 0 if claim == 0 else block_rows - HALO
            for side in (-1, 0, 1):
                shift = {-1: HALO - block_cols, 0: 0, 1: HALO}[side]
                row_code = (tile_row + (ROW_BIAS - first)) * CODE
                codes[claim, vertical, side] = (row_code + tile_col + (shift + COL_BIAS)).astype(F32)
    zero = jnp.zeros((1, slots), F32)
    index = 0
    for row in range(rows):
        for col in range(cols):
            for claim in (0, 1):
                for place, (tile, vertical, side) in enumerate(pieces_of((row, col, claim), rows, cols)):
                    there = tile is not None
                    code = codes[claim, vertical, side][tile : tile + 1] if there else zero
                    out_ref[index, 2 * place : 2 * place + 1, :] = code
                    out_ref[index, 2 * place + 1 : 2 * place + 2, :] = weights[tile] if there else zero
                index += 1


def halves(value):
    high = value.astype(BF16)
    return high, (value - high.astype(F32)).astype(BF16)


def row_prefix(window, prefix):
    side, rows, _ = window.shape
    side -= 1
    lane = lax.broadcasted_iota(jnp.int32, (rows, LANES), 1)
    sub = lax.broadcasted_iota(jnp.int32, (rows // 8, 8, LANES), 1)
    before = window[side]
    for block in range(side + 1):
        after = window[side] if block == side else pltpu.roll(window[block], HALO, axis=1)
        cells = jnp.where(lane < HALO, before, after).reshape(-1, 8, LANES)
        before = after
        for hop in (1, 2, 4):
            cells = cells + jnp.where(sub >= hop, pltpu.roll(cells, hop, axis=1), 0.0)
        carry = jnp.zeros((8, LANES), F32)
        prefix[block, 0:8, :] = carry
        for tile in range(rows // 8):
            total = cells[tile] + carry
            prefix[block, 8 * tile + 8 : 8 * tile + 16, :] = total
            carry = jnp.broadcast_to(total[7:8], (8, LANES))


def band_of(half):
    here = lax.broadcasted_iota(jnp.int32, (LANES, LANES), 0)
    there = lax.broadcasted_iota(jnp.int32, (LANES, LANES), 1)
    gap = here - there
    both = [jnp.where(jnp.abs(gap + shift) <= half, 1.0, 0.0) for shift in (-HALO, LANES - HALO)]
    band = jnp.concatenate(both, axis=1).astype(BF16)
    return jnp.concatenate([band, band], axis=0)


def column_boxes(prefix, half, block_rows, use):
    band = band_of(half)
    before = None
    for block in range(prefix.shape[0]):
        lower = prefix[block, pl.ds(HALO + 8 + half, block_rows), :]
        upper = prefix[block, pl.ds(HALO + 7 - half, block_rows), :]
        product = jnp.dot(
            jnp.concatenate(halves(lower - upper), axis=1), band, preferred_element_type=F32
        )
        if block > 0:
            use(block - 1, before + product[:, LANES:])
        before = product[:, :LANES]


def lanes_of(block):
    return slice(block * LANES, (block + 1) * LANES)


def base_kernel(halves_ref, base_ref, above_ref, below_ref, beside_ref, out_ref, buffer, sems, window, prefix):
    block_rows, block_cols = base_ref.shape
    blocks = block_cols // LANES
    for block in range(blocks):
        window[block, 0:HALO, :] = above_ref[:, lanes_of(block)]
        window[block, HALO : HALO + block_rows, :] = base_ref[:, lanes_of(block)]
        window[block, HALO + block_rows :, :] = below_ref[:, lanes_of(block)]
    window[blocks] = beside_ref[...]
    row_prefix(window, prefix)
    sizes = buffer.shape[0]

    def one_size(step, _):
        def use(block, boxes):
            buffer[step, :, lanes_of(block)] = boxes

        column_boxes(prefix, halves_ref[step], block_rows, use)
        pltpu.make_async_copy(buffer.at[step], out_ref.at[step], sems.at[step]).start()
        return 0

    lax.fori_loop(0, sizes, one_size, 0, unroll=2)

    def finish(step, _):
        pltpu.make_async_copy(buffer.at[step], out_ref.at[step], sems.at[step]).wait()
        return 0

    lax.fori_loop(0, sizes, finish, 0)


def pack16(row):
    return jnp.broadcast_to(row.astype(F32), (16, row.shape[1])).astype(BF16)


def tall(packed, size):
    return jnp.concatenate([packed] * (size // 16), axis=0)


def scan_kernel(
    sides, halves_ref, got_ref, boxes_ref, out_ref, buffer, read_sems, write_sems, prefix, window, code_s, weight_s, *spaces
):
    sizes, block_rows, block_cols = buffer.shape
    blocks = block_cols // LANES
    pairs = blocks // 2
    senders, _, slots = got_ref.shape
    own_rows = block_rows + HALO
    claim = lax.axis_index("claim")

    def read_of(step):
        return pltpu.make_async_copy(boxes_ref.at[step], buffer.at[step], read_sems.at[step])

    def write_of(step):
        return pltpu.make_async_copy(buffer.at[step], out_ref.at[step], write_sems.at[step])

    def begin(step, _):
        read_of(step).start()
        return 0

    lax.fori_loop(0, sizes, begin, 0)
    places = 2 * sides + 2
    for place in range(places):
        code = got_ref[:, 2 * place, :].astype(jnp.int32)
        weight = got_ref[:, 2 * place + 1, :]
        split = senders // 2
        for ref, value in ((code_s, code), (weight_s, weight)):
            ref[place, 0:senders, :] = value[:, :LANES]
            ref[place, senders : senders + split, 0 : slots - LANES] = value[:split, LANES:]
            ref[place, senders : senders + split, slots - LANES : LANES] = value[split:, LANES:]
    depth = spaces[0].shape[1] // LANES
    chunks = code_s.shape[1] // depth
    one, none = jnp.ones((), BF16), jnp.zeros((), BF16)

    def iota16(size):
        return lax.broadcasted_iota(jnp.int32, (size, LANES), 0).astype(F32).astype(BF16)

    def add_chunk(chunk, fresh):
        for place in range(places):
            vertical, side = divmod(place, sides + 1)
            kind = 2 * vertical + (side > 0)
            row_hot, col_hot, acc = spaces[3 * kind : 3 * kind + 3]
            rows = HALO if vertical else own_rows
            here = pl.ds(pl.multiple_of(chunk * depth, 8), depth)
            code = code_s[place, here, :]
            weight = weight_s[place, here, :]
            row = lax.shift_right_logical(code, 12) - ROW_BIAS
            col = (code & (CODE - 1)) - COL_BIAS
            high = weight.astype(BF16).astype(F32)
            parts = (high, weight - high)
            width = LANES if side else 2 * LANES
            if side:
                inside = jnp.where(lax.shift_right_arithmetic(col, 7) == 0, col, -1)
            else:
                inside = col & (2 * LANES - 1)
                pair = lax.shift_right_arithmetic(col, 8)
            row_iota, col_iota = iota16(rows), iota16(width)
            for part in range(depth):
                at, only = lanes_of(part), slice(part, part + 1)
                row_hit = tall(pack16(row[only]), rows) == row_iota
                col_hit = tall(pack16(inside[only]), width) == col_iota
                if side:
                    row_hot[:, at] = jnp.where(row_hit, one, none)
                    for index, value in enumerate(parts):
                        col_hot[lanes_of(index), at] = jnp.where(col_hit, tall(pack16(value[only]), LANES), none)
                else:
                    col_hot[:, at] = jnp.where(col_hit, one, none)
                    for group in range(pairs):
                        for index, value in enumerate(parts):
                            mine = jnp.where(pair[only] == group, value[only], 0.0)
                            start = (2 * group + index) * rows
                            row_hot[start : start + rows, at] = jnp.where(row_hit, tall(pack16(mine), rows), none)
            product = lax.dot_general(
                row_hot[...], col_hot[...], (((1,), (1,)), ((), ())), preferred_element_type=F32
            )
            acc[...] = product if fresh and side < 2 else acc[...] + product
        return 0

    add_chunk(0, True)
    if chunks > 1:
        lax.fori_loop(1, chunks, lambda chunk, _: add_chunk(chunk, False), 0)
    own_acc, side_acc, far_acc, corner_acc = spaces[2::3]
    own_at = pl.multiple_of((1 - claim) * HALO, HALO)
    far_at = pl.multiple_of(claim * own_rows, HALO)
    for block in range(blocks):
        group, here = block // 2, lanes_of(block % 2)
        for acc, rows, start in ((own_acc, own_rows, own_at), (far_acc, HALO, far_at)):
            top = 2 * group * rows
            window[block, pl.ds(start, rows), :] = acc[top : top + rows, here] + acc[top + rows : top + 2 * rows, here]
    window[blocks, pl.ds(own_at, own_rows), :] = side_acc[:, :LANES] + side_acc[:, LANES:]
    window[blocks, pl.ds(far_at, HALO), :] = corner_acc[:, :LANES] + corner_acc[:, LANES:]
    row_prefix(window, prefix)

    def one_size(step, _):
        half = halves_ref[step]
        inverse = 1.0 / (2 * half + 1).astype(F32)
        read_of(step).wait()

        def use(block, counts):
            here = lanes_of(block)
            base = buffer[step, :, here]
            gain = jnp.log(jnp.maximum(counts, TINY)) - jnp.log(base) - 1.0
            buffer[step, :, here] = (counts * gain + base) * inverse

        column_boxes(prefix, half, block_rows, use)
        write_of(step).start()
        return 0

    lax.fori_loop(0, sizes, one_size, 0, unroll=2)

    def finish(step, _):
        write_of(step).wait()
        return 0

    lax.fori_loop(0, sizes, finish, 0)


def shards(rows, cols, claim_cell, claim_weight, claim_count, baseline, half_widths):
    block_rows, block_cols = baseline.shape
    slots = claim_cell.shape[2]
    sides = side_tiles(cols)
    devices = rows * cols * 2
    whole = pl.BlockSpec(memory_space=pltpu.VMEM)
    scalars = pl.BlockSpec(memory_space=pltpu.SMEM)
    sent = pl.pallas_call(
        functools.partial(pack_kernel, rows, cols, block_rows, block_cols),
        in_specs=[whole, whole, scalars],
        out_shape=jax.ShapeDtypeStruct((devices, 4 * (sides + 1), slots), F32),
    )(claim_cell, claim_weight, claim_count)

    strips = rows * 2
    down = [(i, i + 1) for i in range(strips - 1)]
    up = [(i + 1, i) for i in range(strips - 1)]
    above = lax.ppermute(baseline[block_rows - HALO :], ("row", "claim"), down)
    below = lax.ppermute(baseline[:HALO], ("row", "claim"), up)
    sent, above, below = lax.optimization_barrier((sent, above, below))
    pieces = (above, baseline, below)
    first = jnp.concatenate([piece[:, :HALO] for piece in pieces], axis=0)
    last = jnp.concatenate([piece[:, block_cols - HALO :] for piece in pieces], axis=0)
    if cols == 2:
        col = lax.axis_index("col")
        beside = lax.ppermute(
            jnp.concatenate([jnp.where(col == 0, last, 0.0), jnp.where(col == 1, first, 0.0)], axis=1),
            "col",
            [(0, 1), (1, 0)],
        )
    else:
        beside = jnp.concatenate(
            [
                lax.ppermute(last, "col", [(i, i + 1) for i in range(cols - 1)]),
                lax.ppermute(first, "col", [(i + 1, i) for i in range(cols - 1)]),
            ],
            axis=1,
        )
    got = lax.all_to_all(sent, ("row", "col", "claim"), split_axis=0, concat_axis=0, tiled=True)
    sizes = half_widths.shape[0]
    blocks = block_cols // LANES
    places = 2 * (sides + 1)
    chunk_rows = devices * slots // LANES
    window = pltpu.VMEM((blocks + 1, 2 * block_rows, LANES), F32)
    prefix = pltpu.VMEM((blocks + 1, 2 * block_rows + 8, LANES), F32)
    field = (sizes, block_rows, block_cols)
    work = 2 * sizes * block_rows * (blocks + 1) * (2 * LANES) ** 2
    boxes = pl.pallas_call(
        base_kernel,
        in_specs=[scalars] + [whole] * 4,
        out_specs=pl.BlockSpec(memory_space=pltpu.HBM),
        out_shape=jax.ShapeDtypeStruct(field, F32),
        scratch_shapes=[pltpu.VMEM(field, F32), pltpu.SemaphoreType.DMA((sizes,)), window, prefix],
        cost_estimate=pl.CostEstimate(flops=work, bytes_accessed=4 * sizes * block_rows * block_cols, transcendentals=0),
        compiler_params=pltpu.CompilerParams(vmem_limit_bytes=VMEM_LIMIT),
    )(half_widths, baseline, above, below, beside)
    depth = LANES * max(d for d in (8, 16, 24) if chunk_rows % d == 0)
    spaces = []
    for rows in (block_rows + HALO, HALO):
        for tall_rows in (rows * blocks, rows):
            spaces += [
                pltpu.VMEM((tall_rows, depth), BF16),
                pltpu.VMEM((2 * LANES, depth), BF16),
                pltpu.VMEM((tall_rows, 2 * LANES), F32),
            ]
    return pl.pallas_call(
        functools.partial(scan_kernel, sides),
        in_specs=[scalars, whole, pl.BlockSpec(memory_space=pltpu.HBM)],
        out_specs=pl.BlockSpec(memory_space=pltpu.HBM),
        scratch_shapes=[
            pltpu.VMEM(field, F32),
            pltpu.SemaphoreType.DMA((sizes,)),
            pltpu.SemaphoreType.DMA((sizes,)),
            prefix,
            window,
            pltpu.VMEM((places, chunk_rows, LANES), jnp.int32),
            pltpu.VMEM((places, chunk_rows, LANES), F32),
            *spaces,
        ],
        out_shape=jax.ShapeDtypeStruct(field, F32),
        compiler_params=pltpu.CompilerParams(vmem_limit_bytes=VMEM_LIMIT),
    )(half_widths, got, boxes)


def solution(mesh):
    in_specs = (
        P(("groups", "row", "col", "claim"), None, None),
        P(("groups", "row", "col", "claim"), None, None),
        P(("groups", "row", "col", "claim"), None),
        P(("groups", "row", "claim"), "col"),
        P(),
    )
    out_specs = P(None, ("groups", "row", "claim"), "col")
    body = functools.partial(shards, mesh.shape["row"], mesh.shape["col"])
    return jax.shard_map(body, mesh=mesh, in_specs=in_specs, out_specs=out_specs, check_vma=False)
```

```python
import functools

import jax
import jax.numpy as jnp
from jax import lax
from jax.experimental import pallas as pl
from jax.experimental.pallas import tpu as pltpu
from jax.sharding import PartitionSpec as P

HALO = 64
LANES = 128
CODE = 4096
ROW_BIAS = 256
COL_BIAS = 1024
TINY = 1e-30
BIN_VMEM = 36 * 1024 * 1024
SCAN_VMEM = 24 * 1024 * 1024
F32 = jnp.float32
BF16 = jnp.bfloat16


def side_tiles(cols):
    return min(cols - 1, 2)


def pieces_of(dest, rows, cols):
    row, col, claim = dest
    other = row - 1 if claim == 0 else row + 1
    sides = [(col, 0)]
    if cols == 2:
        sides.append((1 - col, -1 if col == 1 else 1))
    elif cols > 2:
        sides += [(col - 1, -1), (col + 1, 1)]
    found = []
    for tile_row, vertical in ((row, 0), (other, 1)):
        for tile_col, side in sides:
            there = 0 <= tile_row < rows and 0 <= tile_col < cols
            found.append((tile_row * cols + tile_col if there else None, vertical, side))
    return found


def pack_kernel(rows, cols, block_rows, block_cols, cell_ref, weight_ref, count_ref, out_ref):
    cell = cell_ref[0]
    tiles, slots = cell.shape
    slot = lax.broadcasted_iota(jnp.int32, (1, slots), 1)
    weights = [jnp.where(slot < count_ref[0, tile], weight_ref[0, tile : tile + 1, :], 0.0) for tile in range(tiles)]
    tile_row = lax.div(cell, block_cols)
    tile_col = lax.rem(cell, block_cols)
    codes = {}
    for claim in (0, 1):
        for vertical in (0, 1):
            if vertical:
                first = 2 * block_rows - HALO if claim == 0 else 0
            else:
                first = 0 if claim == 0 else block_rows - HALO
            for side in (-1, 0, 1):
                shift = {-1: HALO - block_cols, 0: 0, 1: HALO}[side]
                row_code = (tile_row + (ROW_BIAS - first)) * CODE
                codes[claim, vertical, side] = (row_code + tile_col + (shift + COL_BIAS)).astype(F32)
    zero = jnp.zeros((1, slots), F32)
    index = 0
    for row in range(rows):
        for col in range(cols):
            for claim in (0, 1):
                for place, (tile, vertical, side) in enumerate(pieces_of((row, col, claim), rows, cols)):
                    there = tile is not None
                    code = codes[claim, vertical, side][tile : tile + 1] if there else zero
                    out_ref[index, 2 * place : 2 * place + 1, :] = code
                    out_ref[index, 2 * place + 1 : 2 * place + 2, :] = weights[tile] if there else zero
                index += 1


def halves(value):
    high = value.astype(BF16)
    return high, (value - high.astype(F32)).astype(BF16)


def row_prefix(window, prefix):
    side, rows, _ = window.shape
    side -= 1
    lane = lax.broadcasted_iota(jnp.int32, (rows, LANES), 1)
    sub = lax.broadcasted_iota(jnp.int32, (rows // 8, 8, LANES), 1)
    before = window[side]
    for block in range(side + 1):
        after = window[side] if block == side else pltpu.roll(window[block], HALO, axis=1)
        cells = jnp.where(lane < HALO, before, after).reshape(-1, 8, LANES)
        before = after
        for hop in (1, 2, 4):
            cells = cells + jnp.where(sub >= hop, pltpu.roll(cells, hop, axis=1), 0.0)
        carry = jnp.zeros((8, LANES), F32)
        prefix[block, 0:8, :] = carry
        for tile in range(rows // 8):
            total = cells[tile] + carry
            prefix[block, 8 * tile + 8 : 8 * tile + 16, :] = total
            carry = jnp.broadcast_to(total[7:8], (8, LANES))


def band_of(half):
    here = lax.broadcasted_iota(jnp.int32, (LANES, LANES), 0)
    there = lax.broadcasted_iota(jnp.int32, (LANES, LANES), 1)
    gap = here - there
    both = [jnp.where(jnp.abs(gap + shift) <= half, 1.0, 0.0) for shift in (-HALO, LANES - HALO)]
    band = jnp.concatenate(both, axis=1).astype(BF16)
    return jnp.concatenate([band, band], axis=0)


def lanes_of(block):
    return slice(block * LANES, (block + 1) * LANES)


def strips_kernel(sent_ref, base_ref, top_ref, bottom_ref, edges_ref):
    block_rows, block_cols = base_ref.shape
    top_ref[...] = base_ref[:HALO]
    bottom_ref[...] = base_ref[block_rows - HALO :]
    lane = lax.broadcasted_iota(jnp.int32, (block_rows, LANES), 1)
    last = pltpu.roll(base_ref[:, block_cols - LANES :], HALO, axis=1)
    first = pltpu.roll(base_ref[:, :LANES], HALO, axis=1)
    edges_ref[...] = jnp.where(lane < HALO, last, first)


def pack16(row):
    return jnp.broadcast_to(row.astype(F32), (16, row.shape[1])).astype(BF16)


def tall(packed, size):
    return jnp.concatenate([packed] * (size // 16), axis=0)


def bin_kernel(sides, got_ref, prefix, window, code_s, weight_s, *spaces):
    blocks = window.shape[0] - 1
    block_rows = window.shape[1] // 2
    pairs = blocks // 2
    senders, _, slots = got_ref.shape
    own_rows = block_rows + HALO
    claim = lax.axis_index("claim")
    places = 2 * sides + 2
    for place in range(places):
        code = got_ref[:, 2 * place, :].astype(jnp.int32)
        weight = got_ref[:, 2 * place + 1, :]
        split = senders // 2
        for ref, value in ((code_s, code), (weight_s, weight)):
            ref[place, 0:senders, :] = value[:, :LANES]
            ref[place, senders : senders + split, 0 : slots - LANES] = value[:split, LANES:]
            ref[place, senders : senders + split, slots - LANES : LANES] = value[split:, LANES:]
    depth = spaces[0].shape[1] // LANES
    chunks = code_s.shape[1] // depth
    one, none = jnp.ones((), BF16), jnp.zeros((), BF16)

    def iota16(size):
        return lax.broadcasted_iota(jnp.int32, (size, LANES), 0).astype(F32).astype(BF16)

    def add_chunk(chunk, fresh):
        for place in range(places):
            vertical, side = divmod(place, sides + 1)
            kind = 2 * vertical + (side > 0)
            row_hot, col_hot, acc = spaces[3 * kind : 3 * kind + 3]
            rows = HALO if vertical else own_rows
            here = pl.ds(pl.multiple_of(chunk * depth, 8), depth)
            code = code_s[place, here, :]
            weight = weight_s[place, here, :]
            row = lax.shift_right_logical(code, 12) - ROW_BIAS
            col = (code & (CODE - 1)) - COL_BIAS
            high = weight.astype(BF16).astype(F32)
            parts = (high, weight - high)
            width = LANES if side else 2 * LANES
            if side:
                inside = jnp.where(lax.shift_right_arithmetic(col, 7) == 0, col, -1)
            else:
                inside = col & (2 * LANES - 1)
                pair = lax.shift_right_arithmetic(col, 8)
            row_iota, col_iota = iota16(rows), iota16(width)
            for part in range(depth):
                at, only = lanes_of(part), slice(part, part + 1)
                row_hit = tall(pack16(row[only]), rows) == row_iota
                col_hit = tall(pack16(inside[only]), width) == col_iota
                if side:
                    row_hot[:, at] = jnp.where(row_hit, one, none)
                    for index, value in enumerate(parts):
                        col_hot[lanes_of(index), at] = jnp.where(col_hit, tall(pack16(value[only]), LANES), none)
                else:
                    col_hot[:, at] = jnp.where(col_hit, one, none)
                    for group in range(pairs):
                        for index, value in enumerate(parts):
                            mine = jnp.where(pair[only] == group, value[only], 0.0)
                            start = (2 * group + index) * rows
                            row_hot[start : start + rows, at] = jnp.where(row_hit, tall(pack16(mine), rows), none)
            product = lax.dot_general(
                row_hot[...], col_hot[...], (((1,), (1,)), ((), ())), preferred_element_type=F32
            )
            acc[...] = product if fresh and side < 2 else acc[...] + product
        return 0

    add_chunk(0, True)
    if chunks > 1:
        lax.fori_loop(1, chunks, lambda chunk, _: add_chunk(chunk, False), 0)
    own_acc, side_acc, far_acc, corner_acc = spaces[2::3]
    own_at = pl.multiple_of((1 - claim) * HALO, HALO)
    far_at = pl.multiple_of(claim * own_rows, HALO)
    for block in range(blocks):
        group, here = block // 2, lanes_of(block % 2)
        for acc, rows, start in ((own_acc, own_rows, own_at), (far_acc, HALO, far_at)):
            top = 2 * group * rows
            window[block, pl.ds(start, rows), :] = acc[top : top + rows, here] + acc[top + rows : top + 2 * rows, here]
    window[blocks, pl.ds(own_at, own_rows), :] = side_acc[:, :LANES] + side_acc[:, LANES:]
    window[blocks, pl.ds(far_at, HALO), :] = corner_acc[:, :LANES] + corner_acc[:, LANES:]
    row_prefix(window, prefix)


def scan_kernel(
    group, halves_ref, counts_ref, base_ref, above_ref, below_ref, beside_ref, out_ref, buffer, sems, window, prefix
):
    sizes, block_rows, block_cols = buffer.shape
    blocks = block_cols // LANES
    for block in range(blocks):
        window[block, 0:HALO, :] = above_ref[:, lanes_of(block)]
        window[block, HALO : HALO + block_rows, :] = base_ref[:, lanes_of(block)]
        window[block, HALO + block_rows :, :] = below_ref[:, lanes_of(block)]
    window[blocks] = beside_ref[...]
    row_prefix(window, prefix)

    def one_size(step, _):
        half = halves_ref[step]
        inverse = 1.0 / (2 * half + 1).astype(F32)
        band = band_of(half)
        before = None
        for first in range(0, blocks + 1, group):
            some = range(first, min(first + group, blocks + 1))
            strips = []
            for block in some:
                for field in (counts_ref, prefix):
                    lower = field[block, pl.ds(HALO + 8 + half, block_rows), :]
                    upper = field[block, pl.ds(HALO + 7 - half, block_rows), :]
                    strips.append(jnp.concatenate(halves(lower - upper), axis=1))
            product = jnp.dot(jnp.concatenate(strips, axis=0), band, preferred_element_type=F32)
            for index, block in enumerate(some):
                now = [product[(2 * index + f) * block_rows : (2 * index + f + 1) * block_rows] for f in (0, 1)]
                if block > 0:
                    counts, base = (old[:, :LANES] + new[:, LANES:] for old, new in zip(before, now))
                    gain = jnp.log(jnp.maximum(counts, TINY)) - jnp.log(base) - 1.0
                    buffer[step, :, lanes_of(block - 1)] = (counts * gain + base) * inverse
                before = now
        pltpu.make_async_copy(buffer.at[step], out_ref.at[step], sems.at[step]).start()
        return 0

    lax.fori_loop(0, sizes, one_size, 0, unroll=2)

    def finish(step, _):
        pltpu.make_async_copy(buffer.at[step], out_ref.at[step], sems.at[step]).wait()
        return 0

    lax.fori_loop(0, sizes, finish, 0)


def shards(rows, cols, claim_cell, claim_weight, claim_count, baseline, half_widths):
    block_rows, block_cols = baseline.shape
    slots = claim_cell.shape[2]
    sides = side_tiles(cols)
    devices = rows * cols * 2
    whole = pl.BlockSpec(memory_space=pltpu.VMEM)
    scalars = pl.BlockSpec(memory_space=pltpu.SMEM)
    sent = pl.pallas_call(
        functools.partial(pack_kernel, rows, cols, block_rows, block_cols),
        in_specs=[whole, whole, scalars],
        out_shape=jax.ShapeDtypeStruct((devices, 4 * (sides + 1), slots), F32),
    )(claim_cell, claim_weight, claim_count)

    got = lax.all_to_all(sent, ("row", "col", "claim"), split_axis=0, concat_axis=0, tiled=True)
    top, bottom, edges = pl.pallas_call(
        strips_kernel,
        in_specs=[pl.BlockSpec(memory_space=pltpu.HBM), whole],
        out_specs=[whole] * 3,
        out_shape=[
            jax.ShapeDtypeStruct((HALO, block_cols), F32),
            jax.ShapeDtypeStruct((HALO, block_cols), F32),
            jax.ShapeDtypeStruct((block_rows, LANES), F32),
        ],
    )(sent, baseline)
    strips = rows * 2
    above = lax.ppermute(bottom, ("row", "claim"), [(i, i + 1) for i in range(strips - 1)])
    below = lax.ppermute(top, ("row", "claim"), [(i + 1, i) for i in range(strips - 1)])
    last = jnp.concatenate([above[:, block_cols - HALO :], edges[:, :HALO], below[:, block_cols - HALO :]], axis=0)
    first = jnp.concatenate([above[:, :HALO], edges[:, HALO:], below[:, :HALO]], axis=0)
    if cols == 2:
        col = lax.axis_index("col")
        beside = lax.ppermute(
            jnp.concatenate([jnp.where(col == 0, last, 0.0), jnp.where(col == 1, first, 0.0)], axis=1),
            "col",
            [(0, 1), (1, 0)],
        )
    else:
        beside = jnp.concatenate(
            [
                lax.ppermute(last, "col", [(i, i + 1) for i in range(cols - 1)]),
                lax.ppermute(first, "col", [(i + 1, i) for i in range(cols - 1)]),
            ],
            axis=1,
        )
    sizes = half_widths.shape[0]
    blocks = block_cols // LANES
    places = 2 * (sides + 1)
    chunk_rows = devices * slots // LANES
    window = pltpu.VMEM((blocks + 1, 2 * block_rows, LANES), F32)
    prefix = (blocks + 1, 2 * block_rows + 8, LANES)
    depth = LANES * max(d for d in (8, 16, 24) if chunk_rows % d == 0)
    spaces = []
    for rows_of in (block_rows + HALO, HALO):
        for tall_rows in (rows_of * blocks, rows_of):
            spaces += [
                pltpu.VMEM((tall_rows, depth), BF16),
                pltpu.VMEM((2 * LANES, depth), BF16),
                pltpu.VMEM((tall_rows, 2 * LANES), F32),
            ]
    counts = pl.pallas_call(
        functools.partial(bin_kernel, sides),
        in_specs=[whole],
        out_specs=whole,
        out_shape=jax.ShapeDtypeStruct(prefix, F32),
        scratch_shapes=[
            window,
            pltpu.VMEM((places, chunk_rows, LANES), jnp.int32),
            pltpu.VMEM((places, chunk_rows, LANES), F32),
            *spaces,
        ],
        compiler_params=pltpu.CompilerParams(vmem_limit_bytes=BIN_VMEM),
    )(got)
    field = (sizes, block_rows, block_cols)
    return pl.pallas_call(
        functools.partial(scan_kernel, 3),
        in_specs=[scalars] + [whole] * 5,
        out_specs=pl.BlockSpec(memory_space=pltpu.HBM),
        scratch_shapes=[
            pltpu.VMEM(field, F32),
            pltpu.SemaphoreType.DMA((sizes,)),
            window,
            pltpu.VMEM(prefix, F32),
        ],
        out_shape=jax.ShapeDtypeStruct(field, F32),
        compiler_params=pltpu.CompilerParams(vmem_limit_bytes=SCAN_VMEM),
    )(half_widths, counts, baseline, above, below, beside)


def solution(mesh):
    in_specs = (
        P(("groups", "row", "col", "claim"), None, None),
        P(("groups", "row", "col", "claim"), None, None),
        P(("groups", "row", "col", "claim"), None),
        P(("groups", "row", "claim"), "col"),
        P(),
    )
    out_specs = P(None, ("groups", "row", "claim"), "col")
    body = functools.partial(shards, mesh.shape["row"], mesh.shape["col"])
    return jax.shard_map(body, mesh=mesh, in_specs=in_specs, out_specs=out_specs, check_vma=False)
```

```python
import functools

import jax
import jax.numpy as jnp
from jax import lax
from jax.experimental import pallas as pl
from jax.experimental.pallas import tpu as pltpu
from jax.sharding import PartitionSpec as P

HALO = 64
LANES = 128
CODE = 4096
ROW_BIAS = 256
COL_BIAS = 1024
TINY = 1e-30
BASE_VMEM = 8 * 1024 * 1024
BIN_VMEM = 36 * 1024 * 1024
SCAN_VMEM = 24 * 1024 * 1024
F32 = jnp.float32
BF16 = jnp.bfloat16


def side_tiles(cols):
    return min(cols - 1, 2)


def pieces_of(dest, rows, cols):
    row, col, claim = dest
    other = row - 1 if claim == 0 else row + 1
    sides = [(col, 0)]
    if cols == 2:
        sides.append((1 - col, -1 if col == 1 else 1))
    elif cols > 2:
        sides += [(col - 1, -1), (col + 1, 1)]
    found = []
    for tile_row, vertical in ((row, 0), (other, 1)):
        for tile_col, side in sides:
            there = 0 <= tile_row < rows and 0 <= tile_col < cols
            found.append((tile_row * cols + tile_col if there else None, vertical, side))
    return found


def pack_kernel(rows, cols, block_rows, block_cols, cell_ref, weight_ref, count_ref, out_ref):
    cell = cell_ref[0]
    tiles, slots = cell.shape
    slot = lax.broadcasted_iota(jnp.int32, (1, slots), 1)
    weights = [jnp.where(slot < count_ref[0, tile], weight_ref[0, tile : tile + 1, :], 0.0) for tile in range(tiles)]
    tile_row = lax.div(cell, block_cols)
    tile_col = lax.rem(cell, block_cols)
    codes = {}
    for claim in (0, 1):
        for vertical in (0, 1):
            if vertical:
                first = 2 * block_rows - HALO if claim == 0 else 0
            else:
                first = 0 if claim == 0 else block_rows - HALO
            for side in (-1, 0, 1):
                shift = {-1: HALO - block_cols, 0: 0, 1: HALO}[side]
                row_code = (tile_row + (ROW_BIAS - first)) * CODE
                codes[claim, vertical, side] = (row_code + tile_col + (shift + COL_BIAS)).astype(F32)
    zero = jnp.zeros((1, slots), F32)
    index = 0
    for row in range(rows):
        for col in range(cols):
            for claim in (0, 1):
                for place, (tile, vertical, side) in enumerate(pieces_of((row, col, claim), rows, cols)):
                    there = tile is not None
                    code = codes[claim, vertical, side][tile : tile + 1] if there else zero
                    out_ref[index, 2 * place : 2 * place + 1, :] = code
                    out_ref[index, 2 * place + 1 : 2 * place + 2, :] = weights[tile] if there else zero
                index += 1


def halves(value):
    high = value.astype(BF16)
    return high, (value - high.astype(F32)).astype(BF16)


def row_prefix(window, prefix):
    side, rows, _ = window.shape
    side -= 1
    lane = lax.broadcasted_iota(jnp.int32, (rows, LANES), 1)
    sub = lax.broadcasted_iota(jnp.int32, (rows // 8, 8, LANES), 1)
    before = window[side]
    for block in range(side + 1):
        after = window[side] if block == side else pltpu.roll(window[block], HALO, axis=1)
        cells = jnp.where(lane < HALO, before, after).reshape(-1, 8, LANES)
        before = after
        for hop in (1, 2, 4):
            cells = cells + jnp.where(sub >= hop, pltpu.roll(cells, hop, axis=1), 0.0)
        carry = jnp.zeros((8, LANES), F32)
        prefix[block, 0:8, :] = carry
        for tile in range(rows // 8):
            total = cells[tile] + carry
            prefix[block, 8 * tile + 8 : 8 * tile + 16, :] = total
            carry = jnp.broadcast_to(total[7:8], (8, LANES))


def band_of(half):
    here = lax.broadcasted_iota(jnp.int32, (LANES, LANES), 0)
    there = lax.broadcasted_iota(jnp.int32, (LANES, LANES), 1)
    gap = here - there
    both = [jnp.where(jnp.abs(gap + shift) <= half, 1.0, 0.0) for shift in (-HALO, LANES - HALO)]
    band = jnp.concatenate(both, axis=1).astype(BF16)
    return jnp.concatenate([band, band], axis=0)


def lanes_of(block):
    return slice(block * LANES, (block + 1) * LANES)


def base_kernel(halves_ref, base_ref, above_ref, below_ref, beside_ref, prefix, halves_out, window):
    block_rows, block_cols = base_ref.shape
    blocks = block_cols // LANES
    for step in range(halves_ref.shape[0]):
        halves_out[step] = halves_ref[step]
    for block in range(blocks):
        window[block, 0:HALO, :] = above_ref[:, lanes_of(block)]
        window[block, HALO : HALO + block_rows, :] = base_ref[:, lanes_of(block)]
        window[block, HALO + block_rows :, :] = below_ref[:, lanes_of(block)]
    window[blocks] = beside_ref[...]
    row_prefix(window, prefix)


def pack16(row):
    return jnp.broadcast_to(row.astype(F32), (16, row.shape[1])).astype(BF16)


def tall(packed, size):
    return jnp.concatenate([packed] * (size // 16), axis=0)


def bin_kernel(sides, got_ref, prefix, window, code_s, weight_s, *spaces):
    blocks = window.shape[0] - 1
    block_rows = window.shape[1] // 2
    pairs = blocks // 2
    senders, _, slots = got_ref.shape
    own_rows = block_rows + HALO
    claim = lax.axis_index("claim")
    places = 2 * sides + 2
    for place in range(places):
        code = got_ref[:, 2 * place, :].astype(jnp.int32)
        weight = got_ref[:, 2 * place + 1, :]
        split = senders // 2
        for ref, value in ((code_s, code), (weight_s, weight)):
            ref[place, 0:senders, :] = value[:, :LANES]
            ref[place, senders : senders + split, 0 : slots - LANES] = value[:split, LANES:]
            ref[place, senders : senders + split, slots - LANES : LANES] = value[split:, LANES:]
    depth = spaces[0].shape[1] // LANES
    chunks = code_s.shape[1] // depth
    one, none = jnp.ones((), BF16), jnp.zeros((), BF16)

    def iota16(size):
        return lax.broadcasted_iota(jnp.int32, (size, LANES), 0).astype(F32).astype(BF16)

    def add_chunk(chunk, fresh):
        for place in range(places):
            vertical, side = divmod(place, sides + 1)
            kind = 2 * vertical + (side > 0)
            row_hot, col_hot, acc = spaces[3 * kind : 3 * kind + 3]
            rows = HALO if vertical else own_rows
            here = pl.ds(pl.multiple_of(chunk * depth, 8), depth)
            code = code_s[place, here, :]
            weight = weight_s[place, here, :]
            row = lax.shift_right_logical(code, 12) - ROW_BIAS
            col = (code & (CODE - 1)) - COL_BIAS
            high = weight.astype(BF16).astype(F32)
            parts = (high, weight - high)
            width = LANES if side else 2 * LANES
            if side:
                inside = jnp.where(lax.shift_right_arithmetic(col, 7) == 0, col, -1)
            else:
                inside = col & (2 * LANES - 1)
                pair = lax.shift_right_arithmetic(col, 8)
            row_iota, col_iota = iota16(rows), iota16(width)
            for part in range(depth):
                at, only = lanes_of(part), slice(part, part + 1)
                row_hit = tall(pack16(row[only]), rows) == row_iota
                col_hit = tall(pack16(inside[only]), width) == col_iota
                if side:
                    row_hot[:, at] = jnp.where(row_hit, one, none)
                    for index, value in enumerate(parts):
                        col_hot[lanes_of(index), at] = jnp.where(col_hit, tall(pack16(value[only]), LANES), none)
                else:
                    col_hot[:, at] = jnp.where(col_hit, one, none)
                    for group in range(pairs):
                        for index, value in enumerate(parts):
                            mine = jnp.where(pair[only] == group, value[only], 0.0)
                            start = (2 * group + index) * rows
                            row_hot[start : start + rows, at] = jnp.where(row_hit, tall(pack16(mine), rows), none)
            product = lax.dot_general(
                row_hot[...], col_hot[...], (((1,), (1,)), ((), ())), preferred_element_type=F32
            )
            acc[...] = product if fresh and side < 2 else acc[...] + product
        return 0

    add_chunk(0, True)
    if chunks > 1:
        lax.fori_loop(1, chunks, lambda chunk, _: add_chunk(chunk, False), 0)
    own_acc, side_acc, far_acc, corner_acc = spaces[2::3]
    own_at = pl.multiple_of((1 - claim) * HALO, HALO)
    far_at = pl.multiple_of(claim * own_rows, HALO)
    for block in range(blocks):
        group, here = block // 2, lanes_of(block % 2)
        for acc, rows, start in ((own_acc, own_rows, own_at), (far_acc, HALO, far_at)):
            top = 2 * group * rows
            window[block, pl.ds(start, rows), :] = acc[top : top + rows, here] + acc[top + rows : top + 2 * rows, here]
    window[blocks, pl.ds(own_at, own_rows), :] = side_acc[:, :LANES] + side_acc[:, LANES:]
    window[blocks, pl.ds(far_at, HALO), :] = corner_acc[:, :LANES] + corner_acc[:, LANES:]
    row_prefix(window, prefix)


def scan_kernel(group, halves_ref, counts_ref, prefix_ref, out_ref, buffer, sems):
    sizes, block_rows, block_cols = buffer.shape
    blocks = block_cols // LANES

    def one_size(step, _):
        half = halves_ref[step]
        inverse = 1.0 / (2 * half + 1).astype(F32)
        band = band_of(half)
        before = None
        for first in range(0, blocks + 1, group):
            some = range(first, min(first + group, blocks + 1))
            strips = []
            for block in some:
                for field in (counts_ref, prefix_ref):
                    lower = field[block, pl.ds(HALO + 8 + half, block_rows), :]
                    upper = field[block, pl.ds(HALO + 7 - half, block_rows), :]
                    strips.append(jnp.concatenate(halves(lower - upper), axis=1))
            product = jnp.dot(jnp.concatenate(strips, axis=0), band, preferred_element_type=F32)
            for index, block in enumerate(some):
                now = [product[(2 * index + f) * block_rows : (2 * index + f + 1) * block_rows] for f in (0, 1)]
                if block > 0:
                    counts, base = (old[:, :LANES] + new[:, LANES:] for old, new in zip(before, now))
                    gain = jnp.log(jnp.maximum(counts, TINY)) - jnp.log(base) - 1.0
                    buffer[step, :, lanes_of(block - 1)] = (counts * gain + base) * inverse
                before = now
        pltpu.make_async_copy(buffer.at[step], out_ref.at[step], sems.at[step]).start()
        return 0

    lax.fori_loop(0, sizes, one_size, 0, unroll=2)

    def finish(step, _):
        pltpu.make_async_copy(buffer.at[step], out_ref.at[step], sems.at[step]).wait()
        return 0

    lax.fori_loop(0, sizes, finish, 0)


def shards(rows, cols, claim_cell, claim_weight, claim_count, baseline, half_widths):
    block_rows, block_cols = baseline.shape
    slots = claim_cell.shape[2]
    sides = side_tiles(cols)
    devices = rows * cols * 2
    whole = pl.BlockSpec(memory_space=pltpu.VMEM)
    scalars = pl.BlockSpec(memory_space=pltpu.SMEM)
    sent = pl.pallas_call(
        functools.partial(pack_kernel, rows, cols, block_rows, block_cols),
        in_specs=[whole, whole, scalars],
        out_shape=jax.ShapeDtypeStruct((devices, 4 * (sides + 1), slots), F32),
    )(claim_cell, claim_weight, claim_count)

    strips = rows * 2
    above = lax.ppermute(baseline[block_rows - HALO :], ("row", "claim"), [(i, i + 1) for i in range(strips - 1)])
    below = lax.ppermute(baseline[:HALO], ("row", "claim"), [(i + 1, i) for i in range(strips - 1)])
    sent, _, _ = lax.optimization_barrier((sent, above, below))
    got = lax.all_to_all(sent, ("row", "col", "claim"), split_axis=0, concat_axis=0, tiled=True)
    pieces = (above, baseline, below)
    first = jnp.concatenate([piece[:, :HALO] for piece in pieces], axis=0)
    last = jnp.concatenate([piece[:, block_cols - HALO :] for piece in pieces], axis=0)
    if cols == 2:
        col = lax.axis_index("col")
        beside = lax.ppermute(
            jnp.concatenate([jnp.where(col == 0, last, 0.0), jnp.where(col == 1, first, 0.0)], axis=1),
            "col",
            [(0, 1), (1, 0)],
        )
    else:
        beside = jnp.concatenate(
            [
                lax.ppermute(last, "col", [(i, i + 1) for i in range(cols - 1)]),
                lax.ppermute(first, "col", [(i + 1, i) for i in range(cols - 1)]),
            ],
            axis=1,
        )
    sizes = half_widths.shape[0]
    blocks = block_cols // LANES
    places = 2 * (sides + 1)
    chunk_rows = devices * slots // LANES
    window = pltpu.VMEM((blocks + 1, 2 * block_rows, LANES), F32)
    prefix = (blocks + 1, 2 * block_rows + 8, LANES)
    depth = LANES * max(d for d in (8, 16, 24) if chunk_rows % d == 0)
    spaces = []
    for rows_of in (block_rows + HALO, HALO):
        for tall_rows in (rows_of * blocks, rows_of):
            spaces += [
                pltpu.VMEM((tall_rows, depth), BF16),
                pltpu.VMEM((2 * LANES, depth), BF16),
                pltpu.VMEM((tall_rows, 2 * LANES), F32),
            ]
    base, half_widths = pl.pallas_call(
        base_kernel,
        in_specs=[scalars] + [whole] * 4,
        out_specs=[whole, scalars],
        out_shape=[jax.ShapeDtypeStruct(prefix, F32), jax.ShapeDtypeStruct(half_widths.shape, jnp.int32)],
        scratch_shapes=[window],
        cost_estimate=pl.CostEstimate(flops=0, bytes_accessed=8 * 1024 * 1024, transcendentals=0),
        compiler_params=pltpu.CompilerParams(vmem_limit_bytes=BASE_VMEM),
    )(half_widths, baseline, above, below, beside)
    counts = pl.pallas_call(
        functools.partial(bin_kernel, sides),
        in_specs=[whole],
        out_specs=whole,
        out_shape=jax.ShapeDtypeStruct(prefix, F32),
        scratch_shapes=[
            window,
            pltpu.VMEM((places, chunk_rows, LANES), jnp.int32),
            pltpu.VMEM((places, chunk_rows, LANES), F32),
            *spaces,
        ],
        compiler_params=pltpu.CompilerParams(vmem_limit_bytes=BIN_VMEM),
    )(got)
    field = (sizes, block_rows, block_cols)
    return pl.pallas_call(
        functools.partial(scan_kernel, 3),
        in_specs=[scalars, whole, whole],
        out_specs=pl.BlockSpec(memory_space=pltpu.HBM),
        scratch_shapes=[pltpu.VMEM(field, F32), pltpu.SemaphoreType.DMA((sizes,))],
        out_shape=jax.ShapeDtypeStruct(field, F32),
        compiler_params=pltpu.CompilerParams(vmem_limit_bytes=SCAN_VMEM),
    )(half_widths, counts, base)


def solution(mesh):
    in_specs = (
        P(("groups", "row", "col", "claim"), None, None),
        P(("groups", "row", "col", "claim"), None, None),
        P(("groups", "row", "col", "claim"), None),
        P(("groups", "row", "claim"), "col"),
        P(),
    )
    out_specs = P(None, ("groups", "row", "claim"), "col")
    body = functools.partial(shards, mesh.shape["row"], mesh.shape["col"])
    return jax.shard_map(body, mesh=mesh, in_specs=in_specs, out_specs=out_specs, check_vma=False)
```

```python
import functools

import jax
import jax.numpy as jnp
from jax import lax
from jax.experimental import pallas as pl
from jax.experimental.pallas import tpu as pltpu
from jax.sharding import PartitionSpec as P

HALO = 64
LANES = 128
CODE = 4096
ROW_BIAS = 256
COL_BIAS = 1024
TINY = 1e-30
BASE_VMEM = 8 * 1024 * 1024
BIN_VMEM = 36 * 1024 * 1024
SCAN_VMEM = 24 * 1024 * 1024
F32 = jnp.float32
BF16 = jnp.bfloat16


def side_tiles(cols):
    return min(cols - 1, 2)


def pieces_of(dest, rows, cols):
    row, col, claim = dest
    other = row - 1 if claim == 0 else row + 1
    sides = [(col, 0)]
    if cols == 2:
        sides.append((1 - col, -1 if col == 1 else 1))
    elif cols > 2:
        sides += [(col - 1, -1), (col + 1, 1)]
    found = []
    for tile_row, vertical in ((row, 0), (other, 1)):
        for tile_col, side in sides:
            there = 0 <= tile_row < rows and 0 <= tile_col < cols
            found.append((tile_row * cols + tile_col if there else None, vertical, side))
    return found


def pack_kernel(rows, cols, block_rows, block_cols, cell_ref, weight_ref, count_ref, out_ref):
    cell = cell_ref[0]
    tiles, slots = cell.shape
    slot = lax.broadcasted_iota(jnp.int32, (1, slots), 1)
    weights = [jnp.where(slot < count_ref[0, tile], weight_ref[0, tile : tile + 1, :], 0.0) for tile in range(tiles)]
    tile_row = lax.div(cell, block_cols)
    tile_col = lax.rem(cell, block_cols)
    codes = {}
    for claim in (0, 1):
        for vertical in (0, 1):
            if vertical:
                first = 2 * block_rows - HALO if claim == 0 else 0
            else:
                first = 0 if claim == 0 else block_rows - HALO
            for side in (-1, 0, 1):
                shift = {-1: HALO - block_cols, 0: 0, 1: HALO}[side]
                row_code = (tile_row + (ROW_BIAS - first)) * CODE
                codes[claim, vertical, side] = (row_code + tile_col + (shift + COL_BIAS)).astype(F32)
    zero = jnp.zeros((1, slots), F32)
    index = 0
    for row in range(rows):
        for col in range(cols):
            for claim in (0, 1):
                for place, (tile, vertical, side) in enumerate(pieces_of((row, col, claim), rows, cols)):
                    there = tile is not None
                    code = codes[claim, vertical, side][tile : tile + 1] if there else zero
                    out_ref[index, 2 * place : 2 * place + 1, :] = code
                    out_ref[index, 2 * place + 1 : 2 * place + 2, :] = weights[tile] if there else zero
                index += 1


def halves(value):
    high = value.astype(BF16)
    return high, (value - high.astype(F32)).astype(BF16)


def row_prefix(window, prefix):
    side, rows, _ = window.shape
    side -= 1
    lane = lax.broadcasted_iota(jnp.int32, (rows, LANES), 1)
    sub = lax.broadcasted_iota(jnp.int32, (rows // 8, 8, LANES), 1)
    before = window[side]
    for block in range(side + 1):
        after = window[side] if block == side else pltpu.roll(window[block], HALO, axis=1)
        cells = jnp.where(lane < HALO, before, after).reshape(-1, 8, LANES)
        before = after
        for hop in (1, 2, 4):
            cells = cells + jnp.where(sub >= hop, pltpu.roll(cells, hop, axis=1), 0.0)
        carry = jnp.zeros((8, LANES), F32)
        prefix[block, 0:8, :] = carry
        for tile in range(rows // 8):
            total = cells[tile] + carry
            prefix[block, 8 * tile + 8 : 8 * tile + 16, :] = total
            carry = jnp.broadcast_to(total[7:8], (8, LANES))


def band_of(half):
    here = lax.broadcasted_iota(jnp.int32, (LANES, LANES), 0)
    there = lax.broadcasted_iota(jnp.int32, (LANES, LANES), 1)
    gap = here - there
    both = [jnp.where(jnp.abs(gap + shift) <= half, 1.0, 0.0) for shift in (-HALO, LANES - HALO)]
    band = jnp.concatenate(both, axis=1).astype(BF16)
    return jnp.concatenate([band, band], axis=0)


def lanes_of(block):
    return slice(block * LANES, (block + 1) * LANES)


def base_kernel(halves_ref, base_ref, above_ref, below_ref, upper_ref, beside_ref, lower_ref, prefix, halves_out, window):
    block_rows, block_cols = base_ref.shape
    blocks = block_cols // LANES
    for step in range(halves_ref.shape[0]):
        halves_out[step] = halves_ref[step]
    for block in range(blocks):
        window[block, 0:HALO, :] = above_ref[:, lanes_of(block)]
        window[block, HALO : HALO + block_rows, :] = base_ref[:, lanes_of(block)]
        window[block, HALO + block_rows :, :] = below_ref[:, lanes_of(block)]
    window[blocks, 0:HALO, :] = upper_ref[...]
    window[blocks, HALO : HALO + block_rows, :] = beside_ref[...]
    window[blocks, HALO + block_rows :, :] = lower_ref[...]
    row_prefix(window, prefix)


def pack16(row):
    return jnp.broadcast_to(row.astype(F32), (16, row.shape[1])).astype(BF16)


def tall(packed, size):
    return jnp.concatenate([packed] * (size // 16), axis=0)


def bin_kernel(sides, got_ref, prefix, window, code_s, weight_s, *spaces):
    blocks = window.shape[0] - 1
    block_rows = window.shape[1] // 2
    pairs = blocks // 2
    senders, _, slots = got_ref.shape
    own_rows = block_rows + HALO
    claim = lax.axis_index("claim")
    places = 2 * sides + 2
    for place in range(places):
        code = got_ref[:, 2 * place, :].astype(jnp.int32)
        weight = got_ref[:, 2 * place + 1, :]
        split = senders // 2
        for ref, value in ((code_s, code), (weight_s, weight)):
            ref[place, 0:senders, :] = value[:, :LANES]
            ref[place, senders : senders + split, 0 : slots - LANES] = value[:split, LANES:]
            ref[place, senders : senders + split, slots - LANES : LANES] = value[split:, LANES:]
    depth = spaces[0].shape[1] // LANES
    chunks = code_s.shape[1] // depth
    one, none = jnp.ones((), BF16), jnp.zeros((), BF16)

    def iota16(size):
        return lax.broadcasted_iota(jnp.int32, (size, LANES), 0).astype(F32).astype(BF16)

    def add_chunk(chunk, fresh):
        for place in range(places):
            vertical, side = divmod(place, sides + 1)
            kind = 2 * vertical + (side > 0)
            row_hot, col_hot, acc = spaces[3 * kind : 3 * kind + 3]
            rows = HALO if vertical else own_rows
            here = pl.ds(pl.multiple_of(chunk * depth, 8), depth)
            code = code_s[place, here, :]
            weight = weight_s[place, here, :]
            row = lax.shift_right_logical(code, 12) - ROW_BIAS
            col = (code & (CODE - 1)) - COL_BIAS
            high = weight.astype(BF16).astype(F32)
            parts = (high, weight - high)
            width = LANES if side else 2 * LANES
            if side:
                inside = jnp.where(lax.shift_right_arithmetic(col, 7) == 0, col, -1)
            else:
                inside = col & (2 * LANES - 1)
                pair = lax.shift_right_arithmetic(col, 8)
            row_iota, col_iota = iota16(rows), iota16(width)
            for part in range(depth):
                at, only = lanes_of(part), slice(part, part + 1)
                row_hit = tall(pack16(row[only]), rows) == row_iota
                col_hit = tall(pack16(inside[only]), width) == col_iota
                if side:
                    row_hot[:, at] = jnp.where(row_hit, one, none)
                    for index, value in enumerate(parts):
                        col_hot[lanes_of(index), at] = jnp.where(col_hit, tall(pack16(value[only]), LANES), none)
                else:
                    col_hot[:, at] = jnp.where(col_hit, one, none)
                    for group in range(pairs):
                        for index, value in enumerate(parts):
                            mine = jnp.where(pair[only] == group, value[only], 0.0)
                            start = (2 * group + index) * rows
                            row_hot[start : start + rows, at] = jnp.where(row_hit, tall(pack16(mine), rows), none)
            product = lax.dot_general(
                row_hot[...], col_hot[...], (((1,), (1,)), ((), ())), preferred_element_type=F32
            )
            acc[...] = product if fresh and side < 2 else acc[...] + product
        return 0

    add_chunk(0, True)
    if chunks > 1:
        lax.fori_loop(1, chunks, lambda chunk, _: add_chunk(chunk, False), 0)
    own_acc, side_acc, far_acc, corner_acc = spaces[2::3]
    own_at = pl.multiple_of((1 - claim) * HALO, HALO)
    far_at = pl.multiple_of(claim * own_rows, HALO)
    for block in range(blocks):
        group, here = block // 2, lanes_of(block % 2)
        for acc, rows, start in ((own_acc, own_rows, own_at), (far_acc, HALO, far_at)):
            top = 2 * group * rows
            window[block, pl.ds(start, rows), :] = acc[top : top + rows, here] + acc[top + rows : top + 2 * rows, here]
    window[blocks, pl.ds(own_at, own_rows), :] = side_acc[:, :LANES] + side_acc[:, LANES:]
    window[blocks, pl.ds(far_at, HALO), :] = corner_acc[:, :LANES] + corner_acc[:, LANES:]
    row_prefix(window, prefix)


def scan_kernel(group, halves_ref, counts_ref, prefix_ref, out_ref, buffer, sems):
    sizes, block_rows, block_cols = buffer.shape
    blocks = block_cols // LANES

    def one_size(step, _):
        half = halves_ref[step]
        inverse = 1.0 / (2 * half + 1).astype(F32)
        band = band_of(half)
        before = None
        for first in range(0, blocks + 1, group):
            some = range(first, min(first + group, blocks + 1))
            strips = []
            for block in some:
                for field in (counts_ref, prefix_ref):
                    lower = field[block, pl.ds(HALO + 8 + half, block_rows), :]
                    upper = field[block, pl.ds(HALO + 7 - half, block_rows), :]
                    strips.append(jnp.concatenate(halves(lower - upper), axis=1))
            product = jnp.dot(jnp.concatenate(strips, axis=0), band, preferred_element_type=F32)
            for index, block in enumerate(some):
                now = [product[(2 * index + f) * block_rows : (2 * index + f + 1) * block_rows] for f in (0, 1)]
                if block > 0:
                    counts, base = (old[:, :LANES] + new[:, LANES:] for old, new in zip(before, now))
                    gain = jnp.log(jnp.maximum(counts, TINY)) - jnp.log(base) - 1.0
                    buffer[step, :, lanes_of(block - 1)] = (counts * gain + base) * inverse
                before = now
        pltpu.make_async_copy(buffer.at[step], out_ref.at[step], sems.at[step]).start()
        return 0

    lax.fori_loop(0, sizes, one_size, 0, unroll=2)

    def finish(step, _):
        pltpu.make_async_copy(buffer.at[step], out_ref.at[step], sems.at[step]).wait()
        return 0

    lax.fori_loop(0, sizes, finish, 0)


def shards(rows, cols, claim_cell, claim_weight, claim_count, baseline, half_widths):
    block_rows, block_cols = baseline.shape
    slots = claim_cell.shape[2]
    sides = side_tiles(cols)
    devices = rows * cols * 2
    whole = pl.BlockSpec(memory_space=pltpu.VMEM)
    scalars = pl.BlockSpec(memory_space=pltpu.SMEM)
    sent = pl.pallas_call(
        functools.partial(pack_kernel, rows, cols, block_rows, block_cols),
        in_specs=[whole, whole, scalars],
        out_shape=jax.ShapeDtypeStruct((devices, 4 * (sides + 1), slots), F32),
    )(claim_cell, claim_weight, claim_count)

    got = lax.all_to_all(sent, ("row", "col", "claim"), split_axis=0, concat_axis=0, tiled=True)
    _, block = lax.optimization_barrier((sent, baseline))
    strips = rows * 2
    down = [(i, i + 1) for i in range(strips - 1)]
    up = [(i + 1, i) for i in range(strips - 1)]
    above = lax.ppermute(block[block_rows - HALO :], ("row", "claim"), down)
    below = lax.ppermute(block[:HALO], ("row", "claim"), up)
    first, last = block[:, :HALO], block[:, block_cols - HALO :]
    if cols == 2:
        col = lax.axis_index("col")
        edge = jnp.concatenate([jnp.where(col == 0, last, 0.0), jnp.where(col == 1, first, 0.0)], axis=1)

        def place(strip, column):
            return (strip // 2 * cols + column) * 2 + strip % 2

        def across(pairs):
            return [(place(i, c), place(j, 1 - c)) for i, j in pairs for c in (0, 1)]

        axes = ("row", "col", "claim")
        beside = (
            lax.ppermute(edge[block_rows - HALO :], axes, across(down)),
            lax.ppermute(edge, "col", [(0, 1), (1, 0)]),
            lax.ppermute(edge[:HALO], axes, across(up)),
        )
    else:
        pieces = (above, block, below)
        first = jnp.concatenate([piece[:, :HALO] for piece in pieces], axis=0)
        last = jnp.concatenate([piece[:, block_cols - HALO :] for piece in pieces], axis=0)
        sides_of = jnp.concatenate(
            [
                lax.ppermute(last, "col", [(i, i + 1) for i in range(cols - 1)]),
                lax.ppermute(first, "col", [(i + 1, i) for i in range(cols - 1)]),
            ],
            axis=1,
        )
        beside = (sides_of[:HALO], sides_of[HALO : HALO + block_rows], sides_of[HALO + block_rows :])
    sizes = half_widths.shape[0]
    blocks = block_cols // LANES
    places = 2 * (sides + 1)
    chunk_rows = devices * slots // LANES
    window = pltpu.VMEM((blocks + 1, 2 * block_rows, LANES), F32)
    prefix = (blocks + 1, 2 * block_rows + 8, LANES)
    depth = LANES * max(d for d in (8, 16, 24) if chunk_rows % d == 0)
    spaces = []
    for rows_of in (block_rows + HALO, HALO):
        for tall_rows in (rows_of * blocks, rows_of):
            spaces += [
                pltpu.VMEM((tall_rows, depth), BF16),
                pltpu.VMEM((2 * LANES, depth), BF16),
                pltpu.VMEM((tall_rows, 2 * LANES), F32),
            ]
    base, half_widths = pl.pallas_call(
        base_kernel,
        in_specs=[scalars] + [whole] * 6,
        out_specs=[whole, scalars],
        out_shape=[jax.ShapeDtypeStruct(prefix, F32), jax.ShapeDtypeStruct(half_widths.shape, jnp.int32)],
        scratch_shapes=[window],
        cost_estimate=pl.CostEstimate(flops=0, bytes_accessed=4 * 1024 * 1024, transcendentals=0),
        compiler_params=pltpu.CompilerParams(vmem_limit_bytes=BASE_VMEM),
    )(half_widths, baseline, above, below, *beside)
    counts = pl.pallas_call(
        functools.partial(bin_kernel, sides),
        in_specs=[whole],
        out_specs=whole,
        out_shape=jax.ShapeDtypeStruct(prefix, F32),
        scratch_shapes=[
            window,
            pltpu.VMEM((places, chunk_rows, LANES), jnp.int32),
            pltpu.VMEM((places, chunk_rows, LANES), F32),
            *spaces,
        ],
        cost_estimate=pl.CostEstimate(flops=0, bytes_accessed=20 * 1024 * 1024, transcendentals=0),
        compiler_params=pltpu.CompilerParams(vmem_limit_bytes=BIN_VMEM),
    )(got)
    field = (sizes, block_rows, block_cols)
    return pl.pallas_call(
        functools.partial(scan_kernel, 3),
        in_specs=[scalars, whole, whole],
        out_specs=pl.BlockSpec(memory_space=pltpu.HBM),
        scratch_shapes=[pltpu.VMEM(field, F32), pltpu.SemaphoreType.DMA((sizes,))],
        out_shape=jax.ShapeDtypeStruct(field, F32),
        compiler_params=pltpu.CompilerParams(vmem_limit_bytes=SCAN_VMEM),
    )(half_widths, counts, base)


def solution(mesh):
    in_specs = (
        P(("groups", "row", "col", "claim"), None, None),
        P(("groups", "row", "col", "claim"), None, None),
        P(("groups", "row", "col", "claim"), None),
        P(("groups", "row", "claim"), "col"),
        P(),
    )
    out_specs = P(None, ("groups", "row", "claim"), "col")
    body = functools.partial(shards, mesh.shape["row"], mesh.shape["col"])
    return jax.shard_map(body, mesh=mesh, in_specs=in_specs, out_specs=out_specs, check_vma=False)
```

```python
import functools

import jax
import jax.numpy as jnp
from jax import lax
from jax.experimental import pallas as pl
from jax.experimental.pallas import tpu as pltpu
from jax.sharding import PartitionSpec as P

HALO = 64
LANES = 128
CODE = 4096
ROW_BIAS = 256
COL_BIAS = 1024
TINY = 1e-30
BASE_VMEM = 8 * 1024 * 1024
BIN_VMEM = 36 * 1024 * 1024
SCAN_VMEM = 24 * 1024 * 1024
F32 = jnp.float32
BF16 = jnp.bfloat16


def side_tiles(cols):
    return min(cols - 1, 2)


def pieces_of(dest, rows, cols):
    row, col, claim = dest
    other = row - 1 if claim == 0 else row + 1
    sides = [(col, 0)]
    if cols == 2:
        sides.append((1 - col, -1 if col == 1 else 1))
    elif cols > 2:
        sides += [(col - 1, -1), (col + 1, 1)]
    found = []
    for tile_row, vertical in ((row, 0), (other, 1)):
        for tile_col, side in sides:
            there = 0 <= tile_row < rows and 0 <= tile_col < cols
            found.append((tile_row * cols + tile_col if there else None, vertical, side))
    return found


def pack_kernel(rows, cols, block_rows, block_cols, cell_ref, weight_ref, count_ref, out_ref):
    cell = cell_ref[0]
    tiles, slots = cell.shape
    slot = lax.broadcasted_iota(jnp.int32, (1, slots), 1)
    weights = [jnp.where(slot < count_ref[0, tile], weight_ref[0, tile : tile + 1, :], 0.0) for tile in range(tiles)]
    tile_row = lax.div(cell, block_cols)
    tile_col = lax.rem(cell, block_cols)
    codes = {}
    for claim in (0, 1):
        for vertical in (0, 1):
            if vertical:
                first = 2 * block_rows - HALO if claim == 0 else 0
            else:
                first = 0 if claim == 0 else block_rows - HALO
            for side in (-1, 0, 1):
                shift = {-1: HALO - block_cols, 0: 0, 1: HALO}[side]
                row_code = (tile_row + (ROW_BIAS - first)) * CODE
                codes[claim, vertical, side] = (row_code + tile_col + (shift + COL_BIAS)).astype(F32)
    zero = jnp.zeros((1, slots), F32)
    index = 0
    for row in range(rows):
        for col in range(cols):
            for claim in (0, 1):
                for place, (tile, vertical, side) in enumerate(pieces_of((row, col, claim), rows, cols)):
                    there = tile is not None
                    code = codes[claim, vertical, side][tile : tile + 1] if there else zero
                    out_ref[index, 2 * place : 2 * place + 1, :] = code
                    out_ref[index, 2 * place + 1 : 2 * place + 2, :] = weights[tile] if there else zero
                index += 1


def halves(value):
    high = value.astype(BF16)
    return high, (value - high.astype(F32)).astype(BF16)


def row_prefix(window, prefix):
    side, rows, _ = window.shape
    side -= 1
    lane = lax.broadcasted_iota(jnp.int32, (rows, LANES), 1)
    sub = lax.broadcasted_iota(jnp.int32, (rows // 8, 8, LANES), 1)
    before = window[side]
    for block in range(side + 1):
        after = window[side] if block == side else pltpu.roll(window[block], HALO, axis=1)
        cells = jnp.where(lane < HALO, before, after).reshape(-1, 8, LANES)
        before = after
        for hop in (1, 2, 4):
            cells = cells + jnp.where(sub >= hop, pltpu.roll(cells, hop, axis=1), 0.0)
        carry = jnp.zeros((8, LANES), F32)
        prefix[block, 0:8, :] = carry
        for tile in range(rows // 8):
            total = cells[tile] + carry
            prefix[block, 8 * tile + 8 : 8 * tile + 16, :] = total
            carry = jnp.broadcast_to(total[7:8], (8, LANES))


def band_of(half):
    here = lax.broadcasted_iota(jnp.int32, (LANES, LANES), 0)
    there = lax.broadcasted_iota(jnp.int32, (LANES, LANES), 1)
    gap = here - there
    both = [jnp.where(jnp.abs(gap + shift) <= half, 1.0, 0.0) for shift in (-HALO, LANES - HALO)]
    band = jnp.concatenate(both, axis=1).astype(BF16)
    return jnp.concatenate([band, band], axis=0)


def lanes_of(block):
    return slice(block * LANES, (block + 1) * LANES)


def base_kernel(
    halves_ref, base_ref, inner_ref, outer_ref, beside_ref, inner_side_ref, outer_side_ref, prefix, halves_out, window
):
    block_rows, block_cols = base_ref.shape
    blocks = block_cols // LANES
    for step in range(halves_ref.shape[0]):
        halves_out[step] = halves_ref[step]
    claim = lax.axis_index("claim")
    far_side = HALO + block_rows
    inner_at = pl.multiple_of((1 - claim) * far_side, HALO)
    outer_at = pl.multiple_of(claim * far_side, HALO)
    for block in range(blocks):
        here = lanes_of(block)
        window[block, HALO:far_side, :] = base_ref[:, here]
        window[block, pl.ds(inner_at, HALO), :] = inner_ref[:, here]
        window[block, pl.ds(outer_at, HALO), :] = outer_ref[:, here]
    window[blocks, HALO:far_side, :] = beside_ref[...]
    window[blocks, pl.ds(inner_at, HALO), :] = inner_side_ref[...]
    window[blocks, pl.ds(outer_at, HALO), :] = outer_side_ref[...]
    row_prefix(window, prefix)


def pack16(row):
    return jnp.broadcast_to(row.astype(F32), (16, row.shape[1])).astype(BF16)


def tall(packed, size):
    return jnp.concatenate([packed] * (size // 16), axis=0)


def bin_kernel(sides, got_ref, prefix, window, code_s, weight_s, *spaces):
    blocks = window.shape[0] - 1
    block_rows = window.shape[1] // 2
    pairs = blocks // 2
    senders, _, slots = got_ref.shape
    own_rows = block_rows + HALO
    claim = lax.axis_index("claim")
    places = 2 * sides + 2
    for place in range(places):
        code = got_ref[:, 2 * place, :].astype(jnp.int32)
        weight = got_ref[:, 2 * place + 1, :]
        split = senders // 2
        for ref, value in ((code_s, code), (weight_s, weight)):
            ref[place, 0:senders, :] = value[:, :LANES]
            ref[place, senders : senders + split, 0 : slots - LANES] = value[:split, LANES:]
            ref[place, senders : senders + split, slots - LANES : LANES] = value[split:, LANES:]
    depth = spaces[0].shape[1] // LANES
    chunks = code_s.shape[1] // depth
    one, none = jnp.ones((), BF16), jnp.zeros((), BF16)

    def iota16(size):
        return lax.broadcasted_iota(jnp.int32, (size, LANES), 0).astype(F32).astype(BF16)

    def add_chunk(chunk, fresh):
        for place in range(places):
            vertical, side = divmod(place, sides + 1)
            kind = 2 * vertical + (side > 0)
            row_hot, col_hot, acc = spaces[3 * kind : 3 * kind + 3]
            rows = HALO if vertical else own_rows
            here = pl.ds(pl.multiple_of(chunk * depth, 8), depth)
            code = code_s[place, here, :]
            weight = weight_s[place, here, :]
            row = lax.shift_right_logical(code, 12) - ROW_BIAS
            col = (code & (CODE - 1)) - COL_BIAS
            high = weight.astype(BF16).astype(F32)
            parts = (high, weight - high)
            width = LANES if side else 2 * LANES
            if side:
                inside = jnp.where(lax.shift_right_arithmetic(col, 7) == 0, col, -1)
            else:
                inside = col & (2 * LANES - 1)
                pair = lax.shift_right_arithmetic(col, 8)
            row_iota, col_iota = iota16(rows), iota16(width)
            for part in range(depth):
                at, only = lanes_of(part), slice(part, part + 1)
                row_hit = tall(pack16(row[only]), rows) == row_iota
                col_hit = tall(pack16(inside[only]), width) == col_iota
                if side:
                    row_hot[:, at] = jnp.where(row_hit, one, none)
                    for index, value in enumerate(parts):
                        col_hot[lanes_of(index), at] = jnp.where(col_hit, tall(pack16(value[only]), LANES), none)
                else:
                    col_hot[:, at] = jnp.where(col_hit, one, none)
                    for group in range(pairs):
                        for index, value in enumerate(parts):
                            mine = jnp.where(pair[only] == group, value[only], 0.0)
                            start = (2 * group + index) * rows
                            row_hot[start : start + rows, at] = jnp.where(row_hit, tall(pack16(mine), rows), none)
            product = lax.dot_general(
                row_hot[...], col_hot[...], (((1,), (1,)), ((), ())), preferred_element_type=F32
            )
            acc[...] = product if fresh and side < 2 else acc[...] + product
        return 0

    add_chunk(0, True)
    if chunks > 1:
        lax.fori_loop(1, chunks, lambda chunk, _: add_chunk(chunk, False), 0)
    own_acc, side_acc, far_acc, corner_acc = spaces[2::3]
    own_at = pl.multiple_of((1 - claim) * HALO, HALO)
    far_at = pl.multiple_of(claim * own_rows, HALO)
    for block in range(blocks):
        group, here = block // 2, lanes_of(block % 2)
        for acc, rows, start in ((own_acc, own_rows, own_at), (far_acc, HALO, far_at)):
            top = 2 * group * rows
            window[block, pl.ds(start, rows), :] = acc[top : top + rows, here] + acc[top + rows : top + 2 * rows, here]
    window[blocks, pl.ds(own_at, own_rows), :] = side_acc[:, :LANES] + side_acc[:, LANES:]
    window[blocks, pl.ds(far_at, HALO), :] = corner_acc[:, :LANES] + corner_acc[:, LANES:]
    row_prefix(window, prefix)


def scan_kernel(group, halves_ref, counts_ref, prefix_ref, out_ref, buffer, sems):
    sizes, block_rows, block_cols = buffer.shape
    blocks = block_cols // LANES

    def one_size(step, _):
        half = halves_ref[step]
        inverse = 1.0 / (2 * half + 1).astype(F32)
        band = band_of(half)
        before = None
        for first in range(0, blocks + 1, group):
            some = range(first, min(first + group, blocks + 1))
            strips = []
            for block in some:
                for field in (counts_ref, prefix_ref):
                    lower = field[block, pl.ds(HALO + 8 + half, block_rows), :]
                    upper = field[block, pl.ds(HALO + 7 - half, block_rows), :]
                    strips.append(jnp.concatenate(halves(lower - upper), axis=1))
            product = jnp.dot(jnp.concatenate(strips, axis=0), band, preferred_element_type=F32)
            for index, block in enumerate(some):
                now = [product[(2 * index + f) * block_rows : (2 * index + f + 1) * block_rows] for f in (0, 1)]
                if block > 0:
                    counts, base = (old[:, :LANES] + new[:, LANES:] for old, new in zip(before, now))
                    gain = jnp.log(jnp.maximum(counts, TINY)) - jnp.log(base) - 1.0
                    buffer[step, :, lanes_of(block - 1)] = (counts * gain + base) * inverse
                before = now
        pltpu.make_async_copy(buffer.at[step], out_ref.at[step], sems.at[step]).start()
        return 0

    lax.fori_loop(0, sizes, one_size, 0, unroll=2)

    def finish(step, _):
        pltpu.make_async_copy(buffer.at[step], out_ref.at[step], sems.at[step]).wait()
        return 0

    lax.fori_loop(0, sizes, finish, 0)


def shards(rows, cols, claim_cell, claim_weight, claim_count, baseline, half_widths):
    block_rows, block_cols = baseline.shape
    slots = claim_cell.shape[2]
    sides = side_tiles(cols)
    devices = rows * cols * 2
    whole = pl.BlockSpec(memory_space=pltpu.VMEM)
    scalars = pl.BlockSpec(memory_space=pltpu.SMEM)
    sent = pl.pallas_call(
        functools.partial(pack_kernel, rows, cols, block_rows, block_cols),
        in_specs=[whole, whole, scalars],
        out_shape=jax.ShapeDtypeStruct((devices, 4 * (sides + 1), slots), F32),
    )(claim_cell, claim_weight, claim_count)

    got = lax.all_to_all(sent, ("row", "col", "claim"), split_axis=0, concat_axis=0, tiled=True)
    _, block = lax.optimization_barrier((sent, baseline))
    claim = lax.axis_index("claim")
    seams = [(2 * i + 1, 2 * i + 2) for i in range(rows - 1)]
    seams += [(j, i) for i, j in seams]

    def swapped(cells, within, across, axes):
        top, bottom = cells[:HALO], cells[block_rows - HALO :]
        return (
            lax.ppermute(jnp.where(claim == 0, bottom, top), axes[0], within),
            lax.ppermute(jnp.where(claim == 0, top, bottom), axes[1], across),
        )

    inner, outer = swapped(block, [(0, 1), (1, 0)], seams, ("claim", ("row", "claim")))
    first, last = block[:, :HALO], block[:, block_cols - HALO :]
    if cols == 2:
        col = lax.axis_index("col")
        edge = jnp.concatenate([jnp.where(col == 0, last, 0.0), jnp.where(col == 1, first, 0.0)], axis=1)
        beside = lax.ppermute(edge, "col", [(0, 1), (1, 0)])

        def place(strip, column):
            return (strip // 2 * cols + column) * 2 + strip % 2

        inner_side, outer_side = swapped(
            edge,
            [(2 * c + k, 2 * (1 - c) + 1 - k) for c in (0, 1) for k in (0, 1)],
            [(place(i, c), place(j, 1 - c)) for i, j in seams for c in (0, 1)],
            (("col", "claim"), ("row", "col", "claim")),
        )
    else:

        def sides_of(cells):
            return jnp.concatenate(
                [
                    lax.ppermute(cells[:, block_cols - HALO :], "col", [(i, i + 1) for i in range(cols - 1)]),
                    lax.ppermute(cells[:, :HALO], "col", [(i + 1, i) for i in range(cols - 1)]),
                ],
                axis=1,
            )

        beside, inner_side, outer_side = sides_of(block), sides_of(inner), sides_of(outer)
    sizes = half_widths.shape[0]
    blocks = block_cols // LANES
    places = 2 * (sides + 1)
    chunk_rows = devices * slots // LANES
    window = pltpu.VMEM((blocks + 1, 2 * block_rows, LANES), F32)
    prefix = (blocks + 1, 2 * block_rows + 8, LANES)
    depth = LANES * max(d for d in (8, 16, 24) if chunk_rows % d == 0)
    spaces = []
    for rows_of in (block_rows + HALO, HALO):
        for tall_rows in (rows_of * blocks, rows_of):
            spaces += [
                pltpu.VMEM((tall_rows, depth), BF16),
                pltpu.VMEM((2 * LANES, depth), BF16),
                pltpu.VMEM((tall_rows, 2 * LANES), F32),
            ]
    base, half_widths = pl.pallas_call(
        base_kernel,
        in_specs=[scalars] + [whole] * 6,
        out_specs=[whole, scalars],
        out_shape=[jax.ShapeDtypeStruct(prefix, F32), jax.ShapeDtypeStruct(half_widths.shape, jnp.int32)],
        scratch_shapes=[window],
        cost_estimate=pl.CostEstimate(flops=0, bytes_accessed=4 * 1024 * 1024, transcendentals=0),
        compiler_params=pltpu.CompilerParams(vmem_limit_bytes=BASE_VMEM),
    )(half_widths, baseline, inner, outer, beside, inner_side, outer_side)
    counts = pl.pallas_call(
        functools.partial(bin_kernel, sides),
        in_specs=[whole],
        out_specs=whole,
        out_shape=jax.ShapeDtypeStruct(prefix, F32),
        scratch_shapes=[
            window,
            pltpu.VMEM((places, chunk_rows, LANES), jnp.int32),
            pltpu.VMEM((places, chunk_rows, LANES), F32),
            *spaces,
        ],
        cost_estimate=pl.CostEstimate(flops=0, bytes_accessed=20 * 1024 * 1024, transcendentals=0),
        compiler_params=pltpu.CompilerParams(vmem_limit_bytes=BIN_VMEM),
    )(got)
    field = (sizes, block_rows, block_cols)
    return pl.pallas_call(
        functools.partial(scan_kernel, 3),
        in_specs=[scalars, whole, whole],
        out_specs=pl.BlockSpec(memory_space=pltpu.HBM),
        scratch_shapes=[pltpu.VMEM(field, F32), pltpu.SemaphoreType.DMA((sizes,))],
        out_shape=jax.ShapeDtypeStruct(field, F32),
        compiler_params=pltpu.CompilerParams(vmem_limit_bytes=SCAN_VMEM),
    )(half_widths, counts, base)


def solution(mesh):
    in_specs = (
        P(("groups", "row", "col", "claim"), None, None),
        P(("groups", "row", "col", "claim"), None, None),
        P(("groups", "row", "col", "claim"), None),
        P(("groups", "row", "claim"), "col"),
        P(),
    )
    out_specs = P(None, ("groups", "row", "claim"), "col")
    body = functools.partial(shards, mesh.shape["row"], mesh.shape["col"])
    return jax.shard_map(body, mesh=mesh, in_specs=in_specs, out_specs=out_specs, check_vma=False)
```

```python
import functools

import jax
import jax.numpy as jnp
from jax import lax
from jax.experimental import pallas as pl
from jax.experimental.pallas import tpu as pltpu
from jax.sharding import PartitionSpec as P

HALO = 64
LANES = 128
CODE = 4096
ROW_BIAS = 256
COL_BIAS = 1024
TINY = 1e-30
BASE_VMEM = 8 * 1024 * 1024
BIN_VMEM = 36 * 1024 * 1024
SCAN_VMEM = 24 * 1024 * 1024
F32 = jnp.float32
BF16 = jnp.bfloat16


def side_tiles(cols):
    return min(cols - 1, 2)


def pieces_of(dest, rows, cols):
    row, col, claim = dest
    other = row - 1 if claim == 0 else row + 1
    sides = [(col, 0)]
    if cols == 2:
        sides.append((1 - col, -1 if col == 1 else 1))
    elif cols > 2:
        sides += [(col - 1, -1), (col + 1, 1)]
    found = []
    for tile_row, vertical in ((row, 0), (other, 1)):
        for tile_col, side in sides:
            there = 0 <= tile_row < rows and 0 <= tile_col < cols
            found.append((tile_row * cols + tile_col if there else None, vertical, side))
    return found


def pack_kernel(rows, cols, block_rows, block_cols, cell_ref, weight_ref, count_ref, out_ref):
    cell = cell_ref[0]
    tiles, slots = cell.shape
    slot = lax.broadcasted_iota(jnp.int32, (1, slots), 1)
    weights = [jnp.where(slot < count_ref[0, tile], weight_ref[0, tile : tile + 1, :], 0.0) for tile in range(tiles)]
    tile_row = lax.div(cell, block_cols)
    tile_col = lax.rem(cell, block_cols)
    codes = {}
    for claim in (0, 1):
        for vertical in (0, 1):
            if vertical:
                first = 2 * block_rows - HALO if claim == 0 else 0
            else:
                first = 0 if claim == 0 else block_rows - HALO
            for side in (-1, 0, 1):
                shift = {-1: HALO - block_cols, 0: 0, 1: HALO}[side]
                row_code = (tile_row + (ROW_BIAS - first)) * CODE
                codes[claim, vertical, side] = (row_code + tile_col + (shift + COL_BIAS)).astype(F32)
    zero = jnp.zeros((1, slots), F32)
    index = 0
    for row in range(rows):
        for col in range(cols):
            for claim in (0, 1):
                for place, (tile, vertical, side) in enumerate(pieces_of((row, col, claim), rows, cols)):
                    there = tile is not None
                    code = codes[claim, vertical, side][tile : tile + 1] if there else zero
                    out_ref[index, 2 * place : 2 * place + 1, :] = code
                    out_ref[index, 2 * place + 1 : 2 * place + 2, :] = weights[tile] if there else zero
                index += 1


def halves(value):
    high = value.astype(BF16)
    return high, (value - high.astype(F32)).astype(BF16)


def row_prefix(window, prefix):
    side, rows, _ = window.shape
    side -= 1
    lane = lax.broadcasted_iota(jnp.int32, (rows, LANES), 1)
    sub = lax.broadcasted_iota(jnp.int32, (rows // 8, 8, LANES), 1)
    before = window[side]
    for block in range(side + 1):
        after = window[side] if block == side else pltpu.roll(window[block], HALO, axis=1)
        cells = jnp.where(lane < HALO, before, after).reshape(-1, 8, LANES)
        before = after
        for hop in (1, 2, 4):
            cells = cells + jnp.where(sub >= hop, pltpu.roll(cells, hop, axis=1), 0.0)
        carry = jnp.zeros((8, LANES), F32)
        prefix[block, 0:8, :] = carry
        for tile in range(rows // 8):
            total = cells[tile] + carry
            prefix[block, 8 * tile + 8 : 8 * tile + 16, :] = total
            carry = jnp.broadcast_to(total[7:8], (8, LANES))


def band_of(half):
    here = lax.broadcasted_iota(jnp.int32, (LANES, LANES), 0)
    there = lax.broadcasted_iota(jnp.int32, (LANES, LANES), 1)
    gap = here - there
    both = [jnp.where(jnp.abs(gap + shift) <= half, 1.0, 0.0) for shift in (-HALO, LANES - HALO)]
    band = jnp.concatenate(both, axis=1).astype(BF16)
    return jnp.concatenate([band, band], axis=0)


def lanes_of(block):
    return slice(block * LANES, (block + 1) * LANES)


def base_kernel(halves_ref, base_ref, inner_ref, outer_ref, beside_ref, prefix, halves_out, window):
    block_rows, block_cols = base_ref.shape
    blocks = block_cols // LANES
    for step in range(halves_ref.shape[0]):
        halves_out[step] = halves_ref[step]
    claim = lax.axis_index("claim")
    far_side = HALO + block_rows
    inner_at = pl.multiple_of((1 - claim) * far_side, HALO)
    outer_at = pl.multiple_of(claim * far_side, HALO)
    for block in range(blocks):
        here = lanes_of(block)
        window[block, HALO:far_side, :] = base_ref[:, here]
        window[block, pl.ds(inner_at, HALO), :] = inner_ref[:, here]
        window[block, pl.ds(outer_at, HALO), :] = outer_ref[:, here]
    window[blocks, HALO:far_side, :] = beside_ref[:block_rows]
    window[blocks, pl.ds(inner_at, HALO), :] = beside_ref[block_rows : block_rows + HALO]
    window[blocks, pl.ds(outer_at, HALO), :] = beside_ref[block_rows + HALO :]
    row_prefix(window, prefix)


def pack16(row):
    return jnp.broadcast_to(row.astype(F32), (16, row.shape[1])).astype(BF16)


def tall(packed, size):
    return jnp.concatenate([packed] * (size // 16), axis=0)


def bin_kernel(sides, got_ref, prefix, window, code_s, weight_s, *spaces):
    blocks = window.shape[0] - 1
    block_rows = window.shape[1] // 2
    pairs = blocks // 2
    senders, _, slots = got_ref.shape
    own_rows = block_rows + HALO
    claim = lax.axis_index("claim")
    places = 2 * sides + 2
    for place in range(places):
        code = got_ref[:, 2 * place, :].astype(jnp.int32)
        weight = got_ref[:, 2 * place + 1, :]
        split = senders // 2
        for ref, value in ((code_s, code), (weight_s, weight)):
            ref[place, 0:senders, :] = value[:, :LANES]
            ref[place, senders : senders + split, 0 : slots - LANES] = value[:split, LANES:]
            ref[place, senders : senders + split, slots - LANES : LANES] = value[split:, LANES:]
    depth = spaces[0].shape[1] // LANES
    chunks = code_s.shape[1] // depth
    one, none = jnp.ones((), BF16), jnp.zeros((), BF16)

    def iota16(size):
        return lax.broadcasted_iota(jnp.int32, (size, LANES), 0).astype(F32).astype(BF16)

    def add_chunk(chunk, fresh):
        for place in range(places):
            vertical, side = divmod(place, sides + 1)
            kind = 2 * vertical + (side > 0)
            row_hot, col_hot, acc = spaces[3 * kind : 3 * kind + 3]
            rows = HALO if vertical else own_rows
            here = pl.ds(pl.multiple_of(chunk * depth, 8), depth)
            code = code_s[place, here, :]
            weight = weight_s[place, here, :]
            row = lax.shift_right_logical(code, 12) - ROW_BIAS
            col = (code & (CODE - 1)) - COL_BIAS
            high = weight.astype(BF16).astype(F32)
            parts = (high, weight - high)
            width = LANES if side else 2 * LANES
            if side:
                inside = jnp.where(lax.shift_right_arithmetic(col, 7) == 0, col, -1)
            else:
                inside = col & (2 * LANES - 1)
                pair = lax.shift_right_arithmetic(col, 8)
            row_iota, col_iota = iota16(rows), iota16(width)
            for part in range(depth):
                at, only = lanes_of(part), slice(part, part + 1)
                row_hit = tall(pack16(row[only]), rows) == row_iota
                col_hit = tall(pack16(inside[only]), width) == col_iota
                if side:
                    row_hot[:, at] = jnp.where(row_hit, one, none)
                    for index, value in enumerate(parts):
                        col_hot[lanes_of(index), at] = jnp.where(col_hit, tall(pack16(value[only]), LANES), none)
                else:
                    col_hot[:, at] = jnp.where(col_hit, one, none)
                    for group in range(pairs):
                        for index, value in enumerate(parts):
                            mine = jnp.where(pair[only] == group, value[only], 0.0)
                            start = (2 * group + index) * rows
                            row_hot[start : start + rows, at] = jnp.where(row_hit, tall(pack16(mine), rows), none)
            product = lax.dot_general(
                row_hot[...], col_hot[...], (((1,), (1,)), ((), ())), preferred_element_type=F32
            )
            acc[...] = product if fresh and side < 2 else acc[...] + product
        return 0

    add_chunk(0, True)
    if chunks > 1:
        lax.fori_loop(1, chunks, lambda chunk, _: add_chunk(chunk, False), 0)
    own_acc, side_acc, far_acc, corner_acc = spaces[2::3]
    own_at = pl.multiple_of((1 - claim) * HALO, HALO)
    far_at = pl.multiple_of(claim * own_rows, HALO)
    for block in range(blocks):
        group, here = block // 2, lanes_of(block % 2)
        for acc, rows, start in ((own_acc, own_rows, own_at), (far_acc, HALO, far_at)):
            top = 2 * group * rows
            window[block, pl.ds(start, rows), :] = acc[top : top + rows, here] + acc[top + rows : top + 2 * rows, here]
    window[blocks, pl.ds(own_at, own_rows), :] = side_acc[:, :LANES] + side_acc[:, LANES:]
    window[blocks, pl.ds(far_at, HALO), :] = corner_acc[:, :LANES] + corner_acc[:, LANES:]
    row_prefix(window, prefix)


def scan_kernel(group, halves_ref, counts_ref, prefix_ref, out_ref, buffer, sems):
    sizes, block_rows, block_cols = buffer.shape
    blocks = block_cols // LANES

    def one_size(step, _):
        half = halves_ref[step]
        inverse = 1.0 / (2 * half + 1).astype(F32)
        band = band_of(half)
        before = None
        for first in range(0, blocks + 1, group):
            some = range(first, min(first + group, blocks + 1))
            strips = []
            for block in some:
                for field in (counts_ref, prefix_ref):
                    lower = field[block, pl.ds(HALO + 8 + half, block_rows), :]
                    upper = field[block, pl.ds(HALO + 7 - half, block_rows), :]
                    strips.append(jnp.concatenate(halves(lower - upper), axis=1))
            product = jnp.dot(jnp.concatenate(strips, axis=0), band, preferred_element_type=F32)
            for index, block in enumerate(some):
                now = [product[(2 * index + f) * block_rows : (2 * index + f + 1) * block_rows] for f in (0, 1)]
                if block > 0:
                    counts, base = (old[:, :LANES] + new[:, LANES:] for old, new in zip(before, now))
                    gain = jnp.log(jnp.maximum(counts, TINY)) - jnp.log(base) - 1.0
                    buffer[step, :, lanes_of(block - 1)] = (counts * gain + base) * inverse
                before = now
        pltpu.make_async_copy(buffer.at[step], out_ref.at[step], sems.at[step]).start()
        return 0

    lax.fori_loop(0, sizes, one_size, 0, unroll=2)

    def finish(step, _):
        pltpu.make_async_copy(buffer.at[step], out_ref.at[step], sems.at[step]).wait()
        return 0

    lax.fori_loop(0, sizes, finish, 0)


def shards(rows, cols, claim_cell, claim_weight, claim_count, baseline, half_widths):
    block_rows, block_cols = baseline.shape
    slots = claim_cell.shape[2]
    sides = side_tiles(cols)
    devices = rows * cols * 2
    whole = pl.BlockSpec(memory_space=pltpu.VMEM)
    scalars = pl.BlockSpec(memory_space=pltpu.SMEM)
    sent = pl.pallas_call(
        functools.partial(pack_kernel, rows, cols, block_rows, block_cols),
        in_specs=[whole, whole, scalars],
        out_shape=jax.ShapeDtypeStruct((devices, 4 * (sides + 1), slots), F32),
    )(claim_cell, claim_weight, claim_count)

    got = lax.all_to_all(sent, ("row", "col", "claim"), split_axis=0, concat_axis=0, tiled=True)
    _, block = lax.optimization_barrier((sent, baseline))
    claim = lax.axis_index("claim")
    seams = [(2 * i + 1, 2 * i + 2) for i in range(rows - 1)]
    seams += [(j, i) for i, j in seams]

    top, bottom = block[:HALO], block[block_rows - HALO :]
    inner = lax.ppermute(jnp.where(claim == 0, bottom, top), "claim", [(0, 1), (1, 0)])
    outer = lax.ppermute(jnp.where(claim == 0, top, bottom), ("row", "claim"), seams)
    pieces = (block, inner, outer)
    first = jnp.concatenate([piece[:, :HALO] for piece in pieces], axis=0)
    last = jnp.concatenate([piece[:, block_cols - HALO :] for piece in pieces], axis=0)
    if cols == 2:
        col = lax.axis_index("col")
        edge = jnp.concatenate([jnp.where(col == 0, last, 0.0), jnp.where(col == 1, first, 0.0)], axis=1)
        beside = lax.ppermute(edge, "col", [(0, 1), (1, 0)])
    else:
        beside = jnp.concatenate(
            [
                lax.ppermute(last, "col", [(i, i + 1) for i in range(cols - 1)]),
                lax.ppermute(first, "col", [(i + 1, i) for i in range(cols - 1)]),
            ],
            axis=1,
        )
    sizes = half_widths.shape[0]
    blocks = block_cols // LANES
    places = 2 * (sides + 1)
    chunk_rows = devices * slots // LANES
    window = pltpu.VMEM((blocks + 1, 2 * block_rows, LANES), F32)
    prefix = (blocks + 1, 2 * block_rows + 8, LANES)
    depth = LANES * max(d for d in (8, 16, 24) if chunk_rows % d == 0)
    spaces = []
    for rows_of in (block_rows + HALO, HALO):
        for tall_rows in (rows_of * blocks, rows_of):
            spaces += [
                pltpu.VMEM((tall_rows, depth), BF16),
                pltpu.VMEM((2 * LANES, depth), BF16),
                pltpu.VMEM((tall_rows, 2 * LANES), F32),
            ]
    base, half_widths = pl.pallas_call(
        base_kernel,
        in_specs=[scalars] + [whole] * 4,
        out_specs=[whole, scalars],
        out_shape=[jax.ShapeDtypeStruct(prefix, F32), jax.ShapeDtypeStruct(half_widths.shape, jnp.int32)],
        scratch_shapes=[window],
        cost_estimate=pl.CostEstimate(flops=0, bytes_accessed=4 * 1024 * 1024, transcendentals=0),
        compiler_params=pltpu.CompilerParams(vmem_limit_bytes=BASE_VMEM),
    )(half_widths, baseline, inner, outer, beside)
    counts = pl.pallas_call(
        functools.partial(bin_kernel, sides),
        in_specs=[whole],
        out_specs=whole,
        out_shape=jax.ShapeDtypeStruct(prefix, F32),
        scratch_shapes=[
            window,
            pltpu.VMEM((places, chunk_rows, LANES), jnp.int32),
            pltpu.VMEM((places, chunk_rows, LANES), F32),
            *spaces,
        ],
        cost_estimate=pl.CostEstimate(flops=0, bytes_accessed=20 * 1024 * 1024, transcendentals=0),
        compiler_params=pltpu.CompilerParams(vmem_limit_bytes=BIN_VMEM),
    )(got)
    field = (sizes, block_rows, block_cols)
    return pl.pallas_call(
        functools.partial(scan_kernel, 3),
        in_specs=[scalars, whole, whole],
        out_specs=pl.BlockSpec(memory_space=pltpu.HBM),
        scratch_shapes=[pltpu.VMEM(field, F32), pltpu.SemaphoreType.DMA((sizes,))],
        out_shape=jax.ShapeDtypeStruct(field, F32),
        compiler_params=pltpu.CompilerParams(vmem_limit_bytes=SCAN_VMEM),
    )(half_widths, counts, base)


def solution(mesh):
    in_specs = (
        P(("groups", "row", "col", "claim"), None, None),
        P(("groups", "row", "col", "claim"), None, None),
        P(("groups", "row", "col", "claim"), None),
        P(("groups", "row", "claim"), "col"),
        P(),
    )
    out_specs = P(None, ("groups", "row", "claim"), "col")
    body = functools.partial(shards, mesh.shape["row"], mesh.shape["col"])
    return jax.shard_map(body, mesh=mesh, in_specs=in_specs, out_specs=out_specs, check_vma=False)
```

```python
import functools

import jax
import jax.numpy as jnp
from jax import lax
from jax.experimental import pallas as pl
from jax.experimental.pallas import tpu as pltpu
from jax.sharding import PartitionSpec as P

HALO = 64
LANES = 128
CODE = 4096
ROW_BIAS = 256
COL_BIAS = 1024
TINY = 1e-30
BASE_VMEM = 8 * 1024 * 1024
BIN_VMEM = 36 * 1024 * 1024
SCAN_VMEM = 24 * 1024 * 1024
F32 = jnp.float32
BF16 = jnp.bfloat16


def side_tiles(cols):
    return min(cols - 1, 2)


def pieces_of(dest, rows, cols):
    row, col, claim = dest
    other = row - 1 if claim == 0 else row + 1
    sides = [(col, 0)]
    if cols == 2:
        sides.append((1 - col, -1 if col == 1 else 1))
    elif cols > 2:
        sides += [(col - 1, -1), (col + 1, 1)]
    found = []
    for tile_row, vertical in ((row, 0), (other, 1)):
        for tile_col, side in sides:
            there = 0 <= tile_row < rows and 0 <= tile_col < cols
            found.append((tile_row * cols + tile_col if there else None, vertical, side))
    return found


def pack_kernel(rows, cols, block_rows, block_cols, cell_ref, weight_ref, count_ref, out_ref):
    cell = cell_ref[0]
    tiles, slots = cell.shape
    slot = lax.broadcasted_iota(jnp.int32, (1, slots), 1)
    weights = [jnp.where(slot < count_ref[0, tile], weight_ref[0, tile : tile + 1, :], 0.0) for tile in range(tiles)]
    tile_row = lax.div(cell, block_cols)
    tile_col = lax.rem(cell, block_cols)
    codes = {}
    for claim in (0, 1):
        for vertical in (0, 1):
            if vertical:
                first = 2 * block_rows - HALO if claim == 0 else 0
            else:
                first = 0 if claim == 0 else block_rows - HALO
            for side in (-1, 0, 1):
                shift = {-1: HALO - block_cols, 0: 0, 1: HALO}[side]
                row_code = (tile_row + (ROW_BIAS - first)) * CODE
                codes[claim, vertical, side] = (row_code + tile_col + (shift + COL_BIAS)).astype(F32)
    zero = jnp.zeros((1, slots), F32)
    index = 0
    for row in range(rows):
        for col in range(cols):
            for claim in (0, 1):
                for place, (tile, vertical, side) in enumerate(pieces_of((row, col, claim), rows, cols)):
                    there = tile is not None
                    code = codes[claim, vertical, side][tile : tile + 1] if there else zero
                    out_ref[index, 2 * place : 2 * place + 1, :] = code
                    out_ref[index, 2 * place + 1 : 2 * place + 2, :] = weights[tile] if there else zero
                index += 1


def halves(value):
    high = value.astype(BF16)
    return high, (value - high.astype(F32)).astype(BF16)


def prefix_of(cells, prefix, block):
    sub = lax.broadcasted_iota(jnp.int32, (cells.shape[0] // 8, 8, LANES), 1)
    cells = cells.reshape(-1, 8, LANES)
    for hop in (1, 2, 4):
        cells = cells + jnp.where(sub >= hop, pltpu.roll(cells, hop, axis=1), 0.0)
    carry = jnp.zeros((8, LANES), F32)
    prefix[block, 0:8, :] = carry
    for tile in range(cells.shape[0]):
        total = cells[tile] + carry
        prefix[block, 8 * tile + 8 : 8 * tile + 16, :] = total
        carry = jnp.broadcast_to(total[7:8], (8, LANES))


def row_prefix(window, prefix, ends):
    blocks, rows, _ = prefix.shape[0] - 1, window.shape[1], LANES
    lane = lax.broadcasted_iota(jnp.int32, (rows, LANES), 1)
    before = ends
    for block in range(blocks + 1):
        after = ends if block == blocks else pltpu.roll(window[block], HALO, axis=1)
        prefix_of(jnp.where(lane < HALO, before, after), prefix, block)
        before = after


def band_of(half):
    here = lax.broadcasted_iota(jnp.int32, (LANES, LANES), 0)
    there = lax.broadcasted_iota(jnp.int32, (LANES, LANES), 1)
    gap = here - there
    both = [jnp.where(jnp.abs(gap + shift) <= half, 1.0, 0.0) for shift in (-HALO, LANES - HALO)]
    band = jnp.concatenate(both, axis=1).astype(BF16)
    return jnp.concatenate([band, band], axis=0)


def lanes_of(block):
    return slice(block * LANES, (block + 1) * LANES)


def halo_rows(claim, block_rows):
    far_side = HALO + block_rows
    return pl.multiple_of((1 - claim) * far_side, HALO), pl.multiple_of(claim * far_side, HALO)


def base_kernel(halves_ref, base_ref, inner_ref, outer_ref, prefix, halves_out, window):
    block_rows, block_cols = base_ref.shape
    for step in range(halves_ref.shape[0]):
        halves_out[step] = halves_ref[step]
    inner_at, outer_at = halo_rows(lax.axis_index("claim"), block_rows)
    for block in range(block_cols // LANES):
        here = lanes_of(block)
        window[block, HALO : HALO + block_rows, :] = base_ref[:, here]
        window[block, pl.ds(inner_at, HALO), :] = inner_ref[:, here]
        window[block, pl.ds(outer_at, HALO), :] = outer_ref[:, here]
    row_prefix(window, prefix, jnp.zeros((window.shape[1], LANES), F32))


def pack16(row):
    return jnp.broadcast_to(row.astype(F32), (16, row.shape[1])).astype(BF16)


def tall(packed, size):
    return jnp.concatenate([packed] * (size // 16), axis=0)


def bin_kernel(sides, got_ref, prefix, window, code_s, weight_s, *spaces):
    blocks = window.shape[0] - 1
    block_rows = window.shape[1] // 2
    pairs = blocks // 2
    senders, _, slots = got_ref.shape
    own_rows = block_rows + HALO
    claim = lax.axis_index("claim")
    places = 2 * sides + 2
    for place in range(places):
        code = got_ref[:, 2 * place, :].astype(jnp.int32)
        weight = got_ref[:, 2 * place + 1, :]
        split = senders // 2
        for ref, value in ((code_s, code), (weight_s, weight)):
            ref[place, 0:senders, :] = value[:, :LANES]
            ref[place, senders : senders + split, 0 : slots - LANES] = value[:split, LANES:]
            ref[place, senders : senders + split, slots - LANES : LANES] = value[split:, LANES:]
    depth = spaces[0].shape[1] // LANES
    chunks = code_s.shape[1] // depth
    one, none = jnp.ones((), BF16), jnp.zeros((), BF16)

    def iota16(size):
        return lax.broadcasted_iota(jnp.int32, (size, LANES), 0).astype(F32).astype(BF16)

    def add_chunk(chunk, fresh):
        for place in range(places):
            vertical, side = divmod(place, sides + 1)
            kind = 2 * vertical + (side > 0)
            row_hot, col_hot, acc = spaces[3 * kind : 3 * kind + 3]
            rows = HALO if vertical else own_rows
            here = pl.ds(pl.multiple_of(chunk * depth, 8), depth)
            code = code_s[place, here, :]
            weight = weight_s[place, here, :]
            row = lax.shift_right_logical(code, 12) - ROW_BIAS
            col = (code & (CODE - 1)) - COL_BIAS
            high = weight.astype(BF16).astype(F32)
            parts = (high, weight - high)
            width = LANES if side else 2 * LANES
            if side:
                inside = jnp.where(lax.shift_right_arithmetic(col, 7) == 0, col, -1)
            else:
                inside = col & (2 * LANES - 1)
                pair = lax.shift_right_arithmetic(col, 8)
            row_iota, col_iota = iota16(rows), iota16(width)
            for part in range(depth):
                at, only = lanes_of(part), slice(part, part + 1)
                row_hit = tall(pack16(row[only]), rows) == row_iota
                col_hit = tall(pack16(inside[only]), width) == col_iota
                if side:
                    row_hot[:, at] = jnp.where(row_hit, one, none)
                    for index, value in enumerate(parts):
                        col_hot[lanes_of(index), at] = jnp.where(col_hit, tall(pack16(value[only]), LANES), none)
                else:
                    col_hot[:, at] = jnp.where(col_hit, one, none)
                    for group in range(pairs):
                        for index, value in enumerate(parts):
                            mine = jnp.where(pair[only] == group, value[only], 0.0)
                            start = (2 * group + index) * rows
                            row_hot[start : start + rows, at] = jnp.where(row_hit, tall(pack16(mine), rows), none)
            product = lax.dot_general(
                row_hot[...], col_hot[...], (((1,), (1,)), ((), ())), preferred_element_type=F32
            )
            acc[...] = product if fresh and side < 2 else acc[...] + product
        return 0

    add_chunk(0, True)
    if chunks > 1:
        lax.fori_loop(1, chunks, lambda chunk, _: add_chunk(chunk, False), 0)
    own_acc, side_acc, far_acc, corner_acc = spaces[2::3]
    own_at = pl.multiple_of((1 - claim) * HALO, HALO)
    far_at = pl.multiple_of(claim * own_rows, HALO)
    for block in range(blocks):
        group, here = block // 2, lanes_of(block % 2)
        for acc, rows, start in ((own_acc, own_rows, own_at), (far_acc, HALO, far_at)):
            top = 2 * group * rows
            window[block, pl.ds(start, rows), :] = acc[top : top + rows, here] + acc[top + rows : top + 2 * rows, here]
    window[blocks, pl.ds(own_at, own_rows), :] = side_acc[:, :LANES] + side_acc[:, LANES:]
    window[blocks, pl.ds(far_at, HALO), :] = corner_acc[:, :LANES] + corner_acc[:, LANES:]
    row_prefix(window, prefix, window[blocks])


def scan_kernel(group, halves_ref, counts_ref, prefix_ref, beside_ref, out_ref, buffer, sems, rows_s, ends):
    sizes, block_rows, block_cols = buffer.shape
    blocks = block_cols // LANES
    inner_at, outer_at = halo_rows(lax.axis_index("claim"), block_rows)
    rows_s[HALO : HALO + block_rows, :] = beside_ref[:block_rows]
    rows_s[pl.ds(inner_at, HALO), :] = beside_ref[block_rows : block_rows + HALO]
    rows_s[pl.ds(outer_at, HALO), :] = beside_ref[block_rows + HALO :]
    prefix_of(rows_s[...], ends, 0)
    lane = lax.broadcasted_iota(jnp.int32, ends.shape[1:], 1)
    ends[1] = jnp.where(lane < HALO, prefix_ref[blocks], ends[0])
    ends[0] = jnp.where(lane < HALO, ends[0], prefix_ref[0])

    def one_size(step, _):
        half = halves_ref[step]
        inverse = 1.0 / (2 * half + 1).astype(F32)
        band = band_of(half)
        before = None
        for first in range(0, blocks + 1, group):
            some = range(first, min(first + group, blocks + 1))
            strips = []
            for block in some:
                at_end = block in (0, blocks)
                base_at = (ends, block // blocks) if at_end else (prefix_ref, block)
                for field, index in ((counts_ref, block), base_at):
                    lower = field[index, pl.ds(HALO + 8 + half, block_rows), :]
                    upper = field[index, pl.ds(HALO + 7 - half, block_rows), :]
                    strips.append(jnp.concatenate(halves(lower - upper), axis=1))
            product = jnp.dot(jnp.concatenate(strips, axis=0), band, preferred_element_type=F32)
            for index, block in enumerate(some):
                now = [product[(2 * index + f) * block_rows : (2 * index + f + 1) * block_rows] for f in (0, 1)]
                if block > 0:
                    counts, base = (old[:, :LANES] + new[:, LANES:] for old, new in zip(before, now))
                    gain = jnp.log(jnp.maximum(counts, TINY)) - jnp.log(base) - 1.0
                    buffer[step, :, lanes_of(block - 1)] = (counts * gain + base) * inverse
                before = now
        pltpu.make_async_copy(buffer.at[step], out_ref.at[step], sems.at[step]).start()
        return 0

    lax.fori_loop(0, sizes, one_size, 0, unroll=2)

    def finish(step, _):
        pltpu.make_async_copy(buffer.at[step], out_ref.at[step], sems.at[step]).wait()
        return 0

    lax.fori_loop(0, sizes, finish, 0)


def shards(rows, cols, claim_cell, claim_weight, claim_count, baseline, half_widths):
    block_rows, block_cols = baseline.shape
    slots = claim_cell.shape[2]
    sides = side_tiles(cols)
    devices = rows * cols * 2
    whole = pl.BlockSpec(memory_space=pltpu.VMEM)
    scalars = pl.BlockSpec(memory_space=pltpu.SMEM)
    sent = pl.pallas_call(
        functools.partial(pack_kernel, rows, cols, block_rows, block_cols),
        in_specs=[whole, whole, scalars],
        out_shape=jax.ShapeDtypeStruct((devices, 4 * (sides + 1), slots), F32),
    )(claim_cell, claim_weight, claim_count)

    got = lax.all_to_all(sent, ("row", "col", "claim"), split_axis=0, concat_axis=0, tiled=True)
    _, block = lax.optimization_barrier((sent, baseline))
    claim = lax.axis_index("claim")
    seams = [(2 * i + 1, 2 * i + 2) for i in range(rows - 1)]
    seams += [(j, i) for i, j in seams]

    top, bottom = block[:HALO], block[block_rows - HALO :]
    inner = lax.ppermute(jnp.where(claim == 0, bottom, top), "claim", [(0, 1), (1, 0)])
    outer = lax.ppermute(jnp.where(claim == 0, top, bottom), ("row", "claim"), seams)
    pieces = (block, inner, outer)
    first = jnp.concatenate([piece[:, :HALO] for piece in pieces], axis=0)
    last = jnp.concatenate([piece[:, block_cols - HALO :] for piece in pieces], axis=0)
    if cols == 2:
        col = lax.axis_index("col")
        edge = jnp.concatenate([jnp.where(col == 0, last, 0.0), jnp.where(col == 1, first, 0.0)], axis=1)
        beside = lax.ppermute(edge, "col", [(0, 1), (1, 0)])
    else:
        beside = jnp.concatenate(
            [
                lax.ppermute(last, "col", [(i, i + 1) for i in range(cols - 1)]),
                lax.ppermute(first, "col", [(i + 1, i) for i in range(cols - 1)]),
            ],
            axis=1,
        )
    sizes = half_widths.shape[0]
    blocks = block_cols // LANES
    places = 2 * (sides + 1)
    chunk_rows = devices * slots // LANES
    window = pltpu.VMEM((blocks + 1, 2 * block_rows, LANES), F32)
    prefix = (blocks + 1, 2 * block_rows + 8, LANES)
    depth = LANES * max(d for d in (8, 16, 24) if chunk_rows % d == 0)
    spaces = []
    for rows_of in (block_rows + HALO, HALO):
        for tall_rows in (rows_of * blocks, rows_of):
            spaces += [
                pltpu.VMEM((tall_rows, depth), BF16),
                pltpu.VMEM((2 * LANES, depth), BF16),
                pltpu.VMEM((tall_rows, 2 * LANES), F32),
            ]
    base, half_widths = pl.pallas_call(
        base_kernel,
        in_specs=[scalars] + [whole] * 3,
        out_specs=[whole, scalars],
        out_shape=[jax.ShapeDtypeStruct(prefix, F32), jax.ShapeDtypeStruct(half_widths.shape, jnp.int32)],
        scratch_shapes=[window],
        cost_estimate=pl.CostEstimate(flops=0, bytes_accessed=4 * 1024 * 1024, transcendentals=0),
        compiler_params=pltpu.CompilerParams(vmem_limit_bytes=BASE_VMEM),
    )(half_widths, baseline, inner, outer)
    got, base, half_widths = lax.optimization_barrier((got, base, half_widths))
    counts = pl.pallas_call(
        functools.partial(bin_kernel, sides),
        in_specs=[whole],
        out_specs=whole,
        out_shape=jax.ShapeDtypeStruct(prefix, F32),
        scratch_shapes=[
            window,
            pltpu.VMEM((places, chunk_rows, LANES), jnp.int32),
            pltpu.VMEM((places, chunk_rows, LANES), F32),
            *spaces,
        ],
        cost_estimate=pl.CostEstimate(flops=0, bytes_accessed=20 * 1024 * 1024, transcendentals=0),
        compiler_params=pltpu.CompilerParams(vmem_limit_bytes=BIN_VMEM),
    )(got)
    field = (sizes, block_rows, block_cols)
    return pl.pallas_call(
        functools.partial(scan_kernel, 3),
        in_specs=[scalars, whole, whole, whole],
        out_specs=pl.BlockSpec(memory_space=pltpu.HBM),
        scratch_shapes=[
            pltpu.VMEM(field, F32),
            pltpu.SemaphoreType.DMA((sizes,)),
            pltpu.VMEM((2 * block_rows, LANES), F32),
            pltpu.VMEM((2, 2 * block_rows + 8, LANES), F32),
        ],
        out_shape=jax.ShapeDtypeStruct(field, F32),
        compiler_params=pltpu.CompilerParams(vmem_limit_bytes=SCAN_VMEM),
    )(half_widths, counts, base, beside)


def solution(mesh):
    in_specs = (
        P(("groups", "row", "col", "claim"), None, None),
        P(("groups", "row", "col", "claim"), None, None),
        P(("groups", "row", "col", "claim"), None),
        P(("groups", "row", "claim"), "col"),
        P(),
    )
    out_specs = P(None, ("groups", "row", "claim"), "col")
    body = functools.partial(shards, mesh.shape["row"], mesh.shape["col"])
    return jax.shard_map(body, mesh=mesh, in_specs=in_specs, out_specs=out_specs, check_vma=False)
```

```python
import functools

import jax
import jax.numpy as jnp
from jax import lax
from jax.experimental import pallas as pl
from jax.experimental.pallas import tpu as pltpu
from jax.sharding import PartitionSpec as P

HALO = 64
LANES = 128
CODE = 4096
ROW_BIAS = 256
COL_BIAS = 1024
TINY = 1e-30
BASE_VMEM = 8 * 1024 * 1024
BIN_VMEM = 36 * 1024 * 1024
SCAN_VMEM = 24 * 1024 * 1024
F32 = jnp.float32
BF16 = jnp.bfloat16


def side_tiles(cols):
    return min(cols - 1, 2)


def pieces_of(dest, rows, cols):
    row, col, claim = dest
    other = row - 1 if claim == 0 else row + 1
    sides = [(col, 0)]
    if cols == 2:
        sides.append((1 - col, -1 if col == 1 else 1))
    elif cols > 2:
        sides += [(col - 1, -1), (col + 1, 1)]
    found = []
    for tile_row, vertical in ((row, 0), (other, 1)):
        for tile_col, side in sides:
            there = 0 <= tile_row < rows and 0 <= tile_col < cols
            found.append((tile_row * cols + tile_col if there else None, vertical, side))
    return found


def pack_kernel(rows, cols, block_rows, block_cols, cell_ref, weight_ref, count_ref, base_ref, out_ref, outer_ref, inner_ref, sems):
    claim_here = lax.axis_index("claim")
    last_rows = block_rows - HALO
    starts = ((1 - claim_here) * last_rows, claim_here * last_rows)
    copies = [
        pltpu.make_async_copy(base_ref.at[pl.ds(pl.multiple_of(start, 8), HALO)], ref, sems.at[index])
        for index, (start, ref) in enumerate(zip(starts, (inner_ref, outer_ref)))
    ]
    for copy in copies:
        copy.start()
    cell = cell_ref[0]
    tiles, slots = cell.shape
    slot = lax.broadcasted_iota(jnp.int32, (1, slots), 1)
    weights = [jnp.where(slot < count_ref[0, tile], weight_ref[0, tile : tile + 1, :], 0.0) for tile in range(tiles)]
    tile_row = lax.div(cell, block_cols)
    tile_col = lax.rem(cell, block_cols)
    codes = {}
    for claim in (0, 1):
        for vertical in (0, 1):
            if vertical:
                first = 2 * block_rows - HALO if claim == 0 else 0
            else:
                first = 0 if claim == 0 else block_rows - HALO
            for side in (-1, 0, 1):
                shift = {-1: HALO - block_cols, 0: 0, 1: HALO}[side]
                row_code = (tile_row + (ROW_BIAS - first)) * CODE
                codes[claim, vertical, side] = (row_code + tile_col + (shift + COL_BIAS)).astype(F32)
    zero = jnp.zeros((1, slots), F32)
    index = 0
    for row in range(rows):
        for col in range(cols):
            for claim in (0, 1):
                for place, (tile, vertical, side) in enumerate(pieces_of((row, col, claim), rows, cols)):
                    there = tile is not None
                    code = codes[claim, vertical, side][tile : tile + 1] if there else zero
                    out_ref[index, 2 * place : 2 * place + 1, :] = code
                    out_ref[index, 2 * place + 1 : 2 * place + 2, :] = weights[tile] if there else zero
                index += 1
    for copy in copies:
        copy.wait()


def halves(value):
    high = value.astype(BF16)
    return high, (value - high.astype(F32)).astype(BF16)


def prefix_of(cells, prefix, block):
    sub = lax.broadcasted_iota(jnp.int32, (cells.shape[0] // 8, 8, LANES), 1)
    cells = cells.reshape(-1, 8, LANES)
    for hop in (1, 2, 4):
        cells = cells + jnp.where(sub >= hop, pltpu.roll(cells, hop, axis=1), 0.0)
    carry = jnp.zeros((8, LANES), F32)
    prefix[block, 0:8, :] = carry
    for tile in range(cells.shape[0]):
        total = cells[tile] + carry
        prefix[block, 8 * tile + 8 : 8 * tile + 16, :] = total
        carry = jnp.broadcast_to(total[7:8], (8, LANES))


def row_prefix(window, prefix, ends):
    blocks, rows, _ = prefix.shape[0] - 1, window.shape[1], LANES
    lane = lax.broadcasted_iota(jnp.int32, (rows, LANES), 1)
    before = ends
    for block in range(blocks + 1):
        after = ends if block == blocks else pltpu.roll(window[block], HALO, axis=1)
        prefix_of(jnp.where(lane < HALO, before, after), prefix, block)
        before = after


def band_of(half):
    here = lax.broadcasted_iota(jnp.int32, (LANES, LANES), 0)
    there = lax.broadcasted_iota(jnp.int32, (LANES, LANES), 1)
    gap = here - there
    both = [jnp.where(jnp.abs(gap + shift) <= half, 1.0, 0.0) for shift in (-HALO, LANES - HALO)]
    band = jnp.concatenate(both, axis=1).astype(BF16)
    return jnp.concatenate([band, band], axis=0)


def lanes_of(block):
    return slice(block * LANES, (block + 1) * LANES)


def halo_rows(claim, block_rows):
    far_side = HALO + block_rows
    return pl.multiple_of((1 - claim) * far_side, HALO), pl.multiple_of(claim * far_side, HALO)


def base_kernel(halves_ref, base_ref, inner_ref, outer_ref, prefix, halves_out, window):
    block_rows, block_cols = base_ref.shape
    for step in range(halves_ref.shape[0]):
        halves_out[step] = halves_ref[step]
    inner_at, outer_at = halo_rows(lax.axis_index("claim"), block_rows)
    for block in range(block_cols // LANES):
        here = lanes_of(block)
        window[block, HALO : HALO + block_rows, :] = base_ref[:, here]
        window[block, pl.ds(inner_at, HALO), :] = inner_ref[:, here]
        window[block, pl.ds(outer_at, HALO), :] = outer_ref[:, here]
    row_prefix(window, prefix, jnp.zeros((window.shape[1], LANES), F32))


def pack16(row):
    return jnp.broadcast_to(row.astype(F32), (16, row.shape[1])).astype(BF16)


def tall(packed, size):
    return jnp.concatenate([packed] * (size // 16), axis=0)


def bin_kernel(sides, got_ref, prefix, window, code_s, weight_s, *spaces):
    blocks = window.shape[0] - 1
    block_rows = window.shape[1] // 2
    pairs = blocks // 2
    senders, _, slots = got_ref.shape
    own_rows = block_rows + HALO
    claim = lax.axis_index("claim")
    places = 2 * sides + 2
    for place in range(places):
        code = got_ref[:, 2 * place, :].astype(jnp.int32)
        weight = got_ref[:, 2 * place + 1, :]
        split = senders // 2
        for ref, value in ((code_s, code), (weight_s, weight)):
            ref[place, 0:senders, :] = value[:, :LANES]
            ref[place, senders : senders + split, 0 : slots - LANES] = value[:split, LANES:]
            ref[place, senders : senders + split, slots - LANES : LANES] = value[split:, LANES:]
    depth = spaces[0].shape[1] // LANES
    chunks = code_s.shape[1] // depth
    one, none = jnp.ones((), BF16), jnp.zeros((), BF16)

    def iota16(size):
        return lax.broadcasted_iota(jnp.int32, (size, LANES), 0).astype(F32).astype(BF16)

    def add_chunk(chunk, fresh):
        for place in range(places):
            vertical, side = divmod(place, sides + 1)
            kind = 2 * vertical + (side > 0)
            row_hot, col_hot, acc = spaces[3 * kind : 3 * kind + 3]
            rows = HALO if vertical else own_rows
            here = pl.ds(pl.multiple_of(chunk * depth, 8), depth)
            code = code_s[place, here, :]
            weight = weight_s[place, here, :]
            row = lax.shift_right_logical(code, 12) - ROW_BIAS
            col = (code & (CODE - 1)) - COL_BIAS
            high = weight.astype(BF16).astype(F32)
            parts = (high, weight - high)
            width = LANES if side else 2 * LANES
            if side:
                inside = jnp.where(lax.shift_right_arithmetic(col, 7) == 0, col, -1)
            else:
                inside = col & (2 * LANES - 1)
                pair = lax.shift_right_arithmetic(col, 8)
            row_iota, col_iota = iota16(rows), iota16(width)
            for part in range(depth):
                at, only = lanes_of(part), slice(part, part + 1)
                row_hit = tall(pack16(row[only]), rows) == row_iota
                col_hit = tall(pack16(inside[only]), width) == col_iota
                if side:
                    row_hot[:, at] = jnp.where(row_hit, one, none)
                    for index, value in enumerate(parts):
                        col_hot[lanes_of(index), at] = jnp.where(col_hit, tall(pack16(value[only]), LANES), none)
                else:
                    col_hot[:, at] = jnp.where(col_hit, one, none)
                    for group in range(pairs):
                        for index, value in enumerate(parts):
                            mine = jnp.where(pair[only] == group, value[only], 0.0)
                            start = (2 * group + index) * rows
                            row_hot[start : start + rows, at] = jnp.where(row_hit, tall(pack16(mine), rows), none)
            product = lax.dot_general(
                row_hot[...], col_hot[...], (((1,), (1,)), ((), ())), preferred_element_type=F32
            )
            acc[...] = product if fresh and side < 2 else acc[...] + product
        return 0

    add_chunk(0, True)
    if chunks > 1:
        lax.fori_loop(1, chunks, lambda chunk, _: add_chunk(chunk, False), 0)
    own_acc, side_acc, far_acc, corner_acc = spaces[2::3]
    own_at = pl.multiple_of((1 - claim) * HALO, HALO)
    far_at = pl.multiple_of(claim * own_rows, HALO)
    for block in range(blocks):
        group, here = block // 2, lanes_of(block % 2)
        for acc, rows, start in ((own_acc, own_rows, own_at), (far_acc, HALO, far_at)):
            top = 2 * group * rows
            window[block, pl.ds(start, rows), :] = acc[top : top + rows, here] + acc[top + rows : top + 2 * rows, here]
    window[blocks, pl.ds(own_at, own_rows), :] = side_acc[:, :LANES] + side_acc[:, LANES:]
    window[blocks, pl.ds(far_at, HALO), :] = corner_acc[:, :LANES] + corner_acc[:, LANES:]
    row_prefix(window, prefix, window[blocks])


def scan_kernel(group, halves_ref, counts_ref, prefix_ref, beside_ref, out_ref, buffer, sems, rows_s, ends):
    sizes, block_rows, block_cols = buffer.shape
    blocks = block_cols // LANES
    inner_at, outer_at = halo_rows(lax.axis_index("claim"), block_rows)
    rows_s[HALO : HALO + block_rows, :] = beside_ref[:block_rows]
    rows_s[pl.ds(inner_at, HALO), :] = beside_ref[block_rows : block_rows + HALO]
    rows_s[pl.ds(outer_at, HALO), :] = beside_ref[block_rows + HALO :]
    prefix_of(rows_s[...], ends, 0)
    lane = lax.broadcasted_iota(jnp.int32, ends.shape[1:], 1)
    ends[1] = jnp.where(lane < HALO, prefix_ref[blocks], ends[0])
    ends[0] = jnp.where(lane < HALO, ends[0], prefix_ref[0])

    def one_size(step, _):
        half = halves_ref[step]
        inverse = 1.0 / (2 * half + 1).astype(F32)
        band = band_of(half)
        before = None
        for first in range(0, blocks + 1, group):
            some = range(first, min(first + group, blocks + 1))
            strips = []
            for block in some:
                at_end = block in (0, blocks)
                base_at = (ends, block // blocks) if at_end else (prefix_ref, block)
                for field, index in ((counts_ref, block), base_at):
                    lower = field[index, pl.ds(HALO + 8 + half, block_rows), :]
                    upper = field[index, pl.ds(HALO + 7 - half, block_rows), :]
                    strips.append(jnp.concatenate(halves(lower - upper), axis=1))
            product = jnp.dot(jnp.concatenate(strips, axis=0), band, preferred_element_type=F32)
            for index, block in enumerate(some):
                now = [product[(2 * index + f) * block_rows : (2 * index + f + 1) * block_rows] for f in (0, 1)]
                if block > 0:
                    counts, base = (old[:, :LANES] + new[:, LANES:] for old, new in zip(before, now))
                    gain = jnp.log(jnp.maximum(counts, TINY)) - jnp.log(base) - 1.0
                    buffer[step, :, lanes_of(block - 1)] = (counts * gain + base) * inverse
                before = now
        pltpu.make_async_copy(buffer.at[step], out_ref.at[step], sems.at[step]).start()
        return 0

    lax.fori_loop(0, sizes, one_size, 0, unroll=2)

    def finish(step, _):
        pltpu.make_async_copy(buffer.at[step], out_ref.at[step], sems.at[step]).wait()
        return 0

    lax.fori_loop(0, sizes, finish, 0)


def shards(rows, cols, claim_cell, claim_weight, claim_count, baseline, half_widths):
    block_rows, block_cols = baseline.shape
    slots = claim_cell.shape[2]
    sides = side_tiles(cols)
    devices = rows * cols * 2
    whole = pl.BlockSpec(memory_space=pltpu.VMEM)
    scalars = pl.BlockSpec(memory_space=pltpu.SMEM)
    remote = pl.BlockSpec(memory_space=pltpu.HBM)
    strip = jax.ShapeDtypeStruct((HALO, block_cols), F32)
    sent, outer, inner = pl.pallas_call(
        functools.partial(pack_kernel, rows, cols, block_rows, block_cols),
        in_specs=[whole, whole, scalars, remote],
        out_specs=[whole, remote, remote],
        out_shape=[jax.ShapeDtypeStruct((devices, 4 * (sides + 1), slots), F32), strip, strip],
        scratch_shapes=[pltpu.SemaphoreType.DMA((2,))],
    )(claim_cell, claim_weight, claim_count, baseline)
    got = lax.all_to_all(sent, ("row", "col", "claim"), split_axis=0, concat_axis=0, tiled=True)
    _, block = lax.optimization_barrier((sent, baseline))
    seams = [(2 * i + 1, 2 * i + 2) for i in range(rows - 1)]
    seams += [(j, i) for i, j in seams]

    outer = lax.ppermute(outer, ("row", "claim"), seams)
    inner = lax.ppermute(inner, "claim", [(0, 1), (1, 0)])
    pieces = (block, inner, outer)
    first = jnp.concatenate([piece[:, :HALO] for piece in pieces], axis=0)
    last = jnp.concatenate([piece[:, block_cols - HALO :] for piece in pieces], axis=0)
    if cols == 2:
        col = lax.axis_index("col")
        edge = jnp.concatenate([jnp.where(col == 0, last, 0.0), jnp.where(col == 1, first, 0.0)], axis=1)
        beside = lax.ppermute(edge, "col", [(0, 1), (1, 0)])
    else:
        beside = jnp.concatenate(
            [
                lax.ppermute(last, "col", [(i, i + 1) for i in range(cols - 1)]),
                lax.ppermute(first, "col", [(i + 1, i) for i in range(cols - 1)]),
            ],
            axis=1,
        )
    sizes = half_widths.shape[0]
    blocks = block_cols // LANES
    places = 2 * (sides + 1)
    chunk_rows = devices * slots // LANES
    window = pltpu.VMEM((blocks + 1, 2 * block_rows, LANES), F32)
    prefix = (blocks + 1, 2 * block_rows + 8, LANES)
    depth = LANES * max(d for d in (8, 16, 24) if chunk_rows % d == 0)
    spaces = []
    for rows_of in (block_rows + HALO, HALO):
        for tall_rows in (rows_of * blocks, rows_of):
            spaces += [
                pltpu.VMEM((tall_rows, depth), BF16),
                pltpu.VMEM((2 * LANES, depth), BF16),
                pltpu.VMEM((tall_rows, 2 * LANES), F32),
            ]
    base, half_widths = pl.pallas_call(
        base_kernel,
        in_specs=[scalars] + [whole] * 3,
        out_specs=[whole, scalars],
        out_shape=[jax.ShapeDtypeStruct(prefix, F32), jax.ShapeDtypeStruct(half_widths.shape, jnp.int32)],
        scratch_shapes=[window],
        cost_estimate=pl.CostEstimate(flops=0, bytes_accessed=4 * 1024 * 1024, transcendentals=0),
        compiler_params=pltpu.CompilerParams(vmem_limit_bytes=BASE_VMEM),
    )(half_widths, baseline, inner, outer)
    got, base, half_widths = lax.optimization_barrier((got, base, half_widths))
    counts = pl.pallas_call(
        functools.partial(bin_kernel, sides),
        in_specs=[whole],
        out_specs=whole,
        out_shape=jax.ShapeDtypeStruct(prefix, F32),
        scratch_shapes=[
            window,
            pltpu.VMEM((places, chunk_rows, LANES), jnp.int32),
            pltpu.VMEM((places, chunk_rows, LANES), F32),
            *spaces,
        ],
        cost_estimate=pl.CostEstimate(flops=0, bytes_accessed=20 * 1024 * 1024, transcendentals=0),
        compiler_params=pltpu.CompilerParams(vmem_limit_bytes=BIN_VMEM),
    )(got)
    field = (sizes, block_rows, block_cols)
    return pl.pallas_call(
        functools.partial(scan_kernel, 3),
        in_specs=[scalars, whole, whole, whole],
        out_specs=pl.BlockSpec(memory_space=pltpu.HBM),
        scratch_shapes=[
            pltpu.VMEM(field, F32),
            pltpu.SemaphoreType.DMA((sizes,)),
            pltpu.VMEM((2 * block_rows, LANES), F32),
            pltpu.VMEM((2, 2 * block_rows + 8, LANES), F32),
        ],
        out_shape=jax.ShapeDtypeStruct(field, F32),
        compiler_params=pltpu.CompilerParams(vmem_limit_bytes=SCAN_VMEM),
    )(half_widths, counts, base, beside)


def solution(mesh):
    in_specs = (
        P(("groups", "row", "col", "claim"), None, None),
        P(("groups", "row", "col", "claim"), None, None),
        P(("groups", "row", "col", "claim"), None),
        P(("groups", "row", "claim"), "col"),
        P(),
    )
    out_specs = P(None, ("groups", "row", "claim"), "col")
    body = functools.partial(shards, mesh.shape["row"], mesh.shape["col"])
    return jax.shard_map(body, mesh=mesh, in_specs=in_specs, out_specs=out_specs, check_vma=False)
```

```python
import functools

import jax
import jax.numpy as jnp
from jax import lax
from jax.experimental import pallas as pl
from jax.experimental.pallas import tpu as pltpu
from jax.sharding import PartitionSpec as P

HALO = 64
LANES = 128
CODE = 4096
ROW_BIAS = 256
COL_BIAS = 1024
TINY = 1e-30
BASE_VMEM = 8 * 1024 * 1024
BIN_VMEM = 36 * 1024 * 1024
SCAN_VMEM = 24 * 1024 * 1024
F32 = jnp.float32
BF16 = jnp.bfloat16


def side_tiles(cols):
    return min(cols - 1, 2)


def pieces_of(dest, rows, cols):
    row, col, claim = dest
    other = row - 1 if claim == 0 else row + 1
    sides = [(col, 0)]
    if cols == 2:
        sides.append((1 - col, -1 if col == 1 else 1))
    elif cols > 2:
        sides += [(col - 1, -1), (col + 1, 1)]
    found = []
    for tile_row, vertical in ((row, 0), (other, 1)):
        for tile_col, side in sides:
            there = 0 <= tile_row < rows and 0 <= tile_col < cols
            found.append((tile_row * cols + tile_col if there else None, vertical, side))
    return found


def pack_kernel(rows, cols, block_rows, block_cols, cell_ref, weight_ref, count_ref, out_ref):
    cell = cell_ref[0]
    tiles, slots = cell.shape
    slot = lax.broadcasted_iota(jnp.int32, (1, slots), 1)
    weights = [jnp.where(slot < count_ref[0, tile], weight_ref[0, tile : tile + 1, :], 0.0) for tile in range(tiles)]
    tile_row = lax.div(cell, block_cols)
    tile_col = lax.rem(cell, block_cols)
    codes = {}
    for claim in (0, 1):
        for vertical in (0, 1):
            if vertical:
                first = 2 * block_rows - HALO if claim == 0 else 0
            else:
                first = 0 if claim == 0 else block_rows - HALO
            for side in (-1, 0, 1):
                shift = {-1: HALO - block_cols, 0: 0, 1: HALO}[side]
                row_code = (tile_row + (ROW_BIAS - first)) * CODE
                codes[claim, vertical, side] = (row_code + tile_col + (shift + COL_BIAS)).astype(F32)
    zero = jnp.zeros((1, slots), F32)
    index = 0
    for row in range(rows):
        for col in range(cols):
            for claim in (0, 1):
                for place, (tile, vertical, side) in enumerate(pieces_of((row, col, claim), rows, cols)):
                    there = tile is not None
                    code = codes[claim, vertical, side][tile : tile + 1] if there else zero
                    out_ref[index, 2 * place : 2 * place + 1, :] = code
                    out_ref[index, 2 * place + 1 : 2 * place + 2, :] = weights[tile] if there else zero
                index += 1


def halves(value):
    high = value.astype(BF16)
    return high, (value - high.astype(F32)).astype(BF16)


def prefix_of(cells, prefix, block):
    sub = lax.broadcasted_iota(jnp.int32, (cells.shape[0] // 8, 8, LANES), 1)
    cells = cells.reshape(-1, 8, LANES)
    for hop in (1, 2, 4):
        cells = cells + jnp.where(sub >= hop, pltpu.roll(cells, hop, axis=1), 0.0)
    carry = jnp.zeros((8, LANES), F32)
    prefix[block, 0:8, :] = carry
    for tile in range(cells.shape[0]):
        total = cells[tile] + carry
        prefix[block, 8 * tile + 8 : 8 * tile + 16, :] = total
        carry = jnp.broadcast_to(total[7:8], (8, LANES))


def row_prefix(window, prefix, ends):
    blocks, rows, _ = prefix.shape[0] - 1, window.shape[1], LANES
    lane = lax.broadcasted_iota(jnp.int32, (rows, LANES), 1)
    before = ends
    for block in range(blocks + 1):
        after = ends if block == blocks else pltpu.roll(window[block], HALO, axis=1)
        prefix_of(jnp.where(lane < HALO, before, after), prefix, block)
        before = after


def band_of(half):
    here = lax.broadcasted_iota(jnp.int32, (LANES, LANES), 0)
    there = lax.broadcasted_iota(jnp.int32, (LANES, LANES), 1)
    gap = here - there
    both = [jnp.where(jnp.abs(gap + shift) <= half, 1.0, 0.0) for shift in (-HALO, LANES - HALO)]
    band = jnp.concatenate(both, axis=1).astype(BF16)
    return jnp.concatenate([band, band], axis=0)


def lanes_of(block):
    return slice(block * LANES, (block + 1) * LANES)


def halo_rows(claim, block_rows):
    far_side = HALO + block_rows
    return pl.multiple_of((1 - claim) * far_side, HALO), pl.multiple_of(claim * far_side, HALO)


def base_kernel(halves_ref, base_ref, inner_ref, outer_ref, prefix, halves_out, window):
    block_rows, block_cols = base_ref.shape
    for step in range(halves_ref.shape[0]):
        halves_out[step] = halves_ref[step]
    inner_at, outer_at = halo_rows(lax.axis_index("claim"), block_rows)
    for block in range(block_cols // LANES):
        here = lanes_of(block)
        window[block, HALO : HALO + block_rows, :] = base_ref[:, here]
        window[block, pl.ds(inner_at, HALO), :] = inner_ref[:, here]
        window[block, pl.ds(outer_at, HALO), :] = outer_ref[:, here]
    row_prefix(window, prefix, jnp.zeros((window.shape[1], LANES), F32))


def pack16(row):
    return jnp.broadcast_to(row.astype(F32), (16, row.shape[1])).astype(BF16)


def tall(packed, size):
    return jnp.concatenate([packed] * (size // 16), axis=0)


def bin_kernel(sides, got_ref, prefix, window, code_s, weight_s, *spaces):
    blocks = window.shape[0] - 1
    block_rows = window.shape[1] // 2
    pairs = blocks // 2
    senders, _, slots = got_ref.shape
    own_rows = block_rows + HALO
    claim = lax.axis_index("claim")
    places = 2 * sides + 2
    for place in range(places):
        code = got_ref[:, 2 * place, :].astype(jnp.int32)
        weight = got_ref[:, 2 * place + 1, :]
        split = senders // 2
        for ref, value in ((code_s, code), (weight_s, weight)):
            ref[place, 0:senders, :] = value[:, :LANES]
            ref[place, senders : senders + split, 0 : slots - LANES] = value[:split, LANES:]
            ref[place, senders : senders + split, slots - LANES : LANES] = value[split:, LANES:]
    depth = spaces[0].shape[1] // LANES
    chunks = code_s.shape[1] // depth
    one, none = jnp.ones((), BF16), jnp.zeros((), BF16)

    def iota16(size):
        return lax.broadcasted_iota(jnp.int32, (size, LANES), 0).astype(F32).astype(BF16)

    def add_chunk(chunk, fresh):
        for place in range(places):
            vertical, side = divmod(place, sides + 1)
            kind = 2 * vertical + (side > 0)
            row_hot, col_hot, acc = spaces[3 * kind : 3 * kind + 3]
            rows = HALO if vertical else own_rows
            here = pl.ds(pl.multiple_of(chunk * depth, 8), depth)
            code = code_s[place, here, :]
            weight = weight_s[place, here, :]
            row = lax.shift_right_logical(code, 12) - ROW_BIAS
            col = (code & (CODE - 1)) - COL_BIAS
            high = weight.astype(BF16).astype(F32)
            parts = (high, weight - high)
            width = LANES if side else 2 * LANES
            if side:
                inside = jnp.where(lax.shift_right_arithmetic(col, 7) == 0, col, -1)
            else:
                inside = col & (2 * LANES - 1)
                pair = lax.shift_right_arithmetic(col, 8)
            row_iota, col_iota = iota16(rows), iota16(width)
            for part in range(depth):
                at, only = lanes_of(part), slice(part, part + 1)
                row_hit = tall(pack16(row[only]), rows) == row_iota
                col_hit = tall(pack16(inside[only]), width) == col_iota
                if side:
                    row_hot[:, at] = jnp.where(row_hit, one, none)
                    for index, value in enumerate(parts):
                        col_hot[lanes_of(index), at] = jnp.where(col_hit, tall(pack16(value[only]), LANES), none)
                else:
                    col_hot[:, at] = jnp.where(col_hit, one, none)
                    for group in range(pairs):
                        for index, value in enumerate(parts):
                            mine = jnp.where(pair[only] == group, value[only], 0.0)
                            start = (2 * group + index) * rows
                            row_hot[start : start + rows, at] = jnp.where(row_hit, tall(pack16(mine), rows), none)
            product = lax.dot_general(
                row_hot[...], col_hot[...], (((1,), (1,)), ((), ())), preferred_element_type=F32
            )
            acc[...] = product if fresh and side < 2 else acc[...] + product
        return 0

    add_chunk(0, True)
    if chunks > 1:
        lax.fori_loop(1, chunks, lambda chunk, _: add_chunk(chunk, False), 0)
    own_acc, side_acc, far_acc, corner_acc = spaces[2::3]
    own_at = pl.multiple_of((1 - claim) * HALO, HALO)
    far_at = pl.multiple_of(claim * own_rows, HALO)
    for block in range(blocks):
        group, here = block // 2, lanes_of(block % 2)
        for acc, rows, start in ((own_acc, own_rows, own_at), (far_acc, HALO, far_at)):
            top = 2 * group * rows
            window[block, pl.ds(start, rows), :] = acc[top : top + rows, here] + acc[top + rows : top + 2 * rows, here]
    window[blocks, pl.ds(own_at, own_rows), :] = side_acc[:, :LANES] + side_acc[:, LANES:]
    window[blocks, pl.ds(far_at, HALO), :] = corner_acc[:, :LANES] + corner_acc[:, LANES:]
    row_prefix(window, prefix, window[blocks])


def scan_kernel(group, halves_ref, counts_ref, prefix_ref, beside_ref, out_ref, buffer, sems, rows_s, ends):
    sizes, block_rows, block_cols = buffer.shape
    blocks = block_cols // LANES
    inner_at, outer_at = halo_rows(lax.axis_index("claim"), block_rows)
    rows_s[HALO : HALO + block_rows, :] = beside_ref[:block_rows]
    rows_s[pl.ds(inner_at, HALO), :] = beside_ref[block_rows : block_rows + HALO]
    rows_s[pl.ds(outer_at, HALO), :] = beside_ref[block_rows + HALO :]
    prefix_of(rows_s[...], ends, 0)
    lane = lax.broadcasted_iota(jnp.int32, ends.shape[1:], 1)
    ends[1] = jnp.where(lane < HALO, prefix_ref[blocks], ends[0])
    ends[0] = jnp.where(lane < HALO, ends[0], prefix_ref[0])

    def one_size(step, _):
        half = halves_ref[step]
        inverse = 1.0 / (2 * half + 1).astype(F32)
        band = band_of(half)
        before = None
        for first in range(0, blocks + 1, group):
            some = range(first, min(first + group, blocks + 1))
            strips = []
            for block in some:
                at_end = block in (0, blocks)
                base_at = (ends, block // blocks) if at_end else (prefix_ref, block)
                for field, index in ((counts_ref, block), base_at):
                    lower = field[index, pl.ds(HALO + 8 + half, block_rows), :]
                    upper = field[index, pl.ds(HALO + 7 - half, block_rows), :]
                    strips.append(jnp.concatenate(halves(lower - upper), axis=1))
            product = jnp.dot(jnp.concatenate(strips, axis=0), band, preferred_element_type=F32)
            for index, block in enumerate(some):
                now = [product[(2 * index + f) * block_rows : (2 * index + f + 1) * block_rows] for f in (0, 1)]
                if block > 0:
                    counts, base = (old[:, :LANES] + new[:, LANES:] for old, new in zip(before, now))
                    gain = jnp.log(jnp.maximum(counts, TINY)) - jnp.log(base) - 1.0
                    buffer[step, :, lanes_of(block - 1)] = (counts * gain + base) * inverse
                before = now
        pltpu.make_async_copy(buffer.at[step], out_ref.at[step], sems.at[step]).start()
        return 0

    lax.fori_loop(0, sizes, one_size, 0, unroll=4)

    def finish(step, _):
        pltpu.make_async_copy(buffer.at[step], out_ref.at[step], sems.at[step]).wait()
        return 0

    lax.fori_loop(0, sizes, finish, 0)


def shards(rows, cols, claim_cell, claim_weight, claim_count, baseline, half_widths):
    block_rows, block_cols = baseline.shape
    slots = claim_cell.shape[2]
    sides = side_tiles(cols)
    devices = rows * cols * 2
    whole = pl.BlockSpec(memory_space=pltpu.VMEM)
    scalars = pl.BlockSpec(memory_space=pltpu.SMEM)
    sent = pl.pallas_call(
        functools.partial(pack_kernel, rows, cols, block_rows, block_cols),
        in_specs=[whole, whole, scalars],
        out_shape=jax.ShapeDtypeStruct((devices, 4 * (sides + 1), slots), F32),
    )(claim_cell, claim_weight, claim_count)

    got = lax.all_to_all(sent, ("row", "col", "claim"), split_axis=0, concat_axis=0, tiled=True)
    _, block = lax.optimization_barrier((sent, baseline))
    claim = lax.axis_index("claim")
    seams = [(2 * i + 1, 2 * i + 2) for i in range(rows - 1)]
    seams += [(j, i) for i, j in seams]

    top, bottom = block[:HALO], block[block_rows - HALO :]
    inner = lax.ppermute(jnp.where(claim == 0, bottom, top), "claim", [(0, 1), (1, 0)])
    outer = lax.ppermute(jnp.where(claim == 0, top, bottom), ("row", "claim"), seams)
    pieces = (block, inner, outer)
    first = jnp.concatenate([piece[:, :HALO] for piece in pieces], axis=0)
    last = jnp.concatenate([piece[:, block_cols - HALO :] for piece in pieces], axis=0)
    if cols == 2:
        col = lax.axis_index("col")
        edge = jnp.concatenate([jnp.where(col == 0, last, 0.0), jnp.where(col == 1, first, 0.0)], axis=1)
        beside = lax.ppermute(edge, "col", [(0, 1), (1, 0)])
    else:
        beside = jnp.concatenate(
            [
                lax.ppermute(last, "col", [(i, i + 1) for i in range(cols - 1)]),
                lax.ppermute(first, "col", [(i + 1, i) for i in range(cols - 1)]),
            ],
            axis=1,
        )
    sizes = half_widths.shape[0]
    blocks = block_cols // LANES
    places = 2 * (sides + 1)
    chunk_rows = devices * slots // LANES
    window = pltpu.VMEM((blocks + 1, 2 * block_rows, LANES), F32)
    prefix = (blocks + 1, 2 * block_rows + 8, LANES)
    depth = LANES * max(d for d in (8, 16, 24) if chunk_rows % d == 0)
    spaces = []
    for rows_of in (block_rows + HALO, HALO):
        for tall_rows in (rows_of * blocks, rows_of):
            spaces += [
                pltpu.VMEM((tall_rows, depth), BF16),
                pltpu.VMEM((2 * LANES, depth), BF16),
                pltpu.VMEM((tall_rows, 2 * LANES), F32),
            ]
    base, half_widths = pl.pallas_call(
        base_kernel,
        in_specs=[scalars] + [whole] * 3,
        out_specs=[whole, scalars],
        out_shape=[jax.ShapeDtypeStruct(prefix, F32), jax.ShapeDtypeStruct(half_widths.shape, jnp.int32)],
        scratch_shapes=[window],
        cost_estimate=pl.CostEstimate(flops=0, bytes_accessed=4 * 1024 * 1024, transcendentals=0),
        compiler_params=pltpu.CompilerParams(vmem_limit_bytes=BASE_VMEM),
    )(half_widths, baseline, inner, outer)
    got, base, half_widths = lax.optimization_barrier((got, base, half_widths))
    counts = pl.pallas_call(
        functools.partial(bin_kernel, sides),
        in_specs=[whole],
        out_specs=whole,
        out_shape=jax.ShapeDtypeStruct(prefix, F32),
        scratch_shapes=[
            window,
            pltpu.VMEM((places, chunk_rows, LANES), jnp.int32),
            pltpu.VMEM((places, chunk_rows, LANES), F32),
            *spaces,
        ],
        cost_estimate=pl.CostEstimate(flops=0, bytes_accessed=20 * 1024 * 1024, transcendentals=0),
        compiler_params=pltpu.CompilerParams(vmem_limit_bytes=BIN_VMEM),
    )(got)
    field = (sizes, block_rows, block_cols)
    return pl.pallas_call(
        functools.partial(scan_kernel, 1),
        in_specs=[scalars, whole, whole, whole],
        out_specs=pl.BlockSpec(memory_space=pltpu.HBM),
        scratch_shapes=[
            pltpu.VMEM(field, F32),
            pltpu.SemaphoreType.DMA((sizes,)),
            pltpu.VMEM((2 * block_rows, LANES), F32),
            pltpu.VMEM((2, 2 * block_rows + 8, LANES), F32),
        ],
        out_shape=jax.ShapeDtypeStruct(field, F32),
        compiler_params=pltpu.CompilerParams(vmem_limit_bytes=SCAN_VMEM),
    )(half_widths, counts, base, beside)


def solution(mesh):
    in_specs = (
        P(("groups", "row", "col", "claim"), None, None),
        P(("groups", "row", "col", "claim"), None, None),
        P(("groups", "row", "col", "claim"), None),
        P(("groups", "row", "claim"), "col"),
        P(),
    )
    out_specs = P(None, ("groups", "row", "claim"), "col")
    body = functools.partial(shards, mesh.shape["row"], mesh.shape["col"])
    return jax.shard_map(body, mesh=mesh, in_specs=in_specs, out_specs=out_specs, check_vma=False)
```

```python
import functools

import jax
import jax.numpy as jnp
from jax import lax
from jax.experimental import pallas as pl
from jax.experimental.pallas import tpu as pltpu
from jax.sharding import PartitionSpec as P

HALO = 64
LANES = 128
CODE = 4096
ROW_BIAS = 256
COL_BIAS = 1024
TINY = 1e-30
BASE_VMEM = 8 * 1024 * 1024
BIN_VMEM = 36 * 1024 * 1024
SCAN_VMEM = 24 * 1024 * 1024
F32 = jnp.float32
BF16 = jnp.bfloat16


def side_tiles(cols):
    return min(cols - 1, 2)


def pieces_of(dest, rows, cols):
    row, col, claim = dest
    other = row - 1 if claim == 0 else row + 1
    sides = [(col, 0)]
    if cols == 2:
        sides.append((1 - col, -1 if col == 1 else 1))
    elif cols > 2:
        sides += [(col - 1, -1), (col + 1, 1)]
    found = []
    for tile_row, vertical in ((row, 0), (other, 1)):
        for tile_col, side in sides:
            there = 0 <= tile_row < rows and 0 <= tile_col < cols
            found.append((tile_row * cols + tile_col if there else None, vertical, side))
    return found


def pack_kernel(rows, cols, block_rows, block_cols, cell_ref, weight_ref, count_ref, out_ref):
    cell = cell_ref[0]
    tiles, slots = cell.shape
    slot = lax.broadcasted_iota(jnp.int32, (1, slots), 1)
    weights = [jnp.where(slot < count_ref[0, tile], weight_ref[0, tile : tile + 1, :], 0.0) for tile in range(tiles)]
    tile_row = lax.div(cell, block_cols)
    tile_col = lax.rem(cell, block_cols)
    codes = {}
    for claim in (0, 1):
        for vertical in (0, 1):
            if vertical:
                first = 2 * block_rows - HALO if claim == 0 else 0
            else:
                first = 0 if claim == 0 else block_rows - HALO
            for side in (-1, 0, 1):
                shift = {-1: HALO - block_cols, 0: 0, 1: HALO}[side]
                row_code = (tile_row + (ROW_BIAS - first)) * CODE
                codes[claim, vertical, side] = (row_code + tile_col + (shift + COL_BIAS)).astype(F32)
    zero = jnp.zeros((1, slots), F32)
    index = 0
    for row in range(rows):
        for col in range(cols):
            for claim in (0, 1):
                for place, (tile, vertical, side) in enumerate(pieces_of((row, col, claim), rows, cols)):
                    there = tile is not None
                    code = codes[claim, vertical, side][tile : tile + 1] if there else zero
                    out_ref[index, 2 * place : 2 * place + 1, :] = code
                    out_ref[index, 2 * place + 1 : 2 * place + 2, :] = weights[tile] if there else zero
                index += 1


def halves(value):
    high = value.astype(BF16)
    return high, (value - high.astype(F32)).astype(BF16)


def prefix_of(cells, prefix, block):
    sub = lax.broadcasted_iota(jnp.int32, (cells.shape[0] // 8, 8, LANES), 1)
    cells = cells.reshape(-1, 8, LANES)
    for hop in (1, 2, 4):
        cells = cells + jnp.where(sub >= hop, pltpu.roll(cells, hop, axis=1), 0.0)
    carry = jnp.zeros((8, LANES), F32)
    prefix[block, 0:8, :] = carry
    for tile in range(cells.shape[0]):
        total = cells[tile] + carry
        prefix[block, 8 * tile + 8 : 8 * tile + 16, :] = total
        carry = jnp.broadcast_to(total[7:8], (8, LANES))


def row_prefix(window, prefix, ends):
    blocks, rows, _ = prefix.shape[0] - 1, window.shape[1], LANES
    lane = lax.broadcasted_iota(jnp.int32, (rows, LANES), 1)
    before = ends
    for block in range(blocks + 1):
        after = ends if block == blocks else pltpu.roll(window[block], HALO, axis=1)
        prefix_of(jnp.where(lane < HALO, before, after), prefix, block)
        before = after


def band_of(half):
    here = lax.broadcasted_iota(jnp.int32, (LANES, LANES), 0)
    there = lax.broadcasted_iota(jnp.int32, (LANES, LANES), 1)
    gap = here - there
    both = [jnp.where(jnp.abs(gap + shift) <= half, 1.0, 0.0) for shift in (-HALO, LANES - HALO)]
    band = jnp.concatenate(both, axis=1).astype(BF16)
    return jnp.concatenate([band, band], axis=0)


def lanes_of(block):
    return slice(block * LANES, (block + 1) * LANES)


def halo_rows(claim, block_rows):
    far_side = HALO + block_rows
    return pl.multiple_of((1 - claim) * far_side, HALO), pl.multiple_of(claim * far_side, HALO)


def base_kernel(halves_ref, base_ref, inner_ref, outer_ref, prefix, halves_out, window):
    block_rows, block_cols = base_ref.shape
    for step in range(halves_ref.shape[0]):
        halves_out[step] = halves_ref[step]
    inner_at, outer_at = halo_rows(lax.axis_index("claim"), block_rows)
    for block in range(block_cols // LANES):
        here = lanes_of(block)
        window[block, HALO : HALO + block_rows, :] = base_ref[:, here]
        window[block, pl.ds(inner_at, HALO), :] = inner_ref[:, here]
        window[block, pl.ds(outer_at, HALO), :] = outer_ref[:, here]
    row_prefix(window, prefix, jnp.zeros((window.shape[1], LANES), F32))


def pack16(row):
    return jnp.broadcast_to(row.astype(F32), (16, row.shape[1])).astype(BF16)


def tall(packed, size):
    return jnp.concatenate([packed] * (size // 16), axis=0)


def bin_kernel(sides, got_ref, prefix, window, code_s, weight_s, *spaces):
    blocks = window.shape[0] - 1
    block_rows = window.shape[1] // 2
    pairs = blocks // 2
    senders, _, slots = got_ref.shape
    own_rows = block_rows + HALO
    claim = lax.axis_index("claim")
    places = 2 * sides + 2
    for place in range(places):
        code = got_ref[:, 2 * place, :].astype(jnp.int32)
        weight = got_ref[:, 2 * place + 1, :]
        split = senders // 2
        for ref, value in ((code_s, code), (weight_s, weight)):
            ref[place, 0:senders, :] = value[:, :LANES]
            ref[place, senders : senders + split, 0 : slots - LANES] = value[:split, LANES:]
            ref[place, senders : senders + split, slots - LANES : LANES] = value[split:, LANES:]
    depth = spaces[0].shape[1] // LANES
    chunks = code_s.shape[1] // depth
    one, none = jnp.ones((), BF16), jnp.zeros((), BF16)

    def iota16(size):
        return lax.broadcasted_iota(jnp.int32, (size, LANES), 0).astype(F32).astype(BF16)

    def add_chunk(chunk, fresh):
        for place in range(places):
            vertical, side = divmod(place, sides + 1)
            kind = 2 * vertical + (side > 0)
            row_hot, col_hot, acc = spaces[3 * kind : 3 * kind + 3]
            rows = HALO if vertical else own_rows
            here = pl.ds(pl.multiple_of(chunk * depth, 8), depth)
            code = code_s[place, here, :]
            weight = weight_s[place, here, :]
            row = lax.shift_right_logical(code, 12) - ROW_BIAS
            col = (code & (CODE - 1)) - COL_BIAS
            high = weight.astype(BF16).astype(F32)
            parts = (high, weight - high)
            width = LANES if side else 2 * LANES
            if side:
                inside = jnp.where(lax.shift_right_arithmetic(col, 7) == 0, col, -1)
            else:
                inside = col & (2 * LANES - 1)
                pair = lax.shift_right_arithmetic(col, 8)
            row_iota, col_iota = iota16(rows), iota16(width)
            for part in range(depth):
                at, only = lanes_of(part), slice(part, part + 1)
                row_hit = tall(pack16(row[only]), rows) == row_iota
                col_hit = tall(pack16(inside[only]), width) == col_iota
                if side:
                    row_hot[:, at] = jnp.where(row_hit, one, none)
                    for index, value in enumerate(parts):
                        col_hot[lanes_of(index), at] = jnp.where(col_hit, tall(pack16(value[only]), LANES), none)
                else:
                    col_hot[:, at] = jnp.where(col_hit, one, none)
                    for group in range(pairs):
                        for index, value in enumerate(parts):
                            mine = jnp.where(pair[only] == group, value[only], 0.0)
                            start = (2 * group + index) * rows
                            row_hot[start : start + rows, at] = jnp.where(row_hit, tall(pack16(mine), rows), none)
            product = lax.dot_general(
                row_hot[...], col_hot[...], (((1,), (1,)), ((), ())), preferred_element_type=F32
            )
            acc[...] = product if fresh and side < 2 else acc[...] + product
        return 0

    add_chunk(0, True)
    if chunks > 1:
        lax.fori_loop(1, chunks, lambda chunk, _: add_chunk(chunk, False), 0)
    own_acc, side_acc, far_acc, corner_acc = spaces[2::3]
    own_at = pl.multiple_of((1 - claim) * HALO, HALO)
    far_at = pl.multiple_of(claim * own_rows, HALO)
    for block in range(blocks):
        group, here = block // 2, lanes_of(block % 2)
        for acc, rows, start in ((own_acc, own_rows, own_at), (far_acc, HALO, far_at)):
            top = 2 * group * rows
            window[block, pl.ds(start, rows), :] = acc[top : top + rows, here] + acc[top + rows : top + 2 * rows, here]
    window[blocks, pl.ds(own_at, own_rows), :] = side_acc[:, :LANES] + side_acc[:, LANES:]
    window[blocks, pl.ds(far_at, HALO), :] = corner_acc[:, :LANES] + corner_acc[:, LANES:]
    row_prefix(window, prefix, window[blocks])


def scan_kernel(group, halves_ref, counts_ref, prefix_ref, beside_ref, out_ref, buffer, sems, rows_s, ends):
    sizes, block_rows, block_cols = buffer.shape
    blocks = block_cols // LANES
    inner_at, outer_at = halo_rows(lax.axis_index("claim"), block_rows)
    rows_s[HALO : HALO + block_rows, :] = beside_ref[:block_rows]
    rows_s[pl.ds(inner_at, HALO), :] = beside_ref[block_rows : block_rows + HALO]
    rows_s[pl.ds(outer_at, HALO), :] = beside_ref[block_rows + HALO :]
    prefix_of(rows_s[...], ends, 0)
    lane = lax.broadcasted_iota(jnp.int32, ends.shape[1:], 1)
    ends[1] = jnp.where(lane < HALO, prefix_ref[blocks], ends[0])
    ends[0] = jnp.where(lane < HALO, ends[0], prefix_ref[0])

    def one_size(step, _):
        half = halves_ref[step]
        inverse = 1.0 / (2 * half + 1).astype(F32)
        band = band_of(half)
        before = None
        for first in range(0, blocks + 1, group):
            some = range(first, min(first + group, blocks + 1))
            strips = []
            for block in some:
                at_end = block in (0, blocks)
                base_at = (ends, block // blocks) if at_end else (prefix_ref, block)
                for field, index in ((counts_ref, block), base_at):
                    lower = field[index, pl.ds(HALO + 8 + half, block_rows), :]
                    upper = field[index, pl.ds(HALO + 7 - half, block_rows), :]
                    strips.append(jnp.concatenate(halves(lower - upper), axis=1))
            product = jnp.dot(jnp.concatenate(strips, axis=0), band, preferred_element_type=F32)
            for index, block in enumerate(some):
                now = [product[(2 * index + f) * block_rows : (2 * index + f + 1) * block_rows] for f in (0, 1)]
                if block > 0:
                    counts, base = (old[:, :LANES] + new[:, LANES:] for old, new in zip(before, now))
                    gain = jnp.log(jnp.maximum(counts, TINY)) - jnp.log(base) - 1.0
                    buffer[step, :, lanes_of(block - 1)] = (counts * gain + base) * inverse
                before = now
        pltpu.make_async_copy(buffer.at[step], out_ref.at[step], sems.at[step]).start()
        return 0

    lax.fori_loop(0, sizes, one_size, 0, unroll=8)

    def finish(step, _):
        pltpu.make_async_copy(buffer.at[step], out_ref.at[step], sems.at[step]).wait()
        return 0

    lax.fori_loop(0, sizes, finish, 0)


def shards(rows, cols, claim_cell, claim_weight, claim_count, baseline, half_widths):
    block_rows, block_cols = baseline.shape
    slots = claim_cell.shape[2]
    sides = side_tiles(cols)
    devices = rows * cols * 2
    whole = pl.BlockSpec(memory_space=pltpu.VMEM)
    scalars = pl.BlockSpec(memory_space=pltpu.SMEM)
    sent = pl.pallas_call(
        functools.partial(pack_kernel, rows, cols, block_rows, block_cols),
        in_specs=[whole, whole, scalars],
        out_shape=jax.ShapeDtypeStruct((devices, 4 * (sides + 1), slots), F32),
    )(claim_cell, claim_weight, claim_count)

    got = lax.all_to_all(sent, ("row", "col", "claim"), split_axis=0, concat_axis=0, tiled=True)
    _, block = lax.optimization_barrier((sent, baseline))
    claim = lax.axis_index("claim")
    seams = [(2 * i + 1, 2 * i + 2) for i in range(rows - 1)]
    seams += [(j, i) for i, j in seams]

    top, bottom = block[:HALO], block[block_rows - HALO :]
    inner = lax.ppermute(jnp.where(claim == 0, bottom, top), "claim", [(0, 1), (1, 0)])
    outer = lax.ppermute(jnp.where(claim == 0, top, bottom), ("row", "claim"), seams)
    pieces = (block, inner, outer)
    first = jnp.concatenate([piece[:, :HALO] for piece in pieces], axis=0)
    last = jnp.concatenate([piece[:, block_cols - HALO :] for piece in pieces], axis=0)
    if cols == 2:
        col = lax.axis_index("col")
        edge = jnp.concatenate([jnp.where(col == 0, last, 0.0), jnp.where(col == 1, first, 0.0)], axis=1)
        beside = lax.ppermute(edge, "col", [(0, 1), (1, 0)])
    else:
        beside = jnp.concatenate(
            [
                lax.ppermute(last, "col", [(i, i + 1) for i in range(cols - 1)]),
                lax.ppermute(first, "col", [(i + 1, i) for i in range(cols - 1)]),
            ],
            axis=1,
        )
    sizes = half_widths.shape[0]
    blocks = block_cols // LANES
    places = 2 * (sides + 1)
    chunk_rows = devices * slots // LANES
    window = pltpu.VMEM((blocks + 1, 2 * block_rows, LANES), F32)
    prefix = (blocks + 1, 2 * block_rows + 8, LANES)
    depth = LANES * max(d for d in (8, 16, 24) if chunk_rows % d == 0)
    spaces = []
    for rows_of in (block_rows + HALO, HALO):
        for tall_rows in (rows_of * blocks, rows_of):
            spaces += [
                pltpu.VMEM((tall_rows, depth), BF16),
                pltpu.VMEM((2 * LANES, depth), BF16),
                pltpu.VMEM((tall_rows, 2 * LANES), F32),
            ]
    base, half_widths = pl.pallas_call(
        base_kernel,
        in_specs=[scalars] + [whole] * 3,
        out_specs=[whole, scalars],
        out_shape=[jax.ShapeDtypeStruct(prefix, F32), jax.ShapeDtypeStruct(half_widths.shape, jnp.int32)],
        scratch_shapes=[window],
        cost_estimate=pl.CostEstimate(flops=0, bytes_accessed=4 * 1024 * 1024, transcendentals=0),
        compiler_params=pltpu.CompilerParams(vmem_limit_bytes=BASE_VMEM),
    )(half_widths, baseline, inner, outer)
    got, base, half_widths = lax.optimization_barrier((got, base, half_widths))
    counts = pl.pallas_call(
        functools.partial(bin_kernel, sides),
        in_specs=[whole],
        out_specs=whole,
        out_shape=jax.ShapeDtypeStruct(prefix, F32),
        scratch_shapes=[
            window,
            pltpu.VMEM((places, chunk_rows, LANES), jnp.int32),
            pltpu.VMEM((places, chunk_rows, LANES), F32),
            *spaces,
        ],
        cost_estimate=pl.CostEstimate(flops=0, bytes_accessed=20 * 1024 * 1024, transcendentals=0),
        compiler_params=pltpu.CompilerParams(vmem_limit_bytes=BIN_VMEM),
    )(got)
    field = (sizes, block_rows, block_cols)
    return pl.pallas_call(
        functools.partial(scan_kernel, 1),
        in_specs=[scalars, whole, whole, whole],
        out_specs=pl.BlockSpec(memory_space=pltpu.HBM),
        scratch_shapes=[
            pltpu.VMEM(field, F32),
            pltpu.SemaphoreType.DMA((sizes,)),
            pltpu.VMEM((2 * block_rows, LANES), F32),
            pltpu.VMEM((2, 2 * block_rows + 8, LANES), F32),
        ],
        out_shape=jax.ShapeDtypeStruct(field, F32),
        compiler_params=pltpu.CompilerParams(vmem_limit_bytes=SCAN_VMEM),
    )(half_widths, counts, base, beside)


def solution(mesh):
    in_specs = (
        P(("groups", "row", "col", "claim"), None, None),
        P(("groups", "row", "col", "claim"), None, None),
        P(("groups", "row", "col", "claim"), None),
        P(("groups", "row", "claim"), "col"),
        P(),
    )
    out_specs = P(None, ("groups", "row", "claim"), "col")
    body = functools.partial(shards, mesh.shape["row"], mesh.shape["col"])
    return jax.shard_map(body, mesh=mesh, in_specs=in_specs, out_specs=out_specs, check_vma=False)
```
